32 devices in a mesh: tm: 8 (over z, x), tile: 4 (over y, core).
Axes of the slice: x: 2, y: 2, z: 4, core: 2. Of those that a mesh axis runs over, the one named last changes fastest.
Arguments:
- operator: float32 [8, 768, 768], P('tm', 'tile'), may hold values from -4 to 20, as said below
- initial: float32 [8, 768, 768], P('tm', 'tile'), may hold values from -1 to 2, as said below
- block_sizes: int32 [8], P('tm'), may hold values from 512 to 768, as said below
- link_index: int32 [8, 512], P('tm'), may hold values from 0 to 511, as said below
- link_pair: bfloat16 [8, 768, 512], P('tm', 'tile'), may hold values from -0.4375 to 0.4375
- link_global: bfloat16 [8, 768, 512], P('tm', 'tile'), may hold values from -0.15625 to 0.15625
- schur_base: float32 [512, 512], P('tile'), may hold values from -4 to 20, as said below
- schur_start: float32 [512, 512], P('tile'), may hold values from -1 to 2, as said below
Outputs:
- link_diag: float32 [8, 256, 256], P('tm', 'tile')
- link_off: float32 [8, 256, 256], P('tm', 'tile')
- link_cross: float32 [8, 256, 512], P('tm', 'tile')
- global_schur: float32 [512, 512], P('tile')
- back_cols: float32 [8, 768, 512], P('tm', 'tile')
The draws below stay inside these ranges and needn't reach their ends.
Inputs may be any that keep to these rules, and one draw needn't show every extreme that they name: `operator`: symmetric. `initial`: symmetric. `schur_base`: symmetric. `schur_start`: symmetric. `block_sizes`: some block has 768 live variables and some has 512. `link_index`: each row is a permutation of 0 to 511 that keeps every index j within its group of 128, j // 128.
All inputs are finite; a program needn't handle non-finite values.
Results may differ from the reference program's by a relative error of at most 0.0003.
Values may be sent and summed in bfloat16 or wider, within the bound.
No kernel may reach another device: no remote copies, remote signals or barrier semaphores. Data moves between devices by JAX's collectives and lax.ppermute only.
A program may use at most 64 MiB of HBM per device.

```python
import jax
import jax.numpy as jnp
from jax import lax

NB = 768
LINK = 256
GLINK = 512
STEPS = 2
TIMES = 8
OWN = 128


def spread_scales(key, count, size):
    upper = jnp.log(10.0)
    return jnp.exp(jax.random.uniform(jax.random.fold_in(key, 7), (count, size), jnp.float32, 0.0, upper))


def symmetric_noise(key, count, size, strength):
    raw = jax.random.normal(key, (count, size, size), jnp.float32)
    both = (raw + jnp.swapaxes(raw, 1, 2)) * 0.70710678
    return both * (strength / size ** 0.5)


def scaled_pair(key, count, size, strength, invert):
    scales = spread_scales(key, count, size)
    noise = symmetric_noise(key, count, size, strength)
    unit = jnp.eye(size, dtype=jnp.float32)[None]
    roots = jnp.sqrt(scales)
    if invert:
        roots = 1.0 / roots
    return roots[:, :, None] * (unit + noise) * roots[:, None, :]


def draw_operator(key, part):
    return scaled_pair(jax.random.fold_in(key, 21), TIMES, NB, 0.2, False)


def draw_initial(key, part):
    base = jax.random.fold_in(key, 21)
    scales_key = base
    noise = symmetric_noise(jax.random.fold_in(key, 31), TIMES, NB, 0.1)
    roots = 1.0 / jnp.sqrt(spread_scales(scales_key, TIMES, NB))
    unit = jnp.eye(NB, dtype=jnp.float32)[None]
    return roots[:, :, None] * (unit + noise) * roots[:, None, :]


def draw_schur_base(key, part):
    return scaled_pair(jax.random.fold_in(key, 41), 1, GLINK, 0.2, False)[0]


def draw_schur_start(key, part):
    base = jax.random.fold_in(key, 41)
    noise = symmetric_noise(jax.random.fold_in(key, 51), 1, GLINK, 0.1)
    roots = 1.0 / jnp.sqrt(spread_scales(base, 1, GLINK))
    unit = jnp.eye(GLINK, dtype=jnp.float32)[None]
    return (roots[:, :, None] * (unit + noise) * roots[:, None, :])[0]


def draw_block_sizes(key, part):
    lowest = NB * 2 // 3
    values = jax.random.randint(jax.random.fold_in(key, 61), (TIMES,), lowest, NB + 1)
    high_pos = jax.random.randint(jax.random.fold_in(key, 62), (), 0, TIMES)
    low_pos = (high_pos + 1 + jax.random.randint(jax.random.fold_in(key, 63), (), 0, TIMES - 1)) % TIMES
    values = values.at[high_pos].set(NB)
    values = values.at[low_pos].set(lowest)
    return values.astype(jnp.int32)


def draw_link_index(key, part):
    groups = GLINK // OWN
    keys = jax.random.split(jax.random.fold_in(key, 71), TIMES * groups)
    perms = jax.vmap(lambda single: jax.random.permutation(single, OWN))(keys)
    perms = perms.reshape(TIMES, groups, OWN).astype(jnp.int32)
    offsets = (jnp.arange(groups, dtype=jnp.int32) * OWN)[None, :, None]
    return (perms + offsets).reshape(TIMES, GLINK).astype(jnp.int32)


def with_spikes(entries, stream_key, source, target, parts, factor):
    owner, partner = [(jnp.arange(entries.shape[position]) // (entries.shape[position] // parts)).reshape([-1 if axis == position else 1 for axis in range(entries.ndim)]) for position in (source, target)]
    chosen = jax.random.permutation(stream_key, parts)[partner]
    strong = (owner == chosen) | (owner == (partner + parts // 2) % parts)
    return jnp.where(strong, factor * entries, entries)


def block_levels(own_key, dims, shards, smallest, largest):
    gain = 1.0
    for position, blocks in shards:
        steps = jax.random.uniform(jax.random.fold_in(jax.random.fold_in(own_key, 6), position), (blocks,), jnp.float32, smallest / len(shards), largest / len(shards))
        gain = gain * jnp.repeat(jnp.exp(steps), dims[position] // blocks).reshape((-1,) + (1,) * (len(dims) - 1 - position))
    return gain


def gaussian(rng, extent, scale, bound, cuts=(), held_as=jnp.bfloat16):
    gain = block_levels(rng, extent, cuts, -0.22, 0.18) if cuts else 1.0
    entries = jax.random.normal(rng, extent, jnp.float32) * scale * gain
    return jnp.minimum(jnp.maximum(entries, -bound), bound).astype(held_as)


def bell_draw_with(own_key, extent, deviation, limit, shards, heavy, held_as=jnp.bfloat16):
    values = deviation * jax.random.normal(own_key, extent, jnp.float32)
    if shards:
        values = values * block_levels(own_key, extent, shards, -0.22, 0.18)
    return jnp.clip(with_spikes(values, jax.random.fold_in(own_key, 3), *heavy), -limit, limit).astype(held_as)


def setup_inputs(seed: int = 0) -> dict:
    streams_of = jax.random.split(jax.random.key(seed), 9)
    return {
        "operator": draw_operator(jax.random.fold_in(streams_of[8], 71), 0),
        "initial": draw_initial(jax.random.fold_in(streams_of[8], 71), 0),
        "block_sizes": draw_block_sizes(jax.random.fold_in(streams_of[8], 71), 0),
        "link_index": draw_link_index(jax.random.fold_in(streams_of[8], 71), 0),
        "link_pair": gaussian(streams_of[4], (TIMES, NB, 2 * LINK), (NB // 4) ** -0.5, 0.4375, ((0, 8), (1, 4))),
        "link_global": bell_draw_with(streams_of[5], (TIMES, NB, GLINK), (1.5 / (NB * TIMES) ** 0.5), 0.15625, ((0, 8), (1, 4)), (0, 2, 8, 2.0)),
        "schur_base": draw_schur_base(jax.random.fold_in(streams_of[8], 71), 0),
        "schur_start": draw_schur_start(jax.random.fold_in(streams_of[8], 71), 0),
    }


HIGH = lax.Precision.HIGHEST


def matmul(left_side, right_side):
    return jnp.dot(left_side, right_side, precision=HIGH, preferred_element_type=jnp.float32)


def block_terms(inputs):
    op_block, init_block, pair_block, glob_block, size_value, index_row = inputs
    block_order = op_block.shape[0]
    ids = jnp.arange(block_order, dtype=jnp.int32)
    live = (ids < size_value).astype(jnp.float32)
    unit = jnp.eye(block_order, dtype=jnp.float32)

    def effective(matrix):
        return matrix * live[:, None] * live[None, :] + unit * (1.0 - live)[:, None]

    kmatrix = effective(op_block)
    xmatrix = effective(init_block)
    for step in range(STEPS):
        xmatrix = 2.0 * xmatrix - matmul(matmul(xmatrix, kmatrix), xmatrix)
    pair_live = pair_block.astype(jnp.float32) * live[:, None]
    glob_live = jnp.take(glob_block.astype(jnp.float32), index_row, axis=1) * live[:, None]
    solved = matmul(xmatrix, jnp.concatenate([pair_live, glob_live], axis=1))
    e_part = pair_live[:, :LINK]
    f_part = pair_live[:, LINK:]
    y_e = solved[:, :LINK]
    y_f = solved[:, LINK:2 * LINK]
    y_g = solved[:, 2 * LINK:]

    def inner(left_side, right_side):
        return matmul(left_side.T, right_side)

    return (inner(f_part, y_f), inner(e_part, y_e), inner(e_part, y_f), inner(e_part, y_g),
            inner(f_part, y_g), inner(glob_live, y_g), y_g)


def reference(operator, initial, block_sizes, link_index, link_pair, link_global, schur_base, schur_start):
    terms = lax.map(block_terms, (operator, initial, link_pair, link_global, block_sizes, link_index))
    f_diag, e_diag, e_off, e_cross, f_cross, g_terms, y_glob = terms
    e_next = jnp.concatenate([e_diag[1:], jnp.zeros_like(e_diag[:1])], axis=0)
    c_next = jnp.concatenate([e_cross[1:], jnp.zeros_like(e_cross[:1])], axis=0)
    link_diag = f_diag + e_next
    link_cross = f_cross + c_next
    global_schur = schur_base + jnp.sum(g_terms, axis=0)
    inverse = 2.0 * schur_start - matmul(matmul(schur_start, global_schur), schur_start)
    back_cols = jnp.einsum("tij,jk->tik", y_glob, inverse, precision=HIGH)
    return link_diag, e_off, link_cross, global_schur, back_cols
```

```python
import functools

import jax
import jax.numpy as jnp
from jax import lax
from jax.experimental import pallas as pl
from jax.experimental.pallas import tpu as pltpu
from jax.sharding import PartitionSpec as P

BF16 = jnp.bfloat16
F32 = jnp.float32
TERMS = 3
VMEM_BYTES = 32 * 2**20


def halves(value):
    high = value.astype(BF16)
    return high, (value - high.astype(F32)).astype(BF16)


def dot(left_side, right_side):
    return jnp.dot(left_side, right_side, preferred_element_type=F32)


def both(value):
    return jnp.concatenate(halves(value), axis=1)


def stacked(value):
    return jnp.concatenate(halves(value), axis=0)


def quadrants(product):
    rows, cols = product.shape[0] // 2, product.shape[1] // 2
    return (product[:rows, :cols] + product[:rows, cols:]) + (
        product[rows:, :cols] + product[rows:, cols:]
    )


def at_rows(start, size, unit=16):
    return pl.ds(pl.multiple_of(start, unit), size)


def live_rows(info, half):
    near, size = info[0] // 2, info[1]
    ids = lax.broadcasted_iota(jnp.int32, (half, 1), 0)
    return jnp.concatenate(
        [(ids + near * half) < size, (ids + (1 - near) * half) < size], axis=0
    )


def put_rows(info, pieces, target, offset=0):
    rows = pieces[0].shape[0]
    core = info[0] % 2
    target[at_rows(offset + core * rows, rows), :] = pieces[0]
    target[at_rows(offset + (1 - core) * rows, rows), :] = pieces[1]


def spread(info, own, other, top, bottom, block):
    rows, order = own.shape
    half = order // 2
    near, core = info[0] // 2, info[0] % 2
    for ref, place in ((own, core), (other, 1 - core)):
        for side in range(2):
            cols = pl.ds(pl.multiple_of((near if side == 0 else 1 - near) * half, 128), half)
            value = ref[:, cols]
            high, low = halves(value)
            top[at_rows(place * rows, rows), side * half : (side + 1) * half] = high
            top[at_rows(half + place * rows, rows), side * half : (side + 1) * half] = low
            if side == 1:
                block[at_rows(place * rows, rows), :] = value
    high, low = halves(block[...].T)
    bottom[0:half, 0:half] = high
    bottom[half : 2 * half, 0:half] = low


def corner(info, own, other, target, first):
    rows, half = own.shape
    core = info[0] % 2
    for ref, place in ((own, core), (other, 1 - core)):
        high, low = halves(ref[...])
        target[at_rows(place * rows, rows), first : first + half] = high
        target[at_rows(half + place * rows, rows), first : first + half] = low


def times_x(top, bottom, columns):
    return jnp.concatenate(
        [quadrants(dot(top[...], columns)), quadrants(dot(bottom[...], columns))], axis=0
    )


def times_k(top, bottom, last, columns):
    half = last.shape[1]
    low = dot(bottom[...], columns[:half]) + dot(last[...], columns[half:])
    return jnp.concatenate([quadrants(dot(top[...], columns)), quadrants(low)], axis=0)


def prepare_kernel(
    info, x_own, x_core, x_far, x_cross, k_own, k_core, g_own, g_core, g_far, g_cross, index,
    x_top, x_bottom, k_top, k_bottom, links, first, block, gathered,
):
    half = x_own.shape[1] // 2
    width = g_own.shape[1]
    spread(info, x_own, x_core, x_top, x_bottom, block)
    corner(info, x_far, x_cross, x_bottom, half)
    put_rows(info, (g_own[...], g_core[...]), gathered)
    put_rows(info, (g_far[...], g_cross[...]), gathered, half)
    live = live_rows(info, half)
    hot = lax.broadcasted_iota(jnp.int32, (width, width), 0) == index[...]
    chosen = dot(gathered[...], hot.astype(F32).astype(BF16))
    links[...] = jnp.where(live, chosen, 0.0).astype(BF16)
    group = width // 4
    columns = links[:, pl.ds(pl.multiple_of(info[0] * group, 128), group)]
    for ref, place in ((x_top, 0), (x_bottom, half)):
        product = dot(ref[...], columns)
        product = product[:half] + product[half:]
        first[place : place + half, :] = both(
            jnp.where(live[place : place + half], product, 0.0)
        )
    spread(info, k_own, k_core, k_top, k_bottom, block)


def solve(columns, first, live, x_top, x_bottom, k_top, k_bottom, k_last):
    state = columns
    for step in range(TERMS):
        product = times_k(k_top, k_bottom, k_last, first)
        state = columns + state - jnp.where(live, product, 0.0)
        result = jnp.where(live, times_x(x_top, x_bottom, both(state)), 0.0)
        first = both(result)
    return result


def global_kernel(
    info, k_far, k_cross, x_top, x_bottom, k_top, k_bottom, links, first, base,
    keep, send, y_own, y_core, y_far, y_cross, k_last, pack, solved,
):
    half = k_far.shape[1]
    rows = k_far.shape[0]
    width = links.shape[1]
    group = width // 4
    part, core = info[0], info[0] % 2
    corner(info, k_far, k_cross, k_last, 0)
    live = live_rows(info, half)
    columns = links[:, pl.ds(pl.multiple_of(part * group, 128), group)].astype(F32)
    result = solve(columns, first[...], live, x_top, x_bottom, k_top, k_bottom, k_last)
    solved[...] = result
    y_own[...] = solved[at_rows(core * rows, rows), :]
    y_core[...] = solved[at_rows((1 - core) * rows, rows), :]
    y_far[...] = solved[at_rows(half + core * rows, rows), :]
    y_cross[...] = solved[at_rows(half + (1 - core) * rows, rows), :]
    left_side = stacked(result.T)

    def block(shift):
        place = pl.ds(pl.multiple_of(((part + shift) % 4) * group, 128), group)
        both_parts = dot(left_side, links[:, place])
        added = jnp.where(info[2] == 0, base[:, place], 0.0)
        return both_parts[:group] + both_parts[group:] + added

    pack[0:group, :] = block(0)
    pack[group : 2 * group, :] = block(1)
    across = block(2)
    pack[2 * group :, :] = jnp.where(
        part < 2, across[: group // 2, :], across.T[group // 2 :, :]
    )
    size = keep.shape[0]
    side = info[2] % 2
    keep[...] = pack[at_rows(side * size, size, 8), :]
    send[...] = pack[at_rows((1 - side) * size, size, 8), :]


def pair_kernel(
    info, p_own, p_core, p_far, p_cross, x_top, x_bottom, k_top, k_bottom, k_last, links,
    own_terms, off_terms, next_terms, gathered,
):
    half = k_last.shape[1]
    width = p_own.shape[1]
    link = width // 2
    share = link // 4
    part = info[0]
    put_rows(info, (p_own[...], p_core[...]), gathered)
    put_rows(info, (p_far[...], p_cross[...]), gathered, half)
    live = live_rows(info, half)
    masked = jnp.where(live, gathered[...], jnp.zeros((), BF16))
    source = lax.broadcasted_iota(jnp.int32, (width, 2 * share), 0)
    place = lax.broadcasted_iota(jnp.int32, (width, 2 * share), 1)
    wanted = part * share + place + jnp.where(place < share, 0, link - share)
    columns = dot(masked, (source == wanted).astype(F32).astype(BF16))
    product = times_x(x_top, x_bottom, both(columns))
    first = both(jnp.where(live, product, 0.0))
    result = solve(columns, first, live, x_top, x_bottom, k_top, k_bottom, k_last)
    left_side = stacked(result.T)
    terms = dot(left_side, masked)
    terms = terms[: 2 * share] + terms[2 * share :]
    cross = dot(left_side, links[...])
    cross = cross[: 2 * share] + cross[2 * share :]
    next_terms[:, :link] = terms[:share, :link]
    next_terms[:, link:] = cross[:share]
    off_terms[...] = terms[:share, link:]
    own_terms[:, :link] = terms[share:, link:]
    own_terms[:, link:] = cross[share:]


def start_kernel(
    info, s_own, s_core, s_far, s_cross, y_own, y_core, y_far, y_cross, start, scaled
):
    part = info[0]
    group = s_own.shape[0]
    width = s_own.shape[1]
    total = None
    for ref, mask, rows in (
        (s_own, 0, y_own), (s_core, 1, y_core), (s_far, 2, y_far), (s_cross, 3, y_cross)
    ):
        value = both(ref[...])
        start[at_rows((part ^ mask) * group, group), :] = value
        product = quadrants(dot(stacked(rows[...]), value))
        total = product if total is None else total + product
    scaled[...] = total


def back_kernel(
    info, *refs
):
    sums, (start, scaled, own_terms, came), outs = refs[:8], refs[8:12], refs[12:]
    link_diag, link_cross, schur, back, whole, full = outs
    part, side = info[0], info[2] % 2
    size = sums[0].shape[0]
    group = schur.shape[0]
    width = schur.shape[1]
    for mask in range(4):
        for half in range(2):
            place = at_rows((part ^ mask) * (2 * size) + (side ^ half) * size, size, 8)
            whole[place, :] = sums[2 * mask + half][...]
    for row in range(4):
        first = row * 2 * size
        diagonal = whole[first : first + group, :]
        after = whole[first + group : first + 2 * group, :]
        nxt = (row + 1) % 4
        full[row * group : (row + 1) * group, row * group : (row + 1) * group] = diagonal
        full[row * group : (row + 1) * group, nxt * group : (nxt + 1) * group] = after
        full[nxt * group : (nxt + 1) * group, row * group : (row + 1) * group] = after.T
        if row < 2:
            other = (row + 2) * 2 * size
            across = jnp.concatenate(
                [whole[first + 2 * group : first + 2 * size, :],
                 whole[other + 2 * group : other + 2 * size, :]], axis=0
            )
            far = row + 2
            full[row * group : (row + 1) * group, far * group : (far + 1) * group] = across
            full[far * group : (far + 1) * group, row * group : (row + 1) * group] = across.T
    schur[...] = full[at_rows(part * group, group, 8), :]
    value = scaled[...]
    product = quadrants(dot(stacked(value), both(full[...])))
    product = quadrants(dot(stacked(product), start[...]))
    back[...] = 2.0 * value - product
    link = link_diag.shape[1]
    link_diag[...] = own_terms[:, :link] + came[:, :link]
    link_cross[...] = own_terms[:, link:] + came[:, link:]


def call(kernel, outs, scratch, flops, *args):
    smem = pl.BlockSpec(memory_space=pltpu.SMEM)
    vmem = pl.BlockSpec(memory_space=pltpu.VMEM)
    moved = sum(a.size * a.dtype.itemsize for a in args)
    return pl.pallas_call(
        kernel,
        out_shape=[jax.ShapeDtypeStruct(shape, dtype) for shape, dtype in outs],
        in_specs=[smem] + [vmem] * (len(args) - 1),
        out_specs=[vmem] * len(outs),
        scratch_shapes=[pltpu.VMEM(shape, dtype) for shape, dtype in scratch],
        compiler_params=pltpu.CompilerParams(vmem_limit_bytes=VMEM_BYTES),
        cost_estimate=pl.CostEstimate(flops=flops, bytes_accessed=moved, transcendentals=0),
        name=kernel.__name__,
    )(*args)


def shards(
    blocks, operator, initial, block_sizes, link_index, link_pair, link_global, schur_base,
    schur_start,
):
    part, block = lax.axis_index("tile"), lax.axis_index("tm")
    info = jnp.stack([part, block_sizes[0], block]).astype(jnp.int32)
    operator, initial = operator[0], initial[0]
    pair, glob = link_pair[0], link_global[0]
    rows, order = operator.shape
    half = order // 2
    link, width = pair.shape[1] // 2, glob.shape[1]
    group, share = width // 4, link // 4
    size = group + group // 4

    def tile_swap(value, mask):
        return lax.ppermute(value, "tile", [(i, i ^ mask) for i in range(4)])

    def block_swap(value, mask):
        return lax.ppermute(value, "tm", [(i, i ^ mask) for i in range(blocks)])

    def gathered(own, sent):
        far = tile_swap(sent, 2)
        return own, tile_swap(own, 1), far, tile_swap(far, 1)

    near_cols = (part // 2) * half
    g_all = gathered(glob, glob)
    x_all = gathered(initial, lax.dynamic_slice_in_dim(initial, near_cols, half, 1))
    k_all = gathered(operator, lax.dynamic_slice_in_dim(operator, near_cols, half, 1))
    p_all = gathered(pair, pair)
    s_all = gathered(schur_start, schur_start)

    apply_flops = 2 * 2 * order * order * 2 * group
    x_top, x_bottom, k_top, k_bottom, links, first = call(
        prepare_kernel,
        [((2 * half, order), BF16), ((2 * half, order), BF16), ((2 * half, order), BF16),
         ((2 * half, half), BF16), ((order, width), BF16), ((order, 2 * group), BF16)],
        [((half, half), F32), ((order, width), BF16)],
        2 * apply_flops,
        info, *x_all, *k_all[:2], *g_all, link_index,
    )
    keep, send, y_own, y_core, y_far, y_cross, k_last = call(
        global_kernel,
        [((size, group), F32)] * 2 + [((rows, group), F32)] * 4 + [((2 * half, half), BF16)],
        [((2 * size, group), F32), ((order, group), F32)],
        7 * apply_flops,
        info, *k_all[2:], x_top, x_bottom, k_top, k_bottom, links, first, schur_base,
    )

    total = keep + block_swap(send, 1)
    step = 2
    while step < blocks:
        if 2 * step < blocks:
            near = total + block_swap(total, step)
            far = block_swap(total, 2 * step) + block_swap(total, 3 * step)
            total = near + far
            step *= 4
        else:
            total = total + block_swap(total, step)
            step *= 2

    def diagonal_swap(value):
        pairs = [
            (b * 4 + i, (b ^ 1) * 4 + (i ^ 2)) for b in range(blocks) for i in range(4)
        ]
        return lax.ppermute(value, ("tm", "tile"), pairs)

    here = (total, block_swap(total, 1))
    there = (tile_swap(total, 2), diagonal_swap(total))
    sums = []
    for pieces in (here, there):
        sums += [*pieces, *(tile_swap(piece, 1) for piece in pieces)]

    own_terms, off_terms, next_terms = call(
        pair_kernel,
        [((share, link + width), F32), ((share, link), F32), ((share, link + width), F32)],
        [((order, 2 * link), BF16)],
        8 * apply_flops,
        info, *p_all, x_top, x_bottom, k_top, k_bottom, k_last, links,
    )
    came = lax.ppermute(next_terms, "tm", [(i + 1, i) for i in range(blocks - 1)])
    start, scaled = call(
        start_kernel,
        [((width, 2 * width), BF16), ((rows, width), F32)],
        [],
        apply_flops,
        info, *s_all, y_own, tile_swap(y_core, 1), tile_swap(y_far, 2), tile_swap(y_cross, 3),
    )
    link_diag, link_cross, global_schur, back_cols = call(
        back_kernel,
        [((share, link), F32), ((share, width), F32), ((group, width), F32),
         ((rows, width), F32)],
        [((8 * size, group), F32), ((width, width), F32)],
        apply_flops,
        info, *sums, start, scaled, own_terms, came,
    )
    return (
        link_diag[None], off_terms[None], link_cross[None], global_schur, back_cols[None],
    )


def solution(mesh):
    return jax.shard_map(
        functools.partial(shards, mesh.shape["tm"]),
        mesh=mesh,
        in_specs=(
            P("tm", "tile", None),
            P("tm", "tile", None),
            P("tm"),
            P("tm", None),
            P("tm", "tile", None),
            P("tm", "tile", None),
            P("tile", None),
            P("tile", None),
        ),
        out_specs=(
            P("tm", "tile", None),
            P("tm", "tile", None),
            P("tm", "tile", None),
            P("tile", None),
            P("tm", "tile", None),
        ),
        check_vma=False,
    )
```

```python
import functools

import jax
import jax.numpy as jnp
from jax import lax
from jax.experimental import pallas as pl
from jax.experimental.pallas import tpu as pltpu
from jax.sharding import PartitionSpec as P

BF16 = jnp.bfloat16
F32 = jnp.float32
STEPS = 2
TERMS = 2**STEPS - 1
VMEM_BYTES = 32 * 2**20


def halves(value):
    high = value.astype(BF16)
    return high, (value - high.astype(F32)).astype(BF16)


def dot(left_side, right_side):
    return jnp.dot(left_side, right_side, preferred_element_type=F32)


def both(value):
    return jnp.concatenate(halves(value), axis=1)


def stacked(value):
    return jnp.concatenate(halves(value), axis=0)


def quadrants(product):
    rows, cols = product.shape[0] // 2, product.shape[1] // 2
    return (product[:rows, :cols] + product[:rows, cols:]) + (
        product[rows:, :cols] + product[rows:, cols:]
    )


def at_rows(start, size, unit=16):
    return pl.ds(pl.multiple_of(start, unit), size)


def live_rows(info, half):
    near, size = info[0] // 2, info[1]
    ids = lax.broadcasted_iota(jnp.int32, (half, 1), 0)
    return jnp.concatenate(
        [(ids + near * half) < size, (ids + (1 - near) * half) < size], axis=0
    )


def put_rows(info, pieces, target, offset=0):
    rows = pieces[0].shape[0]
    core = info[0] % 2
    target[at_rows(offset + core * rows, rows), :] = pieces[0]
    target[at_rows(offset + (1 - core) * rows, rows), :] = pieces[1]


def pack_kernel(info, x_rows, k_rows, out, x_part, k_part, sems):
    rows, half = x_part.shape
    unit = half // 3
    near, core = info[0] // 2, info[0] % 2
    cols = pl.ds(pl.multiple_of(near * half, 128), half)
    copies = [
        pltpu.make_async_copy(ref.at[:, cols], part, sems.at[i])
        for i, (ref, part) in enumerate(((x_rows, x_part), (k_rows, k_part)))
    ]
    for copy in copies:
        copy.start()
    large = at_rows(core * (rows - unit), unit, 8)
    small = at_rows((1 - core) * unit, rows - unit, 8)
    edge = pl.ds(pl.multiple_of(core * 2 * unit, 128), unit)
    opposite = pl.ds(pl.multiple_of((1 - core) * 2 * unit, 128), unit)
    for i, (copy, part) in enumerate(zip(copies, (x_part, k_part))):
        copy.wait()
        first = i * 3 * unit
        out[first : first + unit, :] = part[large, edge]
        out[first + unit : first + 2 * unit, :] = part[large, unit : 2 * unit]
        out[first + 2 * unit : first + unit + rows, :] = part[small, unit : 2 * unit]
        block = part[large, opposite]
        out[first + unit + rows : first + 3 * unit, :] = jnp.where(
            core == 0, block[: unit // 2, :], block.T[unit // 2 :, :]
        )


def corner(info, far, cross, target, packed, live=None):
    order = target.shape[1]
    half = order // 2
    unit = half // 3
    core = info[0] % 2
    packed[core] = far
    packed[1 - core] = cross
    zero, one = packed.at[0], packed.at[1]

    def put(row, col, value):
        first = half + row * unit
        if live is not None:
            value = jnp.where(live[first : first + unit], value, 0.0)
        high, low = halves(value)
        place = slice(half + col * unit, half + (col + 1) * unit)
        target[first : first + unit, place] = high
        target[order + first : order + first + unit, place] = low

    def joined(first, last):
        return jnp.concatenate([zero[first:last, :], one[first:last, :]], axis=0)

    put(0, 0, zero[0:unit, :])
    put(2, 2, one[0:unit, :])
    side = zero[unit : 2 * unit, :]
    put(0, 1, side)
    put(1, 0, side.T)
    side = one[unit : 2 * unit, :]
    put(2, 1, side)
    put(1, 2, side.T)
    put(1, 1, joined(2 * unit, 2 * unit + unit // 2))
    side = joined(2 * unit + unit // 2, 3 * unit)
    put(0, 2, side)
    put(2, 0, side.T)


def spread(info, own, other, target, whole, live=None):
    rows, order = own.shape
    half = order // 2
    near, core = info[0] // 2, info[0] % 2
    for ref, place in ((own, core), (other, 1 - core)):
        for side in range(2):
            cols = pl.ds(pl.multiple_of((near if side == 0 else 1 - near) * half, 128), half)
            whole[at_rows(place * rows, rows), side * half : (side + 1) * half] = ref[:, cols]
    for rows, cols, value in (
        (slice(0, half), slice(0, order), whole[...]),
        (slice(half, order), slice(0, half), whole[:, half:].T),
    ):
        if live is not None:
            value = jnp.where(live[rows], value, 0.0)
        high, low = halves(value)
        target[rows, cols] = high
        target[order + rows.start : order + rows.stop, cols] = low


def times(matrix, columns):
    return quadrants(dot(matrix[...], both(columns)))


def spread_kernel(
    info, x_own, x_core, k_own, k_core, g_own, g_core, g_far, g_cross, index,
    x, k, links, whole, gathered,
):
    half = x.shape[1] // 2
    width = g_own.shape[1]
    live = live_rows(info, half)
    spread(info, x_own, x_core, x, whole, live)
    spread(info, k_own, k_core, k, whole, live)
    put_rows(info, (g_own[...], g_core[...]), gathered)
    put_rows(info, (g_far[...], g_cross[...]), gathered, half)
    hot = lax.broadcasted_iota(jnp.int32, (width, width), 0) == index[...]
    chosen = dot(gathered[...], hot.astype(F32).astype(BF16))
    links[...] = jnp.where(live, chosen, 0.0).astype(BF16)


def global_kernel(
    info, far, cross, x_in, k_in, links, base,
    keep, send, y_own, y_core, y_far, y_cross, x, k, pack, solved, packed,
):
    del x_in, k_in
    order, width = links.shape
    half = order // 2
    rows = half // 2
    group = width // 4
    part, core = info[0], info[0] % 2
    live = live_rows(info, half)
    corner(info, far[:half, :], cross[:half, :], x, packed, live)
    columns = links[:, pl.ds(pl.multiple_of(part * group, 128), group)].astype(F32)
    value = times(x, columns)
    corner(info, far[half:, :], cross[half:, :], k, packed, live)
    value = 2.0 * columns - times(k, value)
    for step in range(TERMS - 1):
        value = columns + value - times(k, times(x, value))
    result = times(x, value)
    solved[...] = result
    y_own[...] = solved[at_rows(core * rows, rows), :]
    y_core[...] = solved[at_rows((1 - core) * rows, rows), :]
    y_far[...] = solved[at_rows(half + core * rows, rows), :]
    y_cross[...] = solved[at_rows(half + (1 - core) * rows, rows), :]
    left_side = stacked(result.T)

    def block(shift):
        place = pl.ds(pl.multiple_of(((part + shift) % 4) * group, 128), group)
        both_parts = dot(left_side, links[:, place])
        added = jnp.where(info[2] == 0, base[:, place], 0.0)
        return both_parts[:group] + both_parts[group:] + added

    pack[0:group, :] = block(0)
    pack[group : 2 * group, :] = block(1)
    across = block(2)
    pack[2 * group :, :] = jnp.where(
        part < 2, across[: group // 2, :], across.T[group // 2 :, :]
    )
    size = keep.shape[0]
    side = info[2] % 2
    keep[...] = pack[at_rows(side * size, size, 8), :]
    send[...] = pack[at_rows((1 - side) * size, size, 8), :]


def pair_kernel(
    info, p_own, p_core, p_far, p_cross, x, k, masked, columns, state, gathered
):
    half = x.shape[1] // 2
    width = p_own.shape[1]
    link = width // 2
    share = link // 4
    put_rows(info, (p_own[...], p_core[...]), gathered)
    put_rows(info, (p_far[...], p_cross[...]), gathered, half)
    masked[...] = jnp.where(live_rows(info, half), gathered[...], jnp.zeros((), BF16))
    source = lax.broadcasted_iota(jnp.int32, (width, 2 * share), 0)
    place = lax.broadcasted_iota(jnp.int32, (width, 2 * share), 1)
    wanted = info[0] * share + place + jnp.where(place < share, 0, link - share)
    chosen = dot(masked[...], (source == wanted).astype(F32).astype(BF16))
    columns[...] = chosen
    value = chosen
    for step in range(TERMS - 1):
        value = chosen + value - times(k, times(x, value))
    state[...] = value


def terms_kernel(
    info, masked, columns, state, x, k, links, own_terms, off_terms, next_terms
):
    link = masked.shape[1] // 2
    share = link // 4
    value = state[...]
    value = columns[...] + value - times(k, times(x, value))
    left_side = stacked(times(x, value).T)
    terms = dot(left_side, masked[...])
    terms = terms[: 2 * share] + terms[2 * share :]
    cross = dot(left_side, links[...])
    cross = cross[: 2 * share] + cross[2 * share :]
    next_terms[:, :link] = terms[:share, :link]
    next_terms[:, link:] = cross[:share]
    off_terms[...] = terms[:share, link:]
    own_terms[:, :link] = terms[share:, link:]
    own_terms[:, link:] = cross[share:]


def start_kernel(
    info, s_own, s_core, s_far, s_cross, y_own, y_core, y_far, y_cross, start, scaled
):
    part = info[0]
    group = s_own.shape[0]
    width = s_own.shape[1]
    total = None
    for ref, mask, rows in (
        (s_own, 0, y_own), (s_core, 1, y_core), (s_far, 2, y_far), (s_cross, 3, y_cross)
    ):
        value = both(ref[...])
        start[at_rows((part ^ mask) * group, group), :] = value
        product = quadrants(dot(stacked(rows[...]), value))
        total = product if total is None else total + product
    scaled[...] = total


def back_kernel(
    info, *refs
):
    sums, (start, scaled, own_terms, came), outs = refs[:8], refs[8:12], refs[12:]
    link_diag, link_cross, schur, back, whole, full = outs
    part, side = info[0], info[2] % 2
    size = sums[0].shape[0]
    group = schur.shape[0]
    width = schur.shape[1]
    for mask in range(4):
        for half in range(2):
            place = at_rows((part ^ mask) * (2 * size) + (side ^ half) * size, size, 8)
            whole[place, :] = sums[2 * mask + half][...]
    for row in range(4):
        first = row * 2 * size
        diagonal = whole[first : first + group, :]
        after = whole[first + group : first + 2 * group, :]
        nxt = (row + 1) % 4
        full[row * group : (row + 1) * group, row * group : (row + 1) * group] = diagonal
        full[row * group : (row + 1) * group, nxt * group : (nxt + 1) * group] = after
        full[nxt * group : (nxt + 1) * group, row * group : (row + 1) * group] = after.T
        if row < 2:
            other = (row + 2) * 2 * size
            across = jnp.concatenate(
                [whole[first + 2 * group : first + 2 * size, :],
                 whole[other + 2 * group : other + 2 * size, :]], axis=0
            )
            far = row + 2
            full[row * group : (row + 1) * group, far * group : (far + 1) * group] = across
            full[far * group : (far + 1) * group, row * group : (row + 1) * group] = across.T
    schur[...] = full[at_rows(part * group, group, 8), :]
    value = scaled[...]
    product = quadrants(dot(stacked(value), both(full[...])))
    product = quadrants(dot(stacked(product), start[...]))
    back[...] = 2.0 * value - product
    link = link_diag.shape[1]
    link_diag[...] = own_terms[:, :link] + came[:, :link]
    link_cross[...] = own_terms[:, link:] + came[:, link:]


def call(kernel, outs, scratch, info, *args, whole=False, alias={}):
    vmem = pl.BlockSpec(memory_space=pltpu.VMEM)
    return pl.pallas_call(
        kernel,
        out_shape=[jax.ShapeDtypeStruct(shape, dtype) for shape, dtype in outs],
        in_specs=[pl.BlockSpec(memory_space=pltpu.SMEM)]
        + [pl.BlockSpec(memory_space=pltpu.HBM) if whole else vmem] * len(args),
        out_specs=[vmem] * len(outs),
        scratch_shapes=scratch,
        input_output_aliases=alias,
        compiler_params=pltpu.CompilerParams(vmem_limit_bytes=VMEM_BYTES),
        cost_estimate=pl.CostEstimate(flops=0, bytes_accessed=0, transcendentals=0),
        name=kernel.__name__,
    )(info, *args)


def after(value, *others):
    return lax.optimization_barrier((value, *others))[0]


def shards(
    blocks, operator, initial, block_sizes, link_index, link_pair, link_global, schur_base,
    schur_start,
):
    part, block = lax.axis_index("tile"), lax.axis_index("tm")
    info = jnp.stack([part, block_sizes[0], block]).astype(jnp.int32)
    operator, initial = operator[0], initial[0]
    pair, glob = link_pair[0], link_global[0]
    rows, order = operator.shape
    half = order // 2
    unit = half // 3
    link, width = pair.shape[1] // 2, glob.shape[1]
    group, share = width // 4, link // 4
    size = group + group // 4

    def tile_swap(value, mask):
        return lax.ppermute(value, "tile", [(i, i ^ mask) for i in range(4)])

    def block_swap(value, mask):
        return lax.ppermute(value, "tm", [(i, i ^ mask) for i in range(blocks)])

    def diagonal_swap(value):
        pairs = [
            (b * 4 + i, (b ^ 1) * 4 + (i ^ 2)) for b in range(blocks) for i in range(4)
        ]
        return lax.ppermute(value, ("tm", "tile"), pairs)

    vmem, matrix = pltpu.VMEM, ((2 * order, order), BF16)

    g_far = tile_swap(glob, 2)
    sent = call(
        pack_kernel,
        [((6 * unit, unit), F32)],
        [vmem((rows, half), F32), vmem((rows, half), F32), pltpu.SemaphoreType.DMA((2,))],
        info, initial, operator, whole=True,
    )[0]
    far = tile_swap(sent, 2)
    x_core, k_core, g_core = (tile_swap(v, 1) for v in (initial, operator, glob))
    g_far = after(g_far, sent)
    x, k, links = call(
        spread_kernel,
        [matrix, matrix, ((order, width), BF16)],
        [vmem((half, order), F32), vmem((order, width), BF16)],
        info, initial, x_core, operator, k_core, glob, g_core, g_far, tile_swap(g_far, 1),
        link_index,
    )
    far = after(far, links)
    keep, send, y_own, y_core, y_far, y_cross, x, k = call(
        global_kernel,
        [((size, group), F32)] * 2 + [((rows, group), F32)] * 4 + [matrix, matrix],
        [vmem((2 * size, group), F32), vmem((order, group), F32),
         vmem((2, 3 * unit, unit), F32)],
        info, far, tile_swap(far, 1), x, k, links, schur_base, alias={3: 6, 4: 7},
    )
    p_far, s_far = tile_swap(after(pair, far), 2), tile_swap(after(schur_start, far), 2)

    p_far = after(p_far, keep)
    p_all = (pair, tile_swap(pair, 1), p_far, tile_swap(p_far, 1))
    masked, columns, state = call(
        pair_kernel,
        [((order, 2 * link), BF16), ((order, 2 * share), F32), ((order, 2 * share), F32)],
        [vmem((order, 2 * link), BF16)],
        info, *p_all, x, k,
    )
    y_all = (y_own, tile_swap(y_core, 1), tile_swap(y_far, 2), tile_swap(y_cross, 3))
    came = [block_swap(send, 1)]
    if blocks > 2:
        came += [block_swap(keep, 2), block_swap(send, 3)]
        came[0], state = lax.optimization_barrier((came[0], state))
        total = (keep + came[1]) + (came[0] + came[2])
    else:
        total = keep + came[0]
    s_far = after(s_far, total)
    s_all = (schur_start, tile_swap(schur_start, 1), s_far, tile_swap(s_far, 1))
    own_terms, off_terms, next_terms = call(
        terms_kernel,
        [((share, link + width), F32), ((share, link), F32), ((share, link + width), F32)],
        [],
        info, masked, columns, after(state, total), x, k, links,
    )
    step = 4
    while step < blocks:
        other = block_swap(total, step)
        if step == 4:
            other = after(other, off_terms)
        total = total + other
        step *= 2
    total, *y_all = lax.optimization_barrier((total, *y_all))
    start, scaled = call(
        start_kernel,
        [((width, 2 * width), BF16), ((rows, width), F32)],
        [],
        info, *s_all, *y_all,
    )

    here = (total, block_swap(total, 1))
    there = (tile_swap(total, 2), diagonal_swap(total))
    sums = []
    for pieces in (here, there):
        sums += [*pieces, *(tile_swap(piece, 1) for piece in pieces)]
    came = lax.ppermute(next_terms, "tm", [(i + 1, i) for i in range(blocks - 1)])
    link_diag, link_cross, global_schur, back_cols = call(
        back_kernel,
        [((share, link), F32), ((share, width), F32), ((group, width), F32),
         ((rows, width), F32)],
        [vmem((8 * size, group), F32), vmem((width, width), F32)],
        info, *sums, start, scaled, own_terms, came,
    )
    return (
        link_diag[None], off_terms[None], link_cross[None], global_schur, back_cols[None],
    )


def solution(mesh):
    return jax.shard_map(
        functools.partial(shards, mesh.shape["tm"]),
        mesh=mesh,
        in_specs=(
            P("tm", "tile", None),
            P("tm", "tile", None),
            P("tm"),
            P("tm", None),
            P("tm", "tile", None),
            P("tm", "tile", None),
            P("tile", None),
            P("tile", None),
        ),
        out_specs=(
            P("tm", "tile", None),
            P("tm", "tile", None),
            P("tm", "tile", None),
            P("tile", None),
            P("tm", "tile", None),
        ),
        check_vma=False,
    )
```

```python
import functools

import jax
import jax.numpy as jnp
from jax import lax
from jax.experimental import pallas as pl
from jax.experimental.pallas import tpu as pltpu
from jax.sharding import PartitionSpec as P

BF16 = jnp.bfloat16
F32 = jnp.float32
STEPS = 2
TERMS = 2**STEPS - 1
SPARE = 8
VMEM_BYTES = 32 * 2**20


def halves(value):
    high = value.astype(BF16)
    return high, (value - high.astype(F32)).astype(BF16)


def dot(left_side, right_side):
    return jnp.dot(left_side, right_side, preferred_element_type=F32)


def both(value):
    return jnp.concatenate(halves(value), axis=1)


def stacked(value):
    return jnp.concatenate(halves(value), axis=0)


def at(start, size, unit=16):
    return pl.ds(pl.multiple_of(start, unit), size)


def place():
    part = lax.axis_index("tile")
    return part, part // 2, part % 2


def live_rows(sizes, half):
    near, size = place()[1], sizes[0]
    ids = lax.broadcasted_iota(jnp.int32, (half, 1), 0)
    return jnp.concatenate(
        [(ids + near * half) < size, (ids + (1 - near) * half) < size], axis=0
    )


def put_rows(own, other, target, offset=0):
    rows = own.shape[0]
    core = place()[2]
    target[at(offset + core * rows, rows), :] = own[...]
    target[at(offset + (1 - core) * rows, rows), :] = other[...]


def started(*pairs, sems):
    copies = [
        pltpu.make_async_copy(source, target, sems.at[i])
        for i, (source, target) in enumerate(pairs)
    ]
    for copy in copies:
        copy.start()
    return copies


def pack_kernel(x_rows, k_rows, s_rows, x_out, k_out, s_out, x_part, k_part, sems):
    rows, half = x_part.shape
    unit = half // 3
    _, near, core = place()
    cols = at(near * half, half, 128)
    copies = started(
        (x_rows.at[:, cols], x_part),
        (k_rows.at[:, cols], k_part),
        (s_rows.at[:, at(near * s_out.shape[1], s_out.shape[1], 128)], s_out),
        sems=sems,
    )
    large = at(core * (rows - unit), unit, 8)
    small = at((1 - core) * unit, rows - unit, 8)
    edge = at(core * 2 * unit, unit, 128)
    opposite = at((1 - core) * 2 * unit, unit, 128)
    for copy, part, out in zip(copies, (x_part, k_part), (x_out, k_out)):
        copy.wait()
        out[0:unit, :] = part[large, edge]
        out[unit : 2 * unit, :] = part[large, unit : 2 * unit]
        out[2 * unit : unit + rows, :] = part[small, unit : 2 * unit]
        block = part[large, opposite]
        out[unit + rows : 3 * unit, :] = jnp.where(
            core == 0, block[: unit // 2, :], block.T[unit // 2 :, :]
        )
        out[3 * unit :, :] = jnp.zeros((out.shape[0] - 3 * unit, unit), F32)
    copies[2].wait()


def corner(far, cross, target, live):
    order = target.shape[1]
    half = order // 2
    unit = half // 3
    core = place()[2]

    def joined(first, last):
        mine, theirs = far[first:last, :], cross[first:last, :]
        return jnp.where(core == 0, mine, theirs), jnp.where(core == 0, theirs, mine)

    def put(row, col, value):
        first = half + row * unit
        high, low = halves(jnp.where(live[first : first + unit], value, 0.0))
        cols = slice(half + col * unit, half + (col + 1) * unit)
        target[first : first + unit, cols] = high
        target[order + first : order + first + unit, cols] = low

    zero, one = joined(0, unit)
    put(0, 0, zero)
    put(2, 2, one)
    zero, one = joined(unit, 2 * unit)
    put(0, 1, zero)
    put(1, 0, zero.T)
    put(2, 1, one)
    put(1, 2, one.T)
    put(1, 1, jnp.concatenate(joined(2 * unit, 2 * unit + unit // 2), axis=0))
    side = jnp.concatenate(joined(2 * unit + unit // 2, 3 * unit), axis=0)
    put(0, 2, side)
    put(2, 0, side.T)


def spread(whole, target, live):
    half, order = whole.shape
    for rows, cols, value in (
        (slice(0, half), slice(0, order), whole[...]),
        (slice(half, order), slice(0, half), whole[:, half:].T),
    ):
        high, low = halves(jnp.where(live[rows], value, 0.0))
        target[rows, cols] = high
        target[order + rows.start : order + rows.stop, cols] = low


def times(matrix, columns):
    order, width = columns.shape
    columns = both(columns)
    step = order // 2
    result = []
    for first in range(0, order, step):
        high = dot(matrix[first : first + step, :], columns)
        low = dot(matrix[order + first : order + first + step, :], columns)
        result.append((high[:, :width] + high[:, width:]) + (low[:, :width] + low[:, width:]))
    return jnp.concatenate(result, axis=0)


def times_wide(left_side, right_side):
    width = right_side.shape[1] // 2
    high, low = halves(left_side)
    product = dot(high, right_side[...])
    return (product[:, :width] + product[:, width:]) + dot(low, right_side[:, :width])


def spread_kernel(
    sizes, x_own, k_own, g_own, index, x_core, k_core, g_core, g_far, g_cross,
    x, k, links, x_whole, k_whole, gathered, g_rows, index_here, sems,
):
    half, order = x_whole.shape
    rows = half // 2
    width = links.shape[1]
    _, near, core = place()
    sides = [at(near * half, half, 128), at((1 - near) * half, half, 128)]
    pairs = [
        (own.at[:, cols], whole.at[at(core * rows, rows), side * half : (side + 1) * half])
        for own, whole in ((x_own, x_whole), (k_own, k_whole))
        for side, cols in enumerate(sides)
    ]
    copies = started(*pairs, (g_own, g_rows), (index, index_here), sems=sems)
    for other, whole in ((x_core, x_whole), (k_core, k_whole)):
        for side, cols in enumerate(sides):
            whole[at((1 - core) * rows, rows), side * half : (side + 1) * half] = other[:, cols]
    put_rows(g_far, g_cross, gathered, half)
    for copy in copies:
        copy.wait()
    put_rows(g_rows, g_core, gathered)
    live = live_rows(sizes, half)
    spread(x_whole, x, live)
    spread(k_whole, k, live)
    hot = lax.broadcasted_iota(jnp.int32, (width, width), 0) == index_here[...]
    chosen = dot(gathered[...], hot.astype(F32).astype(BF16))
    links[...] = jnp.where(live, chosen, 0.0).astype(BF16)


def first_kernel(sizes, far, cross, x_in, links, x, first):
    del x_in
    corner(far, cross, x, live_rows(sizes, x.shape[1] // 2))
    group = links.shape[1] // 4
    columns = links[:, at(place()[0] * group, group, 128)]
    product = dot(x[...], columns)
    first[...] = product[: first.shape[0]] + product[first.shape[0] :]


def global_kernel(
    sizes, far, cross, x, k_in, links, first, base,
    keep, send, y_own, y_core, y_far, y_cross, k, pack, solved,
):
    del k_in
    order, width = links.shape
    half = order // 2
    rows = half // 2
    group = width // 4
    part, _, core = place()
    block = lax.axis_index("tm")
    corner(far, cross, k, live_rows(sizes, half))
    columns = links[:, at(part * group, group, 128)].astype(F32)
    value = 2.0 * columns - times(k, first[...])
    for step in range(TERMS - 1):
        value = columns + value - times(k, times(x, value))
    result = times(x, value)
    solved[...] = result
    y_own[...] = solved[at(core * rows, rows), :]
    y_core[...] = solved[at((1 - core) * rows, rows), :]
    y_far[...] = solved[at(half + core * rows, rows), :]
    y_cross[...] = solved[at(half + (1 - core) * rows, rows), :]
    left_side = stacked(result.T)

    def square(shift):
        cols = at(((part + shift) % 4) * group, group, 128)
        parts = dot(left_side, links[:, cols])
        added = jnp.where(block == 0, base[:, cols], 0.0)
        return parts[:group] + parts[group:] + added

    pack[0:group, :] = square(0)
    pack[group : 2 * group, :] = square(1)
    across = square(2)
    pack[2 * group :, :] = jnp.where(
        part < 2, across[: group // 2, :], across.T[group // 2 :, :]
    )
    size = keep.shape[0]
    side = block % 2
    keep[...] = pack[at(side * size, size, 8), :]
    send[...] = pack[at((1 - side) * size, size, 8), :]


def pair_kernel(
    sizes, p_own, p_core, p_far, p_cross, x, k, links, own_terms, off_terms, next_terms, gathered
):
    half = x.shape[1] // 2
    width = p_own.shape[1]
    link = width // 2
    share = link // 4
    put_rows(p_own, p_core, gathered)
    put_rows(p_far, p_cross, gathered, half)
    masked = jnp.where(live_rows(sizes, half), gathered[...], jnp.zeros((), BF16))
    source = lax.broadcasted_iota(jnp.int32, (width, 2 * share), 0)
    target = lax.broadcasted_iota(jnp.int32, (width, 2 * share), 1)
    wanted = place()[0] * share + target + jnp.where(target < share, 0, link - share)
    columns = dot(masked, (source == wanted).astype(F32).astype(BF16))
    value = columns
    for step in range(TERMS):
        value = columns + value - times(k, times(x, value))
    left_side = stacked(times(x, value).T)
    terms = dot(left_side, masked)
    terms = terms[: 2 * share] + terms[2 * share :]
    cross = dot(left_side, links[...])
    cross = cross[: 2 * share] + cross[2 * share :]
    next_terms[:share, :link] = terms[:share, :link]
    next_terms[:share, link:] = cross[:share]
    next_terms[share:, :] = jnp.zeros((next_terms.shape[0] - share, next_terms.shape[1]), F32)
    off_terms[...] = terms[:share, link:]
    own_terms[:, :link] = terms[share:, link:]
    own_terms[:, link:] = cross[share:]


def start_kernel(
    s_own, s_core, s_far, s_cross, y_own, y_core, y_far, y_cross, start, scaled, s_rows, y_rows
):
    group, width = s_own.shape
    half = width // 2
    part, near, core = place()
    put_rows(s_own, s_core, s_rows)
    top, bottom = at(near * half, half), at((1 - near) * half, half)
    left, right = at(near * half, half, 128), at((1 - near) * half, half, 128)
    low_left, low_right = (at(width + v * half, half, 128) for v in (near, 1 - near))

    def put(rows, cols, low_cols, value):
        start[rows, cols], start[rows, low_cols] = halves(value)

    put(top, left, low_left, s_rows[:, left])
    side = s_rows[:, right]
    put(top, right, low_right, side)
    put(bottom, left, low_left, side.T)
    put_rows(s_far, s_cross, s_rows.at[:, :half])
    put(bottom, right, low_right, s_rows[:, :half])
    for ref, mask in ((y_own, 0), (y_core, 1), (y_far, 2), (y_cross, 3)):
        y_rows[:, at((part ^ mask) * group, group, 128)] = ref[...]
    scaled[...] = times_wide(y_rows[...], start)


def back_kernel(*refs):
    sums, (start, scaled, own_terms, came), outs = refs[:8], refs[8:12], refs[12:]
    link_diag, link_cross, schur, back, whole, full, full_parts = outs
    part = place()[0]
    side = lax.axis_index("tm") % 2
    size = sums[0].shape[0]
    group = schur.shape[0]
    for mask in range(4):
        for half in range(2):
            rows = at((part ^ mask) * (2 * size) + (side ^ half) * size, size, 8)
            whole[rows, :] = sums[2 * mask + half][...]

    def put(row, col, value):
        full[row * group : (row + 1) * group, col * group : (col + 1) * group] = value

    for row in range(4):
        first = row * 2 * size
        put(row, row, whole[first : first + group, :])
        after_it = whole[first + group : first + 2 * group, :]
        put(row, (row + 1) % 4, after_it)
        put((row + 1) % 4, row, after_it.T)
        if row < 2:
            other = (row + 2) * 2 * size
            across = jnp.concatenate(
                [whole[first + 2 * group : first + 2 * size, :],
                 whole[other + 2 * group : other + 2 * size, :]], axis=0
            )
            put(row, row + 2, across)
            put(row + 2, row, across.T)
    schur[...] = full[at(part * group, group, 8), :]
    full_parts[...] = both(full[...])
    value = scaled[...]
    back[...] = 2.0 * value - times_wide(times_wide(value, full_parts), start)
    share, link = link_diag.shape
    link_diag[...] = own_terms[:, :link] + came[:share, :link]
    link_cross[...] = own_terms[:, link:] + came[:share, link:]


def call(kernel, outs, scratch, *args, sizes=None, whole=0, alias={}):
    vmem = pl.BlockSpec(memory_space=pltpu.VMEM)
    specs = [pl.BlockSpec(memory_space=pltpu.HBM)] * whole + [vmem] * (len(args) - whole)
    if sizes is not None:
        specs, args = [pl.BlockSpec(memory_space=pltpu.SMEM), *specs], (sizes, *args)
    return pl.pallas_call(
        kernel,
        out_shape=[jax.ShapeDtypeStruct(shape, dtype) for shape, dtype in outs],
        in_specs=specs,
        out_specs=[vmem] * len(outs),
        scratch_shapes=scratch,
        input_output_aliases=alias,
        compiler_params=pltpu.CompilerParams(vmem_limit_bytes=VMEM_BYTES),
        cost_estimate=pl.CostEstimate(flops=0, bytes_accessed=0, transcendentals=0),
        name=kernel.__name__,
    )(*args)


def after(value, *others):
    return lax.optimization_barrier((value, *others))[0]


def shards(
    blocks, operator, initial, block_sizes, link_index, link_pair, link_global, schur_base,
    schur_start,
):
    operator, initial = operator[0], initial[0]
    pair, glob = link_pair[0], link_global[0]
    rows, order = operator.shape
    half = order // 2
    unit = half // 3
    link, width = pair.shape[1] // 2, glob.shape[1]
    group, share = width // 4, link // 4
    size = group + group // 4

    def tile_swap(value, mask):
        return lax.ppermute(value, "tile", [(i, i ^ mask) for i in range(4)])

    def block_swap(value, mask):
        return lax.ppermute(value, "tm", [(i, i ^ mask) for i in range(blocks)])

    def diagonal_swap(value):
        pairs = [
            (b * 4 + i, (b ^ 1) * 4 + (i ^ 2)) for b in range(blocks) for i in range(4)
        ]
        return lax.ppermute(value, ("tm", "tile"), pairs)

    vmem, dma, matrix = pltpu.VMEM, pltpu.SemaphoreType.DMA, ((2 * order, order), BF16)

    g_far = tile_swap(glob, 2)
    x_sent, k_sent, s_sent = call(
        pack_kernel,
        [((3 * unit + SPARE, unit), F32), ((3 * unit + 2 * SPARE, unit), F32),
         ((group, width // 2), F32)],
        [vmem((rows, half), F32), vmem((rows, half), F32), dma((3,))],
        initial, operator, schur_start, whole=3,
    )
    x_far, k_far = tile_swap(x_sent, 2), tile_swap(k_sent, 2)
    x_core, k_core, g_core = (tile_swap(v, 1) for v in (initial, operator, glob))
    p_core, s_core = tile_swap(pair, 1), tile_swap(schur_start, 1)
    g_far = after(g_far, x_sent)
    x, k, links = call(
        spread_kernel,
        [matrix, matrix, ((order, width), BF16)],
        [vmem((half, order), F32), vmem((half, order), F32), vmem((order, width), BF16),
         vmem((rows, width), BF16), vmem((1, width), jnp.int32), dma((6,))],
        initial, operator, glob, link_index, x_core, k_core, g_core, g_far,
        tile_swap(g_far, 1), sizes=block_sizes, whole=4,
    )
    x_far = after(x_far, x)
    x, first = call(
        first_kernel,
        [matrix, ((order, group), F32)],
        [],
        x_far, tile_swap(x_far, 1), x, links, sizes=block_sizes, alias={3: 0},
    )
    k_far, first, p_core, s_core = lax.optimization_barrier((k_far, first, p_core, s_core))
    p_far, s_far = tile_swap(after(pair, first), 2), tile_swap(after(s_sent, first), 2)
    keep, send, y_own, y_core, y_far, y_cross, k = call(
        global_kernel,
        [((size, group), F32)] * 2 + [((rows, group), F32)] * 4 + [matrix],
        [vmem((2 * size, group), F32), vmem((order, group), F32)],
        k_far, tile_swap(k_far, 1), x, k, links, first, schur_base,
        sizes=block_sizes, alias={4: 6},
    )

    p_far = after(p_far, keep)
    own_terms, off_terms, next_terms = call(
        pair_kernel,
        [((share, link + width), F32), ((share, link), F32),
         ((share + 2 * SPARE, link + width), F32)],
        [vmem((order, 2 * link), BF16)],
        pair, p_core, p_far, tile_swap(p_far, 1), x, k, links, sizes=block_sizes,
    )
    came = lax.ppermute(next_terms, "tm", [(i + 1, i) for i in range(blocks - 1)])
    y_all = (y_own, tile_swap(y_core, 1), tile_swap(y_far, 2), tile_swap(y_cross, 3))
    if blocks > 2:
        parts = [block_swap(send, 1), block_swap(keep, 2), block_swap(send, 3)]
        *parts, off_terms = lax.optimization_barrier((*parts, off_terms))
        total = (keep + parts[1]) + (parts[0] + parts[2])
    else:
        total = keep + block_swap(send, 1)
    s_far = after(s_far, total)
    s_all = (schur_start, s_core, s_far, tile_swap(s_far, 1))
    step = 4
    while step < blocks:
        total = total + block_swap(total, step)
        step *= 2
    total, *y_all = lax.optimization_barrier((total, *y_all))
    start, scaled = call(
        start_kernel,
        [((width, 2 * width), BF16), ((rows, width), F32)],
        [vmem((2 * group, width), F32), vmem((rows, width), F32)],
        *s_all, *y_all,
    )

    here = (total, block_swap(total, 1))
    there = (tile_swap(total, 2), diagonal_swap(total))
    sums = []
    for pieces in (here, there):
        sums += [*pieces, *(tile_swap(piece, 1) for piece in pieces)]
    link_diag, link_cross, global_schur, back_cols = call(
        back_kernel,
        [((share, link), F32), ((share, width), F32), ((group, width), F32),
         ((rows, width), F32)],
        [vmem((8 * size, group), F32), vmem((width, width), F32),
         vmem((width, 2 * width), BF16)],
        *sums, start, scaled, own_terms, came,
    )
    return (
        link_diag[None], off_terms[None], link_cross[None], global_schur, back_cols[None],
    )


def solution(mesh):
    return jax.shard_map(
        functools.partial(shards, mesh.shape["tm"]),
        mesh=mesh,
        in_specs=(
            P("tm", "tile", None),
            P("tm", "tile", None),
            P("tm"),
            P("tm", None),
            P("tm", "tile", None),
            P("tm", "tile", None),
            P("tile", None),
            P("tile", None),
        ),
        out_specs=(
            P("tm", "tile", None),
            P("tm", "tile", None),
            P("tm", "tile", None),
            P("tile", None),
            P("tm", "tile", None),
        ),
        check_vma=False,
    )
```

```python
import functools

import jax
import jax.numpy as jnp
from jax import lax
from jax.experimental import pallas as pl
from jax.experimental.pallas import tpu as pltpu
from jax.sharding import PartitionSpec as P

BF16 = jnp.bfloat16
F32 = jnp.float32
STEPS = 2
TERMS = 2**STEPS - 1
SPARE = 8
VMEM_BYTES = 32 * 2**20


def halves(value):
    high = value.astype(BF16)
    return high, (value - high.astype(F32)).astype(BF16)


def dot(left_side, right_side):
    return jnp.dot(left_side, right_side, preferred_element_type=F32)


def both(value):
    return jnp.concatenate(halves(value), axis=1)


def stacked(value):
    return jnp.concatenate(halves(value), axis=0)


def at(start, size, unit=16):
    return pl.ds(pl.multiple_of(start, unit), size)


def place():
    part = lax.axis_index("tile")
    return part, part // 2, part % 2


def live_rows(live):
    return live[...] > 0.0


def put_rows(own, other, target, offset=0):
    rows = own.shape[0]
    core = place()[2]
    target[at(offset + core * rows, rows), :] = own[...]
    target[at(offset + (1 - core) * rows, rows), :] = other[...]


def started(*pairs, sems):
    copies = [
        pltpu.make_async_copy(source, target, sems.at[i])
        for i, (source, target) in enumerate(pairs)
    ]
    for copy in copies:
        copy.start()
    return copies


def pack_kernel(
    x_rows, k_rows, g_rows, s_rows, index,
    x_out, k_out, x_own, k_own, g_own, s_out, index_out, sems,
):
    rows, order = x_own.shape
    half = order // 2
    unit = half // 3
    group = s_rows.shape[0]
    _, near, core = place()
    copies = started(
        (x_rows, x_own),
        (k_rows, k_own),
        (g_rows, g_own),
        (index, index_out),
        *[
            (s_rows.at[:, at((2 * near + i) * group, group, 128)], s_out.at[first : first + group, :])
            for i, first in enumerate(range(0, s_out.shape[0], group))
        ],
        sems=sems,
    )
    large = at(core * (rows - unit), unit, 8)
    small = at((1 - core) * unit, rows - unit, 8)
    edge = at(near * half + core * 2 * unit, unit, 128)
    middle = at(near * half + unit, unit, 128)
    opposite = at(near * half + (1 - core) * 2 * unit, unit, 128)
    for copy, own, out in zip(copies, (x_own, k_own), (x_out, k_out)):
        copy.wait()
        out[0:unit, :] = own[large, edge]
        out[unit : 2 * unit, :] = own[large, middle]
        out[2 * unit : unit + rows, :] = own[small, middle]
        block = own[large, opposite]
        out[unit + rows : 3 * unit, :] = jnp.where(
            core == 0, block[: unit // 2, :], block.T[unit // 2 :, :]
        )
        out[3 * unit :, :] = jnp.zeros((out.shape[0] - 3 * unit, unit), F32)
    for copy in copies[2:]:
        copy.wait()


def corner(far, cross, target, live):
    order = target.shape[1]
    half = order // 2
    unit = half // 3
    core = place()[2]

    def joined(first, last):
        mine, theirs = far[first:last, :], cross[first:last, :]
        return jnp.where(core == 0, mine, theirs), jnp.where(core == 0, theirs, mine)

    def put(row, col, value):
        first = half + row * unit
        high, low = halves(jnp.where(live[first : first + unit], value, 0.0))
        cols = slice(half + col * unit, half + (col + 1) * unit)
        target[first : first + unit, cols] = high
        target[order + first : order + first + unit, cols] = low

    zero, one = joined(0, unit)
    put(0, 0, zero)
    put(2, 2, one)
    zero, one = joined(unit, 2 * unit)
    put(0, 1, zero)
    put(1, 0, zero.T)
    put(2, 1, one)
    put(1, 2, one.T)
    put(1, 1, jnp.concatenate(joined(2 * unit, 2 * unit + unit // 2), axis=0))
    side = jnp.concatenate(joined(2 * unit + unit // 2, 3 * unit), axis=0)
    put(0, 2, side)
    put(2, 0, side.T)


def spread(whole, target, live):
    half, order = whole.shape
    for rows, cols, value in (
        (slice(0, half), slice(0, order), whole[...]),
        (slice(half, order), slice(0, half), whole[:, half:].T),
    ):
        high, low = halves(jnp.where(live[rows], value, 0.0))
        target[rows, cols] = high
        target[order + rows.start : order + rows.stop, cols] = low


def times(matrix, columns):
    order, width = columns.shape
    columns = both(columns)
    step = order // 2
    result = []
    for first in range(0, order, step):
        high = dot(matrix[first : first + step, :], columns)
        low = dot(matrix[order + first : order + first + step, :], columns)
        result.append((high[:, :width] + high[:, width:]) + (low[:, :width] + low[:, width:]))
    return jnp.concatenate(result, axis=0)


def times_wide(left_side, right_side):
    width = right_side.shape[1] // 2
    high, low = halves(left_side)
    product = dot(high, right_side[...])
    return (product[:, :width] + product[:, width:]) + dot(low, right_side[:, :width])


def spread_kernel(sizes, x_own, k_own, x_core, k_core, x, k, live_out, whole):
    half, order = whole.shape
    rows = half // 2
    _, near, core = place()
    ids = lax.broadcasted_iota(jnp.int32, (half, 1), 0)
    live = jnp.concatenate([ids + near * half, ids + (1 - near) * half], axis=0) < sizes[0]
    live_out[...] = jnp.where(live, 1.0, 0.0)
    for own, other, target in ((x_own, x_core, x), (k_own, k_core, k)):
        for side, first in enumerate((near * half, (1 - near) * half)):
            cols = slice(side * half, (side + 1) * half)
            whole[at(core * rows, rows), cols] = own[:, at(first, half, 128)]
            whole[at((1 - core) * rows, rows), cols] = other[:, at(first, half, 128)]
        spread(whole, target, live)


def first_kernel(
    live_in, far, cross, x_in, g_own, g_core, g_far, g_cross, index, x, first, links, gathered
):
    del x_in
    order, width = links.shape
    group = width // 4
    live = live_rows(live_in)
    put_rows(g_own, g_core, gathered)
    put_rows(g_far, g_cross, gathered, order // 2)
    hot = lax.broadcasted_iota(jnp.int32, (width, width), 0) == index[...]
    chosen = dot(gathered[...], hot.astype(F32).astype(BF16))
    links[...] = jnp.where(live, chosen, 0.0).astype(BF16)
    corner(far, cross, x, live)
    columns = links[:, at(place()[0] * group, group, 128)]
    product = dot(x[...], columns)
    first[...] = product[:order] + product[order:]


def global_kernel(
    live, far, cross, x, k_in, links, first, base, s_sent,
    keep, send, y_own, y_core, y_far, y_cross, k, pack, solved,
):
    del k_in
    order, width = links.shape
    half = order // 2
    rows = half // 2
    group = width // 4
    part, _, core = place()
    block = lax.axis_index("tm")
    corner(far, cross, k, live_rows(live))
    columns = links[:, at(part * group, group, 128)].astype(F32)
    value = 2.0 * columns - times(k, first[...])
    for step in range(TERMS - 1):
        value = columns + value - times(k, times(x, value))
    result = times(x, value)
    solved[...] = result
    y_own[...] = solved[at(core * rows, rows), :]
    y_core[...] = solved[at((1 - core) * rows, rows), :]
    y_far[:rows, :] = solved[at(half + core * rows, rows), :]
    y_cross[:rows, :] = solved[at(half + (1 - core) * rows, rows), :]
    y_far[rows:, :] = s_sent[...]
    y_cross[rows:, :] = s_sent[...]
    left_side = stacked(result.T)

    def square(shift):
        cols = at(((part + shift) % 4) * group, group, 128)
        parts = dot(left_side, links[:, cols])
        added = jnp.where(block == 0, base[:, cols], 0.0)
        return parts[:group] + parts[group:] + added

    pack[0:group, :] = square(0)
    pack[group : 2 * group, :] = square(1)
    across = square(2)
    pack[2 * group :, :] = jnp.where(
        part < 2, across[: group // 2, :], across.T[group // 2 :, :]
    )
    size = keep.shape[0]
    side = block % 2
    keep[...] = pack[at(side * size, size, 8), :]
    send[...] = pack[at((1 - side) * size, size, 8), :]


def pair_kernel(
    live, p_own, p_core, p_far, p_cross, x, k, links, own_terms, off_terms, next_terms, gathered
):
    half = x.shape[1] // 2
    width = p_own.shape[1]
    link = width // 2
    share = link // 4
    put_rows(p_own, p_core, gathered)
    put_rows(p_far, p_cross, gathered, half)
    masked = jnp.where(live_rows(live), gathered[...], jnp.zeros((), BF16))
    source = lax.broadcasted_iota(jnp.int32, (width, 2 * share), 0)
    target = lax.broadcasted_iota(jnp.int32, (width, 2 * share), 1)
    wanted = place()[0] * share + target + jnp.where(target < share, 0, link - share)
    columns = dot(masked, (source == wanted).astype(F32).astype(BF16))
    value = columns
    for step in range(TERMS):
        value = columns + value - times(k, times(x, value))
    left_side = stacked(times(x, value).T)
    terms = dot(left_side, masked)
    terms = terms[: 2 * share] + terms[2 * share :]
    cross = dot(left_side, links[...])
    cross = cross[: 2 * share] + cross[2 * share :]
    next_terms[:share, :link] = terms[:share, :link]
    next_terms[:share, link:] = cross[:share]
    next_terms[share:, :] = jnp.zeros((next_terms.shape[0] - share, next_terms.shape[1]), F32)
    off_terms[...] = terms[:share, link:]
    own_terms[:, :link] = terms[share:, link:]
    own_terms[:, link:] = cross[share:]


def start_kernel(s_own, s_core, y_own, y_core, far, cross, start, scaled, s_rows, y_rows):
    group, width = s_own.shape
    half = width // 2
    rows = y_own.shape[0]
    part, near, core = place()
    put_rows(s_own, s_core, s_rows)
    top, bottom = at(near * half, half), at((1 - near) * half, half)
    left, right = at(near * half, half, 128), at((1 - near) * half, half, 128)
    low_left, low_right = (at(width + v * half, half, 128) for v in (near, 1 - near))

    def put(rows, cols, low_cols, value):
        start[rows, cols], start[rows, low_cols] = halves(value)

    put(top, left, low_left, s_rows[:, left])
    side = s_rows[:, right]
    put(top, right, low_right, side)
    put(bottom, left, low_left, side.T)
    for i in range(2):
        first = slice(rows + i * group, rows + (i + 1) * group)
        put_rows(far.at[first, :], cross.at[first, :], s_rows.at[:, i * group : (i + 1) * group])
    put(bottom, right, low_right, s_rows[:, :half])
    for ref, mask in ((y_own, 0), (y_core, 1), (far, 2), (cross, 3)):
        y_rows[:, at((part ^ mask) * group, group, 128)] = ref[:rows, :]
    scaled[...] = times_wide(y_rows[...], start)


def back_kernel(*refs):
    sums, (start, scaled, own_terms, came), outs = refs[:8], refs[8:12], refs[12:]
    link_diag, link_cross, schur, back, whole, full, full_parts = outs
    part = place()[0]
    side = lax.axis_index("tm") % 2
    size = sums[0].shape[0]
    group = schur.shape[0]
    for mask in range(4):
        for half in range(2):
            rows = at((part ^ mask) * (2 * size) + (side ^ half) * size, size, 8)
            whole[rows, :] = sums[2 * mask + half][...]

    def put(row, col, value):
        full[row * group : (row + 1) * group, col * group : (col + 1) * group] = value

    for row in range(4):
        first = row * 2 * size
        put(row, row, whole[first : first + group, :])
        after_it = whole[first + group : first + 2 * group, :]
        put(row, (row + 1) % 4, after_it)
        put((row + 1) % 4, row, after_it.T)
        if row < 2:
            other = (row + 2) * 2 * size
            across = jnp.concatenate(
                [whole[first + 2 * group : first + 2 * size, :],
                 whole[other + 2 * group : other + 2 * size, :]], axis=0
            )
            put(row, row + 2, across)
            put(row + 2, row, across.T)
    schur[...] = full[at(part * group, group, 8), :]
    full_parts[...] = both(full[...])
    value = scaled[...]
    back[...] = 2.0 * value - times_wide(times_wide(value, full_parts), start)
    share, link = link_diag.shape
    link_diag[...] = own_terms[:, :link] + came[:share, :link]
    link_cross[...] = own_terms[:, link:] + came[:share, link:]


def call(kernel, outs, scratch, *args, sizes=None, whole=False, alias={}):
    vmem = pl.BlockSpec(memory_space=pltpu.VMEM)
    specs = [pl.BlockSpec(memory_space=pltpu.HBM) if whole else vmem] * len(args)
    if whole:
        args = [pltpu.with_memory_space_constraint(arg, pltpu.HBM) for arg in args]
    if sizes is not None:
        specs, args = [pl.BlockSpec(memory_space=pltpu.SMEM), *specs], (sizes, *args)
    return pl.pallas_call(
        kernel,
        out_shape=[jax.ShapeDtypeStruct(shape, dtype) for shape, dtype in outs],
        in_specs=specs,
        out_specs=[vmem] * len(outs),
        scratch_shapes=scratch,
        input_output_aliases=alias,
        compiler_params=pltpu.CompilerParams(vmem_limit_bytes=VMEM_BYTES),
        cost_estimate=pl.CostEstimate(flops=0, bytes_accessed=0, transcendentals=0),
        name=kernel.__name__,
    )(*args)


def after(value, *others):
    return lax.optimization_barrier((value, *others))[0]


def shards(
    blocks, operator, initial, block_sizes, link_index, link_pair, link_global, schur_base,
    schur_start,
):
    operator, initial = operator[0], initial[0]
    pair, glob = link_pair[0], link_global[0]
    rows, order = operator.shape
    half = order // 2
    unit = half // 3
    link, width = pair.shape[1] // 2, glob.shape[1]
    group, share = width // 4, link // 4
    size = group + group // 4

    def tile_swap(value, mask):
        return lax.ppermute(value, "tile", [(i, i ^ mask) for i in range(4)])

    def block_swap(value, mask):
        return lax.ppermute(value, "tm", [(i, i ^ mask) for i in range(blocks)])

    def diagonal_swap(value):
        pairs = [
            (b * 4 + i, (b ^ 1) * 4 + (i ^ 2)) for b in range(blocks) for i in range(4)
        ]
        return lax.ppermute(value, ("tm", "tile"), pairs)

    vmem, matrix = pltpu.VMEM, ((2 * order, order), BF16)

    g_far = tile_swap(glob, 2)
    x_sent, k_sent, x_own, k_own, g_own, s_sent, index = call(
        pack_kernel,
        [((3 * unit + SPARE, unit), F32), ((3 * unit + 4 * SPARE, unit), F32),
         ((rows, order), F32), ((rows, order), F32), ((rows, width), BF16),
         ((2 * group, group), F32), (link_index.shape, jnp.int32)],
        [pltpu.SemaphoreType.DMA((6,))],
        initial, operator, glob, schur_start, link_index, whole=True,
    )
    x_far, k_far = tile_swap(x_sent, 2), tile_swap(k_sent, 2)
    initial, operator, x_sent = lax.optimization_barrier((initial, operator, x_sent))
    x_core, k_core = tile_swap(initial, 1), tile_swap(operator, 1)
    x, k, live = call(
        spread_kernel,
        [matrix, matrix, ((order, 1), F32)],
        [vmem((half, order), F32)],
        x_own, k_own, x_core, k_core, sizes=block_sizes,
    )
    x_far, g_far = after(x_far, x), after(g_far, x)
    g_core, p_core, s_core = (tile_swap(after(v, x), 1) for v in (glob, pair, schur_start))
    x, first, links = call(
        first_kernel,
        [matrix, ((order, group), F32), ((order, width), BF16)],
        [vmem((order, width), BF16)],
        live, x_far, tile_swap(x_far, 1), x, g_own, g_core, g_far, tile_swap(g_far, 1), index,
        alias={3: 0},
    )
    pair = after(pair, x)
    p_far, p_cross = tile_swap(pair, 2), tile_swap(pair, 3)
    k_far, first, p_core, s_core = lax.optimization_barrier((k_far, first, p_core, s_core))
    keep, send, y_own, y_core, y_far, y_cross, k = call(
        global_kernel,
        [((size, group), F32)] * 2 + [((rows, group), F32)] * 2
        + [((rows + 2 * group, group), F32)] * 2 + [matrix],
        [vmem((2 * size, group), F32), vmem((order, group), F32)],
        live, k_far, tile_swap(k_far, 1), x, k, links, first, schur_base, s_sent,
        alias={4: 6},
    )

    p_far, p_cross, keep = lax.optimization_barrier((p_far, p_cross, keep))
    own_terms, off_terms, next_terms = call(
        pair_kernel,
        [((share, link + width), F32), ((share, link), F32),
         ((share + 3 * SPARE, link + width), F32)],
        [vmem((order, 2 * link), BF16)],
        live, pair, p_core, p_far, p_cross, x, k, links,
    )
    came = lax.ppermute(next_terms, "tm", [(i + 1, i) for i in range(blocks - 1)])
    y_all = (y_own, tile_swap(y_core, 1), tile_swap(y_far, 2), tile_swap(y_cross, 3))
    if blocks > 2:
        parts = [block_swap(send, 1), block_swap(keep, 2), block_swap(send, 3)]
        *parts, off_terms = lax.optimization_barrier((*parts, off_terms))
        total = (keep + parts[1]) + (parts[0] + parts[2])
    else:
        total = keep + block_swap(send, 1)
    step = 4
    while step < blocks:
        other = block_swap(total, step)
        if step == 4:
            other, *y_all = lax.optimization_barrier((other, *y_all))
        total = total + other
        step *= 2
    start, scaled = call(
        start_kernel,
        [((width, 2 * width), BF16), ((rows, width), F32)],
        [vmem((2 * group, width), F32), vmem((rows, width), F32)],
        schur_start, s_core, *y_all,
    )

    here = (total, after(block_swap(total, 1), scaled))
    there = (after(tile_swap(total, 2), scaled), after(diagonal_swap(total), scaled))
    sums = []
    for pieces in (here, there):
        sums += [*pieces, *(tile_swap(piece, 1) for piece in pieces)]
    link_diag, link_cross, global_schur, back_cols = call(
        back_kernel,
        [((share, link), F32), ((share, width), F32), ((group, width), F32),
         ((rows, width), F32)],
        [vmem((8 * size, group), F32), vmem((width, width), F32),
         vmem((width, 2 * width), BF16)],
        *sums, start, scaled, own_terms, came,
    )
    return (
        link_diag[None], off_terms[None], link_cross[None], global_schur, back_cols[None],
    )


def solution(mesh):
    return jax.shard_map(
        functools.partial(shards, mesh.shape["tm"]),
        mesh=mesh,
        in_specs=(
            P("tm", "tile", None),
            P("tm", "tile", None),
            P("tm"),
            P("tm", None),
            P("tm", "tile", None),
            P("tm", "tile", None),
            P("tile", None),
            P("tile", None),
        ),
        out_specs=(
            P("tm", "tile", None),
            P("tm", "tile", None),
            P("tm", "tile", None),
            P("tile", None),
            P("tm", "tile", None),
        ),
        check_vma=False,
    )
```

```python
import functools

import jax
import jax.numpy as jnp
from jax import lax
from jax.experimental import pallas as pl
from jax.experimental.pallas import tpu as pltpu
from jax.sharding import PartitionSpec as P

BF16 = jnp.bfloat16
F32 = jnp.float32
STEPS = 2
TERMS = 2**STEPS - 1
SPARE = 8
VMEM_BYTES = 32 * 2**20


def halves(value):
    high = value.astype(BF16)
    return high, (value - high.astype(F32)).astype(BF16)


def dot(left_side, right_side):
    return jnp.dot(left_side, right_side, preferred_element_type=F32)


def both(value):
    return jnp.concatenate(halves(value), axis=1)


def stacked(value):
    return jnp.concatenate(halves(value), axis=0)


def at(start, size, unit=16):
    return pl.ds(pl.multiple_of(start, unit), size)


def place():
    part = lax.axis_index("tile")
    return part, part // 2, part % 2


def live_rows(live):
    return live[...] > 0.0


def put_rows(own, other, target, offset=0):
    rows = own.shape[0]
    core = place()[2]
    target[at(offset + core * rows, rows), :] = own[...]
    target[at(offset + (1 - core) * rows, rows), :] = other[...]


def started(*pairs, sems):
    copies = [
        pltpu.make_async_copy(source, target, sems.at[i])
        for i, (source, target) in enumerate(pairs)
    ]
    for copy in copies:
        copy.start()
    return copies


def pack_kernel(
    x_rows, k_rows, g_rows, s_rows, index,
    x_out, k_out, x_own, k_own, g_own, s_out, index_out, sems,
):
    rows, order = x_rows.shape
    half = order // 2
    unit = half // 3
    group = s_rows.shape[0]
    _, near, core = place()
    copies = started(
        (x_rows, x_own),
        (k_rows, k_own),
        (g_rows, g_own),
        (index, index_out),
        *[
            (s_rows.at[:, at((2 * near + i) * group, group, 128)], s_out.at[first : first + group, :])
            for i, first in enumerate(range(0, s_out.shape[0], group))
        ],
        sems=sems,
    )
    edge = at(near * half + core * 2 * unit, unit, 128)
    middle = at(near * half + unit, unit, 128)
    opposite = at(near * half + (1 - core) * 2 * unit, unit, 128)
    large = at(core * (rows - unit), unit, 8)
    small = at((1 - core) * unit, rows - unit, 8)
    for copy, own, out in zip(copies, (x_own, k_own), (x_out, k_out)):
        copy.wait()
        out[0:unit, :] = own[large, edge]
        out[unit : 2 * unit, :] = own[large, middle]
        out[2 * unit : unit + rows, :] = own[small, middle]
        block = own[large, opposite]
        out[unit + rows : 3 * unit, :] = jnp.where(
            core == 0, block[: unit // 2, :], block.T[unit // 2 :, :]
        )
        out[3 * unit :, :] = jnp.zeros((out.shape[0] - 3 * unit, unit), F32)
    for copy in copies[2:]:
        copy.wait()


def corner(far, cross, target, live):
    order = target.shape[1]
    half = order // 2
    unit = half // 3
    core = place()[2]

    def joined(first, last):
        mine, theirs = far[first:last, :], cross[first:last, :]
        return jnp.where(core == 0, mine, theirs), jnp.where(core == 0, theirs, mine)

    def put(row, col, value):
        first = half + row * unit
        high, low = halves(jnp.where(live[first : first + unit], value, 0.0))
        cols = slice(half + col * unit, half + (col + 1) * unit)
        target[first : first + unit, cols] = high
        target[order + first : order + first + unit, cols] = low

    zero, one = joined(0, unit)
    put(0, 0, zero)
    put(2, 2, one)
    zero, one = joined(unit, 2 * unit)
    put(0, 1, zero)
    put(1, 0, zero.T)
    put(2, 1, one)
    put(1, 2, one.T)
    put(1, 1, jnp.concatenate(joined(2 * unit, 2 * unit + unit // 2), axis=0))
    side = jnp.concatenate(joined(2 * unit + unit // 2, 3 * unit), axis=0)
    put(0, 2, side)
    put(2, 0, side.T)


def spread(whole, target, live):
    half, order = whole.shape
    for rows, cols, value in (
        (slice(0, half), slice(0, order), whole[...]),
        (slice(half, order), slice(0, half), whole[:, half:].T),
    ):
        high, low = halves(jnp.where(live[rows], value, 0.0))
        target[rows, cols] = high
        target[order + rows.start : order + rows.stop, cols] = low


def times(matrix, columns):
    order, width = columns.shape
    columns = both(columns)
    step = order // 2
    result = []
    for first in range(0, order, step):
        high = dot(matrix[first : first + step, :], columns)
        low = dot(matrix[order + first : order + first + step, :], columns)
        result.append((high[:, :width] + high[:, width:]) + (low[:, :width] + low[:, width:]))
    return jnp.concatenate(result, axis=0)


def times_wide(left_side, right_side):
    width = right_side.shape[1] // 2
    high, low = halves(left_side)
    product = dot(high, right_side[...])
    return (product[:, :width] + product[:, width:]) + dot(low, right_side[:, :width])


def prepare_kernel(
    sizes, x_own, k_own, x_core, k_core, g_own, g_core, g_far, g_cross, index, far, cross,
    x, k, links, live_out, first, whole, gathered,
):
    half, order = whole.shape
    rows = half // 2
    width = links.shape[1]
    group = width // 4
    part, near, core = place()
    ids = lax.broadcasted_iota(jnp.int32, (half, 1), 0)
    live = jnp.concatenate([ids + near * half, ids + (1 - near) * half], axis=0) < sizes[0]
    live_out[...] = jnp.where(live, 1.0, 0.0)
    for own, other, target in ((x_own, x_core, x), (k_own, k_core, k)):
        for side, col in enumerate((near * half, (1 - near) * half)):
            cols = slice(side * half, (side + 1) * half)
            whole[at(core * rows, rows), cols] = own[:, at(col, half, 128)]
            whole[at((1 - core) * rows, rows), cols] = other[:, at(col, half, 128)]
        spread(whole, target, live)
    put_rows(g_own, g_core, gathered)
    put_rows(g_far, g_cross, gathered, half)
    hot = lax.broadcasted_iota(jnp.int32, (width, width), 0) == index[...]
    chosen = dot(gathered[...], hot.astype(F32).astype(BF16))
    links[...] = jnp.where(live, chosen, 0.0).astype(BF16)
    corner(far, cross, x, live)
    product = dot(x[...], links[:, at(part * group, group, 128)])
    first[...] = product[:order] + product[order:]


def global_kernel(
    live, far, cross, x, k_in, links, first, base, s_sent,
    keep, send, y_own, y_core, y_far, y_cross, k, pack, solved,
):
    del k_in
    order, width = links.shape
    half = order // 2
    rows = half // 2
    group = width // 4
    part, _, core = place()
    block = lax.axis_index("tm")
    corner(far, cross, k, live_rows(live))
    columns = links[:, at(part * group, group, 128)].astype(F32)
    value = 2.0 * columns - times(k, first[...])
    for step in range(TERMS - 1):
        value = columns + value - times(k, times(x, value))
    result = times(x, value)
    solved[...] = result
    y_own[...] = solved[at(core * rows, rows), :]
    y_core[...] = solved[at((1 - core) * rows, rows), :]
    y_far[:rows, :] = solved[at(half + core * rows, rows), :]
    y_cross[...] = solved[at(half + (1 - core) * rows, rows), :]
    y_far[rows:, :] = s_sent[...]
    left_side = stacked(result.T)

    def square(shift):
        cols = at(((part + shift) % 4) * group, group, 128)
        parts = dot(left_side, links[:, cols])
        added = jnp.where(block == 0, base[:, cols], 0.0)
        return parts[:group] + parts[group:] + added

    pack[0:group, :] = square(0)
    pack[group : 2 * group, :] = square(1)
    across = square(2)
    pack[2 * group :, :] = jnp.where(
        part < 2, across[: group // 2, :], across.T[group // 2 :, :]
    )
    size = keep.shape[0]
    side = block % 2
    keep[...] = pack[at(side * size, size, 8), :]
    send[...] = pack[at((1 - side) * size, size, 8), :]


def pair_kernel(
    live, p_own, p_core, p_far, p_cross, x, k, links, own_terms, off_terms, next_terms, gathered
):
    half = x.shape[1] // 2
    width = p_own.shape[1]
    link = width // 2
    share = link // 4
    put_rows(p_own, p_core, gathered)
    put_rows(p_far, p_cross, gathered, half)
    masked = jnp.where(live_rows(live), gathered[...], jnp.zeros((), BF16))
    source = lax.broadcasted_iota(jnp.int32, (width, 2 * share), 0)
    target = lax.broadcasted_iota(jnp.int32, (width, 2 * share), 1)
    wanted = place()[0] * share + target + jnp.where(target < share, 0, link - share)
    columns = dot(masked, (source == wanted).astype(F32).astype(BF16))
    value = columns
    for step in range(TERMS):
        value = columns + value - times(k, times(x, value))
    left_side = stacked(times(x, value).T)
    terms = dot(left_side, masked)
    terms = terms[: 2 * share] + terms[2 * share :]
    cross = dot(left_side, links[...])
    cross = cross[: 2 * share] + cross[2 * share :]
    next_terms[:, :link] = terms[:share, :link]
    next_terms[:, link:] = cross[:share]
    off_terms[...] = terms[:share, link:]
    own_terms[:, :link] = terms[share:, link:]
    own_terms[:, link:] = cross[share:]


def start_kernel(
    s_own, s_core, y_own, y_core, far, y_cross, s_cross, start, scaled, s_rows, y_rows
):
    group, width = s_own.shape
    half = width // 2
    rows = y_own.shape[0]
    part, near, core = place()
    put_rows(s_own, s_core, s_rows)
    top, bottom = at(near * half, half), at((1 - near) * half, half)
    left, right = at(near * half, half, 128), at((1 - near) * half, half, 128)
    low_left, low_right = (at(width + v * half, half, 128) for v in (near, 1 - near))

    def put(rows, cols, low_cols, value):
        start[rows, cols], start[rows, low_cols] = halves(value)

    put(top, left, low_left, s_rows[:, left])
    side = s_rows[:, right]
    put(top, right, low_right, side)
    put(bottom, left, low_left, side.T)
    for i in range(2):
        first = slice(rows + i * group, rows + (i + 1) * group)
        put_rows(far.at[first, :], s_cross.at[first, :], s_rows.at[:, i * group : (i + 1) * group])
    put(bottom, right, low_right, s_rows[:, :half])
    for ref, mask in ((y_own, 0), (y_core, 1), (far, 2), (y_cross, 3)):
        y_rows[:, at((part ^ mask) * group, group, 128)] = ref[:rows, :]
    scaled[...] = times_wide(y_rows[...], start)


def back_kernel(*refs):
    sums, (start, scaled, schur, back, whole, full, full_parts) = refs[:8], refs[8:]
    part = place()[0]
    side = lax.axis_index("tm") % 2
    size = sums[0].shape[0]
    group = schur.shape[0]
    for mask in range(4):
        for half in range(2):
            rows = at((part ^ mask) * (2 * size) + (side ^ half) * size, size, 8)
            whole[rows, :] = sums[2 * mask + half][...]

    def put(row, col, value):
        full[row * group : (row + 1) * group, col * group : (col + 1) * group] = value

    for row in range(4):
        first = row * 2 * size
        put(row, row, whole[first : first + group, :])
        after_it = whole[first + group : first + 2 * group, :]
        put(row, (row + 1) % 4, after_it)
        put((row + 1) % 4, row, after_it.T)
        if row < 2:
            other = (row + 2) * 2 * size
            across = jnp.concatenate(
                [whole[first + 2 * group : first + 2 * size, :],
                 whole[other + 2 * group : other + 2 * size, :]], axis=0
            )
            put(row, row + 2, across)
            put(row + 2, row, across.T)
    schur[...] = full[at(part * group, group, 8), :]
    full_parts[...] = both(full[...])
    value = scaled[...]
    back[...] = 2.0 * value - times_wide(times_wide(value, full_parts), start)


def finish_kernel(own_terms, came, link_diag, link_cross):
    link = link_diag.shape[1]
    link_diag[...] = own_terms[:, :link] + came[:, :link]
    link_cross[...] = own_terms[:, link:] + came[:, link:]


def call(kernel, outs, scratch, *args, sizes=None, whole=False, alias={}, flops=0):
    vmem = pl.BlockSpec(memory_space=pltpu.VMEM)
    specs = [pl.BlockSpec(memory_space=pltpu.HBM) if whole else vmem] * len(args)
    if whole:
        args = [pltpu.with_memory_space_constraint(arg, pltpu.HBM) for arg in args]
    if sizes is not None:
        specs, args = [pl.BlockSpec(memory_space=pltpu.SMEM), *specs], (sizes, *args)
    return pl.pallas_call(
        kernel,
        out_shape=[jax.ShapeDtypeStruct(shape, dtype) for shape, dtype in outs],
        in_specs=specs,
        out_specs=[vmem] * len(outs),
        scratch_shapes=scratch,
        input_output_aliases=alias,
        compiler_params=pltpu.CompilerParams(vmem_limit_bytes=VMEM_BYTES),
        cost_estimate=pl.CostEstimate(flops=flops, bytes_accessed=0, transcendentals=0),
        name=kernel.__name__,
    )(*args)


def after(value, *others):
    return lax.optimization_barrier((value, *others))[0]


def shards(
    blocks, operator, initial, block_sizes, link_index, link_pair, link_global, schur_base,
    schur_start,
):
    operator, initial = operator[0], initial[0]
    pair, glob = link_pair[0], link_global[0]
    rows, order = operator.shape
    half = order // 2
    unit = half // 3
    link, width = pair.shape[1] // 2, glob.shape[1]
    group, share = width // 4, link // 4
    size = group + group // 4

    def tile_swap(value, mask):
        return lax.ppermute(value, "tile", [(i, i ^ mask) for i in range(4)])

    def block_swap(value, mask):
        return lax.ppermute(value, "tm", [(i, i ^ mask) for i in range(blocks)])

    def diagonal_swap(value):
        pairs = [
            (b * 4 + i, (b ^ 1) * 4 + (i ^ 2)) for b in range(blocks) for i in range(4)
        ]
        return lax.ppermute(value, ("tm", "tile"), pairs)

    vmem, matrix = pltpu.VMEM, ((2 * order, order), BF16)

    g_far = tile_swap(glob, 2)
    x_sent, k_sent, x_own, k_own, g_own, s_sent, index = call(
        pack_kernel,
        [((3 * unit + SPARE, unit), F32), ((3 * unit + 4 * SPARE, unit), F32),
         ((rows, order), F32), ((rows, order), F32), ((rows, width), BF16), ((2 * group, group), F32),
         (link_index.shape, jnp.int32)],
        [pltpu.SemaphoreType.DMA((6,))],
        initial, operator, glob, schur_start, link_index, whole=True,
    )
    x_far, k_far = tile_swap(x_sent, 2), tile_swap(k_sent, 2)
    g_far = after(g_far, x_sent)
    g_cross = tile_swap(g_far, 1)
    x_far, g_cross = lax.optimization_barrier((x_far, g_cross))
    x, k, links, live, first = call(
        prepare_kernel,
        [matrix, matrix, ((order, width), BF16), ((order, 1), F32), ((order, group), F32)],
        [vmem((half, order), F32), vmem((order, width), BF16)],
        x_own, k_own, tile_swap(x_own, 1), tile_swap(k_own, 1), g_own, tile_swap(g_own, 1), g_far, g_cross, index,
        x_far, tile_swap(x_far, 1), sizes=block_sizes,
    )
    k_far = after(k_far, first)
    p_core, p_far, s_core = (
        tile_swap(after(v, first), m) for v, m in ((pair, 1), (pair, 2), (schur_start, 1))
    )
    keep, send, y_own, y_core, y_far, y_cross, k = call(
        global_kernel,
        [((size, group), F32)] * 2 + [((rows, group), F32)] * 2
        + [((rows + 2 * group, group), F32), ((rows, group), F32), matrix],
        [vmem((2 * size, group), F32), vmem((order, group), F32)],
        live, k_far, tile_swap(k_far, 1), x, k, links, first, schur_base, s_sent,
        alias={4: 6},
    )

    y_all = (y_own, tile_swap(y_core, 1), tile_swap(y_far, 2), tile_swap(y_cross, 3))
    if blocks > 2:
        parts = [block_swap(send, 1), block_swap(keep, 2), block_swap(send, 3)]
        total = (keep + parts[1]) + (parts[0] + parts[2])
    else:
        total = keep + block_swap(send, 1)
    p_far = after(p_far, keep)
    own_terms, off_terms, next_terms = call(
        pair_kernel,
        [((share, link + width), F32), ((share, link), F32), ((share, link + width), F32)],
        [vmem((order, 2 * link), BF16)],
        live, pair, p_core, p_far, tile_swap(p_far, 1), x, k, after(links, total),
    )
    step = 4
    while step < blocks:
        other = block_swap(total, step)
        if step == 4:
            other, off_terms, *y_all = lax.optimization_barrier((other, off_terms, *y_all))
        total = total + other
        step *= 2
    start, scaled = call(
        start_kernel,
        [((width, 2 * width), BF16), ((rows, width), F32)],
        [vmem((2 * group, width), F32), vmem((rows, width), F32)],
        schur_start, s_core, *y_all, tile_swap(after(y_all[2], total), 1),
    )

    here = (total, after(block_swap(total, 1), scaled))
    there = (after(tile_swap(total, 2), scaled), after(diagonal_swap(total), scaled))
    sums = []
    for pieces in (here, there):
        sums += [*pieces, *(tile_swap(piece, 1) for piece in pieces)]
    global_schur, back_cols = call(
        back_kernel,
        [((group, width), F32), ((rows, width), F32)],
        [vmem((8 * size, group), F32), vmem((width, width), F32),
         vmem((width, 2 * width), BF16)],
        *sums, start, scaled, flops=2 * rows * order * order * 2,
    )
    next_terms = after(next_terms, scaled)
    came = lax.ppermute(next_terms, "tm", [(i + 1, i) for i in range(blocks - 1)])
    link_diag, link_cross = call(
        finish_kernel,
        [((share, link), F32), ((share, width), F32)],
        [],
        own_terms, came,
    )
    return (
        link_diag[None], off_terms[None], link_cross[None], global_schur, back_cols[None],
    )


def solution(mesh):
    return jax.shard_map(
        functools.partial(shards, mesh.shape["tm"]),
        mesh=mesh,
        in_specs=(
            P("tm", "tile", None),
            P("tm", "tile", None),
            P("tm"),
            P("tm", None),
            P("tm", "tile", None),
            P("tm", "tile", None),
            P("tile", None),
            P("tile", None),
        ),
        out_specs=(
            P("tm", "tile", None),
            P("tm", "tile", None),
            P("tm", "tile", None),
            P("tile", None),
            P("tm", "tile", None),
        ),
        check_vma=False,
    )
```

```python
import functools

import jax
import jax.numpy as jnp
from jax import lax
from jax.experimental import pallas as pl
from jax.experimental.pallas import tpu as pltpu
from jax.sharding import PartitionSpec as P

BF16 = jnp.bfloat16
F32 = jnp.float32
STEPS = 2
TERMS = 2**STEPS - 1
SPARE = 8
VMEM_BYTES = 32 * 2**20


def halves(value):
    high = value.astype(BF16)
    return high, (value - high.astype(F32)).astype(BF16)


def dot(left_side, right_side):
    return jnp.dot(left_side, right_side, preferred_element_type=F32)


def both(value):
    return jnp.concatenate(halves(value), axis=1)


def stacked(value):
    return jnp.concatenate(halves(value), axis=0)


def at(start, size, unit=16):
    return pl.ds(pl.multiple_of(start, unit), size)


def place():
    part = lax.axis_index("tile")
    return part, part // 2, part % 2


def put_rows(own, other, target, offset=0):
    rows = own.shape[0]
    core = place()[2]
    target[at(offset + core * rows, rows), :] = own[...]
    target[at(offset + (1 - core) * rows, rows), :] = other[...]


def started(*pairs, sems):
    copies = [
        pltpu.make_async_copy(source, target, sems.at[i])
        for i, (source, target) in enumerate(pairs)
    ]
    for copy in copies:
        copy.start()
    return copies


def pack_kernel(
    x_rows, k_rows, g_rows, s_rows, index,
    x_out, k_out, x_own, k_own, g_own, s_out, index_out, sems,
):
    rows, order = x_rows.shape
    half = order // 2
    unit = half // 3
    group = s_rows.shape[0]
    _, near, core = place()
    copies = started(
        (x_rows, x_own),
        (k_rows, k_own),
        (g_rows, g_own),
        (index, index_out),
        *[
            (s_rows.at[:, at((2 * near + i) * group, group, 128)], s_out.at[first : first + group, :])
            for i, first in enumerate(range(0, s_out.shape[0], group))
        ],
        sems=sems,
    )
    edge = at(near * half + core * 2 * unit, unit, 128)
    middle = at(near * half + unit, unit, 128)
    opposite = at(near * half + (1 - core) * 2 * unit, unit, 128)
    large = at(core * (rows - unit), unit, 8)
    small = at((1 - core) * unit, rows - unit, 8)
    for copy, own, out in zip(copies, (x_own, k_own), (x_out, k_out)):
        copy.wait()
        out[0:unit, :] = own[large, edge]
        out[unit : 2 * unit, :] = own[large, middle]
        out[2 * unit : unit + rows, :] = own[small, middle]
        block = own[large, opposite]
        out[unit + rows : 3 * unit, :] = jnp.where(
            core == 0, block[: unit // 2, :], block.T[unit // 2 :, :]
        )
        out[3 * unit :, :] = jnp.zeros((out.shape[0] - 3 * unit, unit), F32)
    for copy in copies[2:]:
        copy.wait()


def corner(far, cross, target, live):
    order = target.shape[1]
    half = order // 2
    unit = half // 3
    core = place()[2]

    def joined(first, last):
        mine, theirs = far[first:last, :], cross[first:last, :]
        return jnp.where(core == 0, mine, theirs), jnp.where(core == 0, theirs, mine)

    def put(row, col, value):
        first = half + row * unit
        cols = slice(half + col * unit, half + (col + 1) * unit)
        high, low = halves(value * live[:, cols])
        target[first : first + unit, cols] = high
        target[order + first : order + first + unit, cols] = low

    zero, one = joined(0, unit)
    put(0, 0, zero)
    put(2, 2, one)
    zero, one = joined(unit, 2 * unit)
    put(0, 1, zero)
    put(1, 0, zero.T)
    put(2, 1, one)
    put(1, 2, one.T)
    put(1, 1, jnp.concatenate(joined(2 * unit, 2 * unit + unit // 2), axis=0))
    side = jnp.concatenate(joined(2 * unit + unit // 2, 3 * unit), axis=0)
    put(0, 2, side)
    put(2, 0, side.T)


def spread(whole, target, live):
    half, order = whole.shape
    for rows, cols, value in (
        (slice(0, half), slice(0, order), whole[...]),
        (slice(half, order), slice(0, half), whole[:, half:].T),
    ):
        high, low = halves(value * live[:, cols])
        target[rows, cols] = high
        target[order + rows.start : order + rows.stop, cols] = low


def times(rows, matrix):
    count, order = rows.shape
    high = rows.astype(BF16)
    parts = stacked(rows)
    result = []
    for first in range(0, order, 256):
        cols = slice(first, min(first + 256, order))
        product = dot(parts, matrix[:order, cols])
        result.append((product[:count] + product[count:]) + dot(high, matrix[order:, cols]))
    return jnp.concatenate(result, axis=1)


def times_wide(left_side, right_side):
    width = right_side.shape[1] // 2
    high, low = halves(left_side)
    product = dot(high, right_side[...])
    return (product[:, :width] + product[:, width:]) + dot(low, right_side[:, :width])


def prepare_kernel(
    sizes, x_own, k_own, x_core, k_core, g_own, g_core, g_far, g_cross, index, far, cross,
    x, k, links, live_rows, live_cols, columns, first, whole, gathered,
):
    half, order = whole.shape
    rows = half // 2
    width = links.shape[1]
    group = width // 4
    part, near, core = place()
    for out, axis in ((live_rows, 0), (live_cols, 1)):
        ids = lax.broadcasted_iota(jnp.int32, out.shape, axis)
        ids = jnp.where(ids < half, ids + near * half, ids - near * half)
        out[...] = jnp.where(ids < sizes[0], 1.0, 0.0)
    for own, other, target in ((x_own, x_core, x), (k_own, k_core, k)):
        for side, col in enumerate((near * half, (1 - near) * half)):
            cols = slice(side * half, (side + 1) * half)
            whole[at(core * rows, rows), cols] = own[:, at(col, half, 128)]
            whole[at((1 - core) * rows, rows), cols] = other[:, at(col, half, 128)]
        spread(whole, target, live_cols)
    put_rows(g_own, g_core, gathered)
    put_rows(g_far, g_cross, gathered, half)
    hot = lax.broadcasted_iota(jnp.int32, (width, width), 0) == index[...]
    chosen = dot(gathered[...], hot.astype(F32).astype(BF16))
    links[...] = (chosen * live_rows[...]).astype(BF16)
    corner(far, cross, x, live_cols)
    value = links[:, at(part * group, group, 128)].astype(F32).T
    columns[...] = value
    high = value.astype(BF16)
    first[...] = dot(high, x[:order, :]) + dot(high, x[order:, :])


def global_kernel(
    live, far, cross, x, k_in, links, columns, first, base, s_sent,
    keep, send, y_own, y_core, y_far, k, pack, solved,
):
    del k_in
    order, width = links.shape
    half = order // 2
    rows = half // 2
    group = width // 4
    part, _, core = place()
    block = lax.axis_index("tm")
    corner(far, cross, k, live)
    value = 2.0 * columns[...] - times(first[...], k)
    for step in range(TERMS - 1):
        value = columns[...] + value - times(times(value, x), k)
    result = times(value, x)
    left_side = stacked(result)
    solved[...] = result.T
    y_own[...] = solved[at(core * rows, rows), :]
    y_core[...] = solved[at((1 - core) * rows, rows), :]
    y_far[:rows, :] = solved[at(half + core * rows, rows), :]
    y_far[rows : 2 * rows, :] = solved[at(half + (1 - core) * rows, rows), :]
    y_far[2 * rows :, :] = s_sent[...]

    def square(shift):
        cols = at(((part + shift) % 4) * group, group, 128)
        parts = dot(left_side, links[:, cols])
        added = jnp.where(block == 0, base[:, cols], 0.0)
        return parts[:group] + parts[group:] + added

    pack[0:group, :] = square(0)
    pack[group : 2 * group, :] = square(1)
    across = square(2)
    pack[2 * group :, :] = jnp.where(
        part < 2, across[: group // 2, :], across.T[group // 2 :, :]
    )
    size = keep.shape[0]
    side = block % 2
    keep[...] = pack[at(side * size, size, 8), :]
    send[...] = pack[at((1 - side) * size, size, 8), :]


def pair_kernel(
    live, p_own, p_core, p_far, p_cross, x, k, links, own_terms, off_terms, next_terms, gathered
):
    half = x.shape[1] // 2
    width = p_own.shape[1]
    link = width // 2
    share = link // 4
    put_rows(p_own, p_core, gathered)
    put_rows(p_far, p_cross, gathered, half)
    masked = gathered[...] * live[...].astype(BF16)
    source = lax.broadcasted_iota(jnp.int32, (width, 2 * share), 0)
    target = lax.broadcasted_iota(jnp.int32, (width, 2 * share), 1)
    wanted = place()[0] * share + target + jnp.where(target < share, 0, link - share)
    columns = dot(masked, (source == wanted).astype(F32).astype(BF16)).T
    value = columns
    for step in range(TERMS):
        value = columns + value - times(times(value, x), k)
    left_side = stacked(times(value, x))
    terms = dot(left_side, masked)
    terms = terms[: 2 * share] + terms[2 * share :]
    cross = dot(left_side, links[...])
    cross = cross[: 2 * share] + cross[2 * share :]
    next_terms[:, :link] = terms[:share, :link]
    next_terms[:, link:] = cross[:share]
    off_terms[...] = terms[:share, link:]
    own_terms[:, :link] = terms[share:, link:]
    own_terms[:, link:] = cross[share:]


def start_kernel(
    s_own, s_core, y_own, y_core, far, cross, start, scaled, s_rows, y_rows
):
    group, width = s_own.shape
    half = width // 2
    rows = y_own.shape[0]
    part, near, core = place()
    put_rows(s_own, s_core, s_rows)
    top, bottom = at(near * half, half), at((1 - near) * half, half)
    left, right = at(near * half, half, 128), at((1 - near) * half, half, 128)
    low_left, low_right = (at(width + v * half, half, 128) for v in (near, 1 - near))

    def put(rows, cols, low_cols, value):
        start[rows, cols], start[rows, low_cols] = halves(value)

    put(top, left, low_left, s_rows[:, left])
    side = s_rows[:, right]
    put(top, right, low_right, side)
    put(bottom, left, low_left, side.T)
    for i in range(2):
        first = slice(2 * rows + i * group, 2 * rows + (i + 1) * group)
        put_rows(far.at[first, :], cross.at[first, :], s_rows.at[:, i * group : (i + 1) * group])
    put(bottom, right, low_right, s_rows[:, :half])
    for ref, mask in ((y_own, 0), (y_core, 1), (far, 2), (cross.at[rows:, :], 3)):
        y_rows[:, at((part ^ mask) * group, group, 128)] = ref[:rows, :]
    scaled[...] = times_wide(y_rows[...], start)


def back_kernel(*refs):
    sums, (start, scaled, schur, back, whole, full, full_parts) = refs[:8], refs[8:]
    part = place()[0]
    side = lax.axis_index("tm") % 2
    size = sums[0].shape[0]
    group = schur.shape[0]
    for mask in range(4):
        for half in range(2):
            rows = at((part ^ mask) * (2 * size) + (side ^ half) * size, size, 8)
            whole[rows, :] = sums[2 * mask + half][...]

    def put(row, col, value):
        full[row * group : (row + 1) * group, col * group : (col + 1) * group] = value

    for row in range(4):
        first = row * 2 * size
        put(row, row, whole[first : first + group, :])
        after_it = whole[first + group : first + 2 * group, :]
        put(row, (row + 1) % 4, after_it)
        put((row + 1) % 4, row, after_it.T)
        if row < 2:
            other = (row + 2) * 2 * size
            across = jnp.concatenate(
                [whole[first + 2 * group : first + 2 * size, :],
                 whole[other + 2 * group : other + 2 * size, :]], axis=0
            )
            put(row, row + 2, across)
            put(row + 2, row, across.T)
    schur[...] = full[at(part * group, group, 8), :]
    full_parts[...] = both(full[...])
    value = scaled[...]
    back[...] = 2.0 * value - times_wide(times_wide(value, full_parts), start)


def finish_kernel(own_terms, came, link_diag, link_cross):
    link = link_diag.shape[1]
    there = lax.axis_index("tm") + 1 < lax.axis_size("tm")
    link_diag[...] = own_terms[:, :link] + jnp.where(there, came[:, :link], 0.0)
    link_cross[...] = own_terms[:, link:] + jnp.where(there, came[:, link:], 0.0)


def call(kernel, outs, scratch, *args, sizes=None, whole=False, alias={}, flops=0):
    vmem = pl.BlockSpec(memory_space=pltpu.VMEM)
    specs = [pl.BlockSpec(memory_space=pltpu.HBM) if whole else vmem] * len(args)
    if whole:
        args = [pltpu.with_memory_space_constraint(arg, pltpu.HBM) for arg in args]
    if sizes is not None:
        specs, args = [pl.BlockSpec(memory_space=pltpu.SMEM), *specs], (sizes, *args)
    return pl.pallas_call(
        kernel,
        out_shape=[jax.ShapeDtypeStruct(shape, dtype) for shape, dtype in outs],
        in_specs=specs,
        out_specs=[vmem] * len(outs),
        scratch_shapes=scratch,
        input_output_aliases=alias,
        compiler_params=pltpu.CompilerParams(vmem_limit_bytes=VMEM_BYTES),
        cost_estimate=pl.CostEstimate(flops=flops, bytes_accessed=0, transcendentals=0),
        name=kernel.__name__,
    )(*args)


def after(value, *others):
    return lax.optimization_barrier((value, *others))[0]


def shards(
    blocks, operator, initial, block_sizes, link_index, link_pair, link_global, schur_base,
    schur_start,
):
    operator, initial = operator[0], initial[0]
    pair, glob = link_pair[0], link_global[0]
    rows, order = operator.shape
    half = order // 2
    unit = half // 3
    link, width = pair.shape[1] // 2, glob.shape[1]
    group, share = width // 4, link // 4
    size = group + group // 4

    def tile_swap(value, mask):
        return lax.ppermute(value, "tile", [(i, i ^ mask) for i in range(4)])

    def block_swap(value, mask):
        return lax.ppermute(value, "tm", [(i, i ^ mask) for i in range(blocks)])

    def diagonal_swap(value):
        pairs = [
            (b * 4 + i, (b ^ 1) * 4 + (i ^ 2)) for b in range(blocks) for i in range(4)
        ]
        return lax.ppermute(value, ("tm", "tile"), pairs)

    vmem, matrix = pltpu.VMEM, ((2 * order, order), BF16)

    g_far = tile_swap(glob, 2)
    x_sent, k_sent, x_own, k_own, g_own, s_sent, index = call(
        pack_kernel,
        [((3 * unit + SPARE, unit), F32), ((3 * unit + 4 * SPARE, unit), F32),
         ((rows, order), F32), ((rows, order), F32), ((rows, width), BF16), ((2 * group, group), F32),
         (link_index.shape, jnp.int32)],
        [pltpu.SemaphoreType.DMA((6,))],
        initial, operator, glob, schur_start, link_index, whole=True,
    )
    x_far, k_far = tile_swap(x_sent, 2), tile_swap(k_sent, 2)
    g_far = after(g_far, x_sent)
    g_cross = tile_swap(g_far, 1)
    x_far, g_cross = lax.optimization_barrier((x_far, g_cross))
    x, k, links, live_rows, live_cols, columns, first = call(
        prepare_kernel,
        [matrix, matrix, ((order, width), BF16), ((order, 1), F32), ((1, order), F32),
         ((group, order), F32), ((group, order), F32)],
        [vmem((half, order), F32), vmem((order, width), BF16)],
        x_own, k_own, tile_swap(x_own, 1), tile_swap(k_own, 1), g_own, tile_swap(g_own, 1), g_far, g_cross, index,
        x_far, tile_swap(x_far, 1), sizes=block_sizes,
    )
    k_far = after(k_far, first)
    p_core, p_far, s_core = (
        tile_swap(after(v, first), m) for v, m in ((pair, 1), (pair, 2), (schur_start, 1))
    )
    keep, send, y_own, y_core, y_far, k = call(
        global_kernel,
        [((size, group), F32)] * 2 + [((rows, group), F32)] * 2
        + [((2 * rows + 2 * group, group), F32), matrix],
        [vmem((2 * size, group), F32), vmem((order, group), F32)],
        live_cols, k_far, tile_swap(k_far, 1), x, k, links, columns, first, schur_base, s_sent,
        alias={4: 5},
    )

    y_all = (y_own, tile_swap(y_core, 1), tile_swap(y_far, 2))
    if blocks > 2:
        parts = [block_swap(send, 1), block_swap(keep, 2), block_swap(send, 3)]
        total = (keep + parts[1]) + (parts[0] + parts[2])
    else:
        total = keep + block_swap(send, 1)
    p_far = after(p_far, keep)
    own_terms, off_terms, next_terms = call(
        pair_kernel,
        [((share, link + width), F32), ((share, link), F32), ((share, link + width), F32)],
        [vmem((order, 2 * link), BF16)],
        live_rows, pair, p_core, p_far, tile_swap(p_far, 1), x, k, after(links, total),
    )
    step = 4
    while step < blocks:
        other = block_swap(total, step)
        if step == 4:
            other, off_terms, *y_all = lax.optimization_barrier((other, off_terms, *y_all))
        total = total + other
        step *= 2
    start, scaled = call(
        start_kernel,
        [((width, 2 * width), BF16), ((rows, width), F32)],
        [vmem((2 * group, width), F32), vmem((rows, width), F32)],
        schur_start, s_core, *y_all, tile_swap(after(y_all[2], total), 1),
    )

    here = (total, after(block_swap(total, 1), scaled))
    there = (after(tile_swap(total, 2), scaled), after(diagonal_swap(total), scaled))
    sums = []
    for pieces in (here, there):
        sums += [*pieces, *(tile_swap(piece, 1) for piece in pieces)]
    global_schur, back_cols = call(
        back_kernel,
        [((group, width), F32), ((rows, width), F32)],
        [vmem((8 * size, group), F32), vmem((width, width), F32),
         vmem((width, 2 * width), BF16)],
        *sums, start, scaled, flops=2 * rows * order * order * 2,
    )
    next_terms = after(next_terms, scaled)
    came = lax.ppermute(next_terms, "tm", [(i, (i - 1) % blocks) for i in range(blocks)])
    link_diag, link_cross = call(
        finish_kernel,
        [((share, link), F32), ((share, width), F32)],
        [],
        own_terms, came,
    )
    return (
        link_diag[None], off_terms[None], link_cross[None], global_schur, back_cols[None],
    )


def solution(mesh):
    return jax.shard_map(
        functools.partial(shards, mesh.shape["tm"]),
        mesh=mesh,
        in_specs=(
            P("tm", "tile", None),
            P("tm", "tile", None),
            P("tm"),
            P("tm", None),
            P("tm", "tile", None),
            P("tm", "tile", None),
            P("tile", None),
            P("tile", None),
        ),
        out_specs=(
            P("tm", "tile", None),
            P("tm", "tile", None),
            P("tm", "tile", None),
            P("tile", None),
            P("tm", "tile", None),
        ),
        check_vma=False,
    )
```

```python
import functools

import jax
import jax.numpy as jnp
from jax import lax
from jax.experimental import pallas as pl
from jax.experimental.pallas import tpu as pltpu
from jax.sharding import PartitionSpec as P

BF16 = jnp.bfloat16
F32 = jnp.float32
STEPS = 2
TERMS = 2**STEPS - 1
SPARE = 8
VMEM_BYTES = 32 * 2**20


def halves(value):
    high = value.astype(BF16)
    return high, (value - high.astype(F32)).astype(BF16)


def dot(left_side, right_side):
    return jnp.dot(left_side, right_side, preferred_element_type=F32)


def both(value):
    return jnp.concatenate(halves(value), axis=1)


def stacked(value):
    return jnp.concatenate(halves(value), axis=0)


def at(start, size, unit=16):
    return pl.ds(pl.multiple_of(start, unit), size)


def place():
    part = lax.axis_index("tile")
    return part, part // 2, part % 2


def put_rows(own, other, target, offset=0):
    rows = own.shape[0]
    core = place()[2]
    target[at(offset + core * rows, rows), :] = own[...]
    target[at(offset + (1 - core) * rows, rows), :] = other[...]


def started(*pairs, sems):
    copies = [
        pltpu.make_async_copy(source, target, sems.at[i])
        for i, (source, target) in enumerate(pairs)
    ]
    for copy in copies:
        copy.start()
    return copies


def pack_kernel(
    x_rows, k_rows, g_rows, s_rows, index,
    x_out, k_out, x_own, k_own, g_own, s_out, index_out, sems,
):
    rows, order = x_rows.shape
    half = order // 2
    unit = half // 3
    group = s_rows.shape[0]
    _, near, core = place()
    copies = started(
        (x_rows, x_own),
        (k_rows, k_own),
        (g_rows, g_own),
        (index, index_out),
        *[
            (s_rows.at[:, first : first + group], s_out.at[first : first + group, :])
            for first in range(0, s_out.shape[0], group)
        ],
        sems=sems,
    )
    edge = at(near * half + core * 2 * unit, unit, 128)
    middle = at(near * half + unit, unit, 128)
    opposite = at(near * half + (1 - core) * 2 * unit, unit, 128)
    large = at(core * (rows - unit), unit, 8)
    small = at((1 - core) * unit, rows - unit, 8)
    for copy, own, out in zip(copies, (x_own, k_own), (x_out, k_out)):
        copy.wait()
        out[0:unit, :] = own[large, edge]
        out[unit : 2 * unit, :] = own[large, middle]
        out[2 * unit : unit + rows, :] = own[small, middle]
        block = own[large, opposite]
        out[unit + rows : 3 * unit, :] = jnp.where(
            core == 0, block[: unit // 2, :], block.T[unit // 2 :, :]
        )
        out[3 * unit :, :] = jnp.zeros((out.shape[0] - 3 * unit, unit), F32)
    for copy in copies[2:]:
        copy.wait()


def corner(far, cross, target, live):
    order = target.shape[1]
    half = order // 2
    unit = half // 3
    core = place()[2]

    def joined(first, last):
        mine, theirs = far[first:last, :], cross[first:last, :]
        return jnp.where(core == 0, mine, theirs), jnp.where(core == 0, theirs, mine)

    def put(row, col, value):
        first = half + row * unit
        cols = slice(half + col * unit, half + (col + 1) * unit)
        high, low = halves(value * live[:, cols])
        target[first : first + unit, cols] = high
        target[order + first : order + first + unit, cols] = low

    zero, one = joined(0, unit)
    put(0, 0, zero)
    put(2, 2, one)
    zero, one = joined(unit, 2 * unit)
    put(0, 1, zero)
    put(1, 0, zero.T)
    put(2, 1, one)
    put(1, 2, one.T)
    put(1, 1, jnp.concatenate(joined(2 * unit, 2 * unit + unit // 2), axis=0))
    side = jnp.concatenate(joined(2 * unit + unit // 2, 3 * unit), axis=0)
    put(0, 2, side)
    put(2, 0, side.T)


def spread(whole, target, live):
    half, order = whole.shape
    for rows, cols, value in (
        (slice(0, half), slice(0, order), whole[...]),
        (slice(half, order), slice(0, half), whole[:, half:].T),
    ):
        high, low = halves(value * live[:, cols])
        target[rows, cols] = high
        target[order + rows.start : order + rows.stop, cols] = low


def times(rows, matrix):
    count, order = rows.shape
    high = rows.astype(BF16)
    parts = stacked(rows)
    result = []
    for first in range(0, order, 256):
        cols = slice(first, min(first + 256, order))
        product = dot(parts, matrix[:order, cols])
        result.append((product[:count] + product[count:]) + dot(high, matrix[order:, cols]))
    return jnp.concatenate(result, axis=1)


def times_wide(left_side, right_side):
    width = right_side.shape[1] // 2
    high, low = halves(left_side)
    product = dot(high, right_side[...])
    return (product[:, :width] + product[:, width:]) + dot(low, right_side[:, :width])


def prepare_kernel(
    sizes, x_own, k_own, x_core, k_core, g_own, g_core, g_far, g_cross, index, far, cross,
    x, k, links, live_rows, live_cols, columns, first, whole, gathered,
):
    half, order = whole.shape
    rows = half // 2
    width = links.shape[1]
    group = width // 4
    part, near, core = place()
    for out, axis in ((live_rows, 0), (live_cols, 1)):
        ids = lax.broadcasted_iota(jnp.int32, out.shape, axis)
        ids = jnp.where(ids < half, ids + near * half, ids - near * half)
        out[...] = jnp.where(ids < sizes[0], 1.0, 0.0)
    for own, other, target in ((x_own, x_core, x), (k_own, k_core, k)):
        for side, col in enumerate((near * half, (1 - near) * half)):
            cols = slice(side * half, (side + 1) * half)
            whole[at(core * rows, rows), cols] = own[:, at(col, half, 128)]
            whole[at((1 - core) * rows, rows), cols] = other[:, at(col, half, 128)]
        spread(whole, target, live_cols)
    put_rows(g_own, g_core, gathered)
    put_rows(g_far, g_cross, gathered, half)
    hot = lax.broadcasted_iota(jnp.int32, (width, width), 0) == index[...]
    chosen = dot(gathered[...], hot.astype(F32).astype(BF16))
    links[...] = (chosen * live_rows[...]).astype(BF16)
    corner(far, cross, x, live_cols)
    value = links[:, at(part * group, group, 128)].astype(F32).T
    columns[...] = value
    high = value.astype(BF16)
    first[...] = dot(high, x[:order, :]) + dot(high, x[order:, :])


def global_kernel(
    live, far, cross, x, k_in, links, columns, first, base, s_own,
    keep, send, y_own, y_core, y_far, k, pack, solved,
):
    del k_in
    order, width = links.shape
    half = order // 2
    rows = half // 2
    group = width // 4
    part, near, core = place()
    block = lax.axis_index("tm")
    corner(far, cross, k, live)
    value = 2.0 * columns[...] - times(first[...], k)
    for step in range(TERMS - 1):
        value = columns[...] + value - times(times(value, x), k)
    result = times(value, x)
    left_side = stacked(result)
    solved[...] = result.T
    y_own[...] = solved[at(core * rows, rows), :]
    y_core[:rows, :] = solved[at((1 - core) * rows, rows), :]
    y_core[rows:, :] = s_own[...]
    y_far[:rows, :] = solved[at(half + core * rows, rows), :]
    y_far[rows : 2 * rows, :] = solved[at(half + (1 - core) * rows, rows), :]
    y_far[2 * rows :, :] = s_own[at(2 * near * group, 2 * group, 8), :]

    def square(shift):
        cols = at(((part + shift) % 4) * group, group, 128)
        parts = dot(left_side, links[:, cols])
        added = jnp.where(block == 0, base[:, cols], 0.0)
        return parts[:group] + parts[group:] + added

    pack[0:group, :] = square(0)
    pack[group : 2 * group, :] = square(1)
    across = square(2)
    pack[2 * group :, :] = jnp.where(
        part < 2, across[: group // 2, :], across.T[group // 2 :, :]
    )
    size = keep.shape[0]
    side = block % 2
    keep[...] = pack[at(side * size, size, 8), :]
    send[...] = pack[at((1 - side) * size, size, 8), :]


def pair_kernel(
    live, p_own, p_core, p_far, p_cross, x, k, links,
    own_terms, off_terms, next_terms, gathered,
):
    half = x.shape[1] // 2
    rows, width = p_far.shape
    link = width // 2
    share = link // 4
    put_rows(p_own, p_core, gathered)
    put_rows(p_far, p_cross, gathered, half)
    masked = gathered[...] * live[...].astype(BF16)
    source = lax.broadcasted_iota(jnp.int32, (width, 2 * share), 0)
    target = lax.broadcasted_iota(jnp.int32, (width, 2 * share), 1)
    wanted = place()[0] * share + target + jnp.where(target < share, 0, link - share)
    columns = dot(masked, (source == wanted).astype(F32).astype(BF16)).T
    value = columns
    for step in range(TERMS):
        value = columns + value - times(times(value, x), k)
    left_side = stacked(times(value, x))
    terms = dot(left_side, masked)
    terms = terms[: 2 * share] + terms[2 * share :]
    cross = dot(left_side, links[...])
    cross = cross[: 2 * share] + cross[2 * share :]
    next_terms[:, :link] = terms[:share, :link]
    next_terms[:, link:] = cross[:share]
    off_terms[...] = terms[:share, link:]
    own_terms[:, :link] = terms[share:, link:]
    own_terms[:, link:] = cross[share:]


def start_kernel(
    s_own, y_own, y_core, far, cross, own_terms, came,
    start, scaled, link_diag, link_cross, s_rows, y_rows,
):
    rows, group = y_own.shape
    width = s_rows.shape[1]
    half = width // 2
    part, near, core = place()
    top, bottom = at(near * half, half), at((1 - near) * half, half)
    left, right = at(near * half, half, 128), at((1 - near) * half, half, 128)
    low_left, low_right = (at(width + v * half, half, 128) for v in (near, 1 - near))

    def put(rows, cols, low_cols, value):
        start[rows, cols], start[rows, low_cols] = halves(value)

    for i in range(width // group):
        first, cols = i * group, slice(i * group, (i + 1) * group)
        put_rows(
            s_own.at[first : first + group, :],
            y_core.at[rows + first : rows + first + group, :],
            s_rows.at[:, cols],
        )
    put(top, left, low_left, s_rows[:, left])
    side = s_rows[:, right]
    put(top, right, low_right, side)
    put(bottom, left, low_left, side.T)
    for i in range(half // group):
        first = slice(2 * rows + i * group, 2 * rows + (i + 1) * group)
        put_rows(far.at[first, :], cross.at[first, :], s_rows.at[:, i * group : (i + 1) * group])
    put(bottom, right, low_right, s_rows[:, :half])
    for ref, mask in ((y_own, 0), (y_core, 1), (far, 2), (cross.at[rows:, :], 3)):
        y_rows[:, at((part ^ mask) * group, group, 128)] = ref[:rows, :]
    scaled[...] = times_wide(y_rows[...], start)
    link = link_diag.shape[1]
    there = lax.axis_index("tm") + 1 < lax.axis_size("tm")
    link_diag[...] = own_terms[:, :link] + jnp.where(there, came[:, :link], 0.0)
    link_cross[...] = own_terms[:, link:] + jnp.where(there, came[:, link:], 0.0)


def sum_kernel(mine, came, total):
    total[...] = mine[...] + came[...]


def back_kernel(*refs):
    sums, (start, scaled, schur, back, whole, parts) = refs[:8], refs[8:]
    part = place()[0]
    side = lax.axis_index("tm") % 2
    size = sums[0].shape[0]
    group, width = schur.shape
    span = 2 * size
    for mask in range(4):
        for half in range(2):
            rows = at((part ^ mask) * span + (side ^ half) * size, size, 8)
            whole[rows, :] = sums[2 * mask + half][...]

    def put(row, col, value):
        rows = slice(row * group, (row + 1) * group)
        high, low = halves(value)
        parts[rows, col * group : (col + 1) * group] = high
        parts[rows, width + col * group : width + (col + 1) * group] = low

    def across(row):
        first, other = row * span + 2 * group, (row + 2) * span + 2 * group
        return jnp.concatenate(
            [whole[at(first, group // 2, 8), :], whole[at(other, group // 2, 8), :]], axis=0
        )

    for row in range(4):
        first = row * span
        put(row, row, whole[first : first + group, :])
        value = whole[first + group : first + 2 * group, :]
        put(row, (row + 1) % 4, value)
        put((row + 1) % 4, row, value.T)
        if row < 2:
            value = across(row)
            put(row, row + 2, value)
            put(row + 2, row, value.T)
    before = (part + 3) % 4
    value = across(part % 2)
    for col, value in (
        (part, whole[at(part * span, group, 8), :]),
        ((part + 1) % 4, whole[at(part * span + group, group, 8), :]),
        ((part + 2) % 4, jnp.where(part < 2, value, value.T)),
        (before, whole[at(before * span + group, group, 8), :].T),
    ):
        schur[:, at(col * group, group, 128)] = value
    value = scaled[...]
    back[...] = 2.0 * value - times_wide(times_wide(value, parts), start)


def call(kernel, outs, scratch, *args, sizes=None, whole=False, alias={}, flops=0):
    vmem = pl.BlockSpec(memory_space=pltpu.VMEM)
    specs = [pl.BlockSpec(memory_space=pltpu.HBM) if whole else vmem] * len(args)
    if whole:
        args = [pltpu.with_memory_space_constraint(arg, pltpu.HBM) for arg in args]
    if sizes is not None:
        specs, args = [pl.BlockSpec(memory_space=pltpu.SMEM), *specs], (sizes, *args)
    return pl.pallas_call(
        kernel,
        out_shape=[jax.ShapeDtypeStruct(shape, dtype) for shape, dtype in outs],
        in_specs=specs,
        out_specs=[vmem] * len(outs),
        scratch_shapes=scratch,
        input_output_aliases=alias,
        compiler_params=pltpu.CompilerParams(vmem_limit_bytes=VMEM_BYTES),
        cost_estimate=pl.CostEstimate(flops=flops, bytes_accessed=0, transcendentals=0),
        name=kernel.__name__,
    )(*args)


def after(value, *others):
    return lax.optimization_barrier((value, *others))[0]


def shards(
    blocks, operator, initial, block_sizes, link_index, link_pair, link_global, schur_base,
    schur_start,
):
    operator, initial = operator[0], initial[0]
    pair, glob = link_pair[0], link_global[0]
    rows, order = operator.shape
    half = order // 2
    unit = half // 3
    link, width = pair.shape[1] // 2, glob.shape[1]
    group, share = width // 4, link // 4
    size = group + group // 4

    def tile_swap(value, mask):
        return lax.ppermute(value, "tile", [(i, i ^ mask) for i in range(4)])

    def block_swap(value, mask):
        return lax.ppermute(value, "tm", [(i, i ^ mask) for i in range(blocks)])

    def diagonal_swap(value):
        pairs = [
            (b * 4 + i, (b ^ 1) * 4 + (i ^ 2)) for b in range(blocks) for i in range(4)
        ]
        return lax.ppermute(value, ("tm", "tile"), pairs)

    vmem, matrix = pltpu.VMEM, ((2 * order, order), BF16)

    g_far = tile_swap(glob, 2)
    x_sent, k_sent, x_own, k_own, g_own, s_own, index = call(
        pack_kernel,
        [((3 * unit + SPARE, unit), F32), ((3 * unit + 2 * SPARE, unit), F32),
         ((rows, order), F32), ((rows, order), F32), ((rows, width), BF16),
         ((width, group), F32), (link_index.shape, jnp.int32)],
        [pltpu.SemaphoreType.DMA((8,))],
        initial, operator, glob, schur_start, link_index, whole=True,
    )
    x_far, k_far = tile_swap(x_sent, 2), tile_swap(k_sent, 2)
    g_far = after(g_far, x_sent)
    g_cross = tile_swap(g_far, 1)
    x_far, g_cross = lax.optimization_barrier((x_far, g_cross))
    x, k, links, live_rows, live_cols, columns, first = call(
        prepare_kernel,
        [matrix, matrix, ((order, width), BF16), ((order, 1), F32), ((1, order), F32),
         ((group, order), F32), ((group, order), F32)],
        [vmem((half, order), F32), vmem((order, width), BF16)],
        x_own, k_own, tile_swap(x_own, 1), tile_swap(k_own, 1), g_own, tile_swap(g_own, 1),
        g_far, g_cross, index,
        x_far, tile_swap(x_far, 1), sizes=block_sizes,
    )
    k_far = after(k_far, first)
    p_core, p_far = (tile_swap(after(pair, first), m) for m in (1, 2))
    keep, send, y_own, y_core, y_far, k = call(
        global_kernel,
        [((size, group), F32)] * 2 + [((rows, group), F32), ((rows + width, group), F32)]
        + [((2 * rows + 2 * group, group), F32), matrix],
        [vmem((2 * size, group), F32), vmem((order, group), F32)],
        live_cols, k_far, tile_swap(k_far, 1), x, k, links, columns, first, schur_base, s_own,
        alias={4: 5},
    )

    y_all = (y_own, tile_swap(y_core, 1), tile_swap(y_far, 2))
    p_far = after(p_far, keep)
    own_terms, off_terms, next_terms = call(
        pair_kernel,
        [((share, link + width), F32), ((share, link), F32), ((share, link + width), F32)],
        [vmem((order, 2 * link), BF16)],
        live_rows, pair, p_core, p_far, tile_swap(p_far, 1), x, k, links,
    )
    came = lax.ppermute(next_terms, "tm", [(i, (i - 1) % blocks) for i in range(blocks)])
    parts = [block_swap(send, 1)]
    if blocks > 2:
        parts += [block_swap(keep, 2), block_swap(send, 3)]
        *parts, off_terms = lax.optimization_barrier((*parts, off_terms))
        total = (keep + parts[1]) + (parts[0] + parts[2])
    else:
        total = keep + parts[0]
    step = 4
    while step < blocks:
        total = call(
            sum_kernel, [(total.shape, F32)], [], total, block_swap(total, step),
            flops=32 * rows * order * order,
        )[0]
        step *= 2
    start, scaled, link_diag, link_cross = call(
        start_kernel,
        [((width, 2 * width), BF16), ((rows, width), F32), ((share, link), F32),
         ((share, width), F32)],
        [vmem((2 * group, width), F32), vmem((rows, width), F32)],
        s_own, *y_all, tile_swap(y_all[2], 1), own_terms, came,
    )

    here = (total, after(block_swap(total, 1), scaled))
    there = (after(tile_swap(total, 2), scaled), after(diagonal_swap(total), scaled))
    sums = []
    for pieces in (here, there):
        sums += [*pieces, *(tile_swap(piece, 1) for piece in pieces)]
    global_schur, back_cols = call(
        back_kernel,
        [((group, width), F32), ((rows, width), F32)],
        [vmem((8 * size, group), F32), vmem((width, 2 * width), BF16)],
        *sums, start, scaled,
    )
    return (
        link_diag[None], off_terms[None], link_cross[None], global_schur, back_cols[None],
    )


def solution(mesh):
    return jax.shard_map(
        functools.partial(shards, mesh.shape["tm"]),
        mesh=mesh,
        in_specs=(
            P("tm", "tile", None),
            P("tm", "tile", None),
            P("tm"),
            P("tm", None),
            P("tm", "tile", None),
            P("tm", "tile", None),
            P("tile", None),
            P("tile", None),
        ),
        out_specs=(
            P("tm", "tile", None),
            P("tm", "tile", None),
            P("tm", "tile", None),
            P("tile", None),
            P("tm", "tile", None),
        ),
        check_vma=False,
    )
```

```python
import functools

import jax
import jax.numpy as jnp
from jax import lax
from jax.experimental import pallas as pl
from jax.experimental.pallas import tpu as pltpu
from jax.sharding import PartitionSpec as P

BF16 = jnp.bfloat16
F32 = jnp.float32
STEPS = 2
TERMS = 2**STEPS - 1
SPARE = 8
VMEM_BYTES = 32 * 2**20


def halves(value):
    high = value.astype(BF16)
    return high, (value - high.astype(F32)).astype(BF16)


def dot(left_side, right_side):
    return jnp.dot(left_side, right_side, preferred_element_type=F32)


def both(value):
    return jnp.concatenate(halves(value), axis=1)


def stacked(value):
    return jnp.concatenate(halves(value), axis=0)


def at(start, size, unit=16):
    return pl.ds(pl.multiple_of(start, unit), size)


def place():
    part = lax.axis_index("tile")
    return part, part // 2, part % 2


def put_rows(own, other, target, offset=0):
    rows = own.shape[0]
    core = place()[2]
    target[at(offset + core * rows, rows), :] = own[...]
    target[at(offset + (1 - core) * rows, rows), :] = other[...]


def started(*pairs, sems):
    copies = [
        pltpu.make_async_copy(source, target, sems.at[i])
        for i, (source, target) in enumerate(pairs)
    ]
    for copy in copies:
        copy.start()
    return copies


def pack_kernel(
    x_rows, k_rows, g_rows, s_rows, index,
    x_out, k_out, x_own, k_own, g_own, s_out, index_out, sems,
):
    rows, order = x_rows.shape
    half = order // 2
    unit = half // 3
    group = s_rows.shape[0]
    _, near, core = place()
    copies = started(
        (x_rows, x_own),
        (k_rows, k_own),
        (g_rows, g_own),
        (index, index_out),
        *[
            (s_rows.at[:, first : first + group], s_out.at[first : first + group, :])
            for first in range(0, s_out.shape[0], group)
        ],
        sems=sems,
    )
    edge = at(near * half + core * 2 * unit, unit, 128)
    middle = at(near * half + unit, unit, 128)
    opposite = at(near * half + (1 - core) * 2 * unit, unit, 128)
    large = at(core * (rows - unit), unit, 8)
    small = at((1 - core) * unit, rows - unit, 8)
    for copy, own, out in zip(copies, (x_own, k_own), (x_out, k_out)):
        copy.wait()
        out[0:unit, :] = own[large, edge]
        out[unit : 2 * unit, :] = own[large, middle]
        out[2 * unit : unit + rows, :] = own[small, middle]
        block = own[large, opposite]
        out[unit + rows : 3 * unit, :] = jnp.where(
            core == 0, block[: unit // 2, :], block.T[unit // 2 :, :]
        )
        out[3 * unit :, :] = jnp.zeros((out.shape[0] - 3 * unit, unit), F32)
    for copy in copies[2:]:
        copy.wait()


def corner(far, cross, target, live):
    order = target.shape[1]
    half = order // 2
    unit = half // 3
    core = place()[2]

    def joined(first, last):
        mine, theirs = far[first:last, :], cross[first:last, :]
        return jnp.where(core == 0, mine, theirs), jnp.where(core == 0, theirs, mine)

    def put(row, col, value):
        first = half + row * unit
        cols = slice(half + col * unit, half + (col + 1) * unit)
        high, low = halves(value * live[:, cols])
        target[first : first + unit, cols] = high
        target[order + first : order + first + unit, cols] = low

    zero, one = joined(0, unit)
    put(0, 0, zero)
    put(2, 2, one)
    zero, one = joined(unit, 2 * unit)
    put(0, 1, zero)
    put(1, 0, zero.T)
    put(2, 1, one)
    put(1, 2, one.T)
    put(1, 1, jnp.concatenate(joined(2 * unit, 2 * unit + unit // 2), axis=0))
    side = jnp.concatenate(joined(2 * unit + unit // 2, 3 * unit), axis=0)
    put(0, 2, side)
    put(2, 0, side.T)


def spread(whole, target, live):
    half, order = whole.shape
    for rows, cols, value in (
        (slice(0, half), slice(0, order), whole[...]),
        (slice(half, order), slice(0, half), whole[:, half:].T),
    ):
        high, low = halves(value * live[:, cols])
        target[rows, cols] = high
        target[order + rows.start : order + rows.stop, cols] = low


def times(rows, matrix):
    count, order = rows.shape
    high = rows.astype(BF16)
    parts = stacked(rows)
    result = []
    for first in range(0, order, 256):
        cols = slice(first, min(first + 256, order))
        product = dot(parts, matrix[:order, cols])
        result.append((product[:count] + product[count:]) + dot(high, matrix[order:, cols]))
    return jnp.concatenate(result, axis=1)


def times_wide(left_side, right_side):
    width = right_side.shape[1] // 2
    high, low = halves(left_side)
    product = dot(high, right_side[...])
    return (product[:, :width] + product[:, width:]) + dot(low, right_side[:, :width])


def prepare_kernel(
    sizes, x_own, k_own, x_core, k_core, g_own, g_core, g_far, g_cross, index, far, cross,
    x, k, links, live_rows, live_cols, columns, first, whole, gathered,
):
    half, order = whole.shape
    rows = half // 2
    width = links.shape[1]
    group = width // 4
    part, near, core = place()
    for out, axis in ((live_rows, 0), (live_cols, 1)):
        ids = lax.broadcasted_iota(jnp.int32, out.shape, axis)
        ids = jnp.where(ids < half, ids + near * half, ids - near * half)
        out[...] = jnp.where(ids < sizes[0], 1.0, 0.0)
    for own, other, target in ((x_own, x_core, x), (k_own, k_core, k)):
        for side, col in enumerate((near * half, (1 - near) * half)):
            cols = slice(side * half, (side + 1) * half)
            whole[at(core * rows, rows), cols] = own[:, at(col, half, 128)]
            whole[at((1 - core) * rows, rows), cols] = other[:, at(col, half, 128)]
        spread(whole, target, live_cols)
    put_rows(g_own, g_core, gathered)
    put_rows(g_far, g_cross, gathered, half)
    hot = lax.broadcasted_iota(jnp.int32, (width, width), 0) == index[...]
    chosen = dot(gathered[...], hot.astype(F32).astype(BF16))
    links[...] = (chosen * live_rows[...]).astype(BF16)
    corner(far, cross, x, live_cols)
    value = links[:, at(part * group, group, 128)].astype(F32).T
    columns[...] = value
    high = value.astype(BF16)
    first[...] = dot(high, x[:order, :]) + dot(high, x[order:, :])


def global_kernel(
    live, far, cross, x, k_in, links, columns, first, base, s_own,
    keep, send, y_own, y_core, y_far, k, pack, solved,
):
    del k_in
    order, width = links.shape
    half = order // 2
    rows = half // 2
    group = width // 4
    part, near, core = place()
    block = lax.axis_index("tm")
    corner(far, cross, k, live)
    value = 2.0 * columns[...] - times(first[...], k)
    for step in range(TERMS - 1):
        value = columns[...] + value - times(times(value, x), k)
    result = times(value, x)
    left_side = stacked(result)
    solved[...] = result.T
    y_own[...] = solved[at(core * rows, rows), :]
    y_core[:rows, :] = solved[at((1 - core) * rows, rows), :]
    y_core[rows:, :] = s_own[...]
    y_far[:rows, :] = solved[at(half + core * rows, rows), :]
    y_far[rows : 2 * rows, :] = solved[at(half + (1 - core) * rows, rows), :]
    y_far[2 * rows :, :] = s_own[at(2 * near * group, 2 * group, 8), :]

    def square(shift):
        cols = at(((part + shift) % 4) * group, group, 128)
        parts = dot(left_side, links[:, cols])
        added = jnp.where(block == 0, base[:, cols], 0.0)
        return parts[:group] + parts[group:] + added

    pack[0:group, :] = square(0)
    pack[group : 2 * group, :] = square(1)
    across = square(2)
    pack[2 * group :, :] = jnp.where(
        part < 2, across[: group // 2, :], across.T[group // 2 :, :]
    )
    size = keep.shape[0]
    side = block % 2
    keep[...] = pack[at(side * size, size, 8), :]
    send[...] = pack[at((1 - side) * size, size, 8), :]


def pair_kernel(
    live, p_own, p_core, p_far, p_cross, x, k, links,
    own_terms, off_terms, next_terms, gathered,
):
    half = x.shape[1] // 2
    rows, width = p_far.shape
    link = width // 2
    share = link // 4
    put_rows(p_own, p_core, gathered)
    put_rows(p_far, p_cross, gathered, half)
    masked = gathered[...] * live[...].astype(BF16)
    source = lax.broadcasted_iota(jnp.int32, (width, 2 * share), 0)
    target = lax.broadcasted_iota(jnp.int32, (width, 2 * share), 1)
    wanted = place()[0] * share + target + jnp.where(target < share, 0, link - share)
    columns = dot(masked, (source == wanted).astype(F32).astype(BF16)).T
    value = columns
    for step in range(TERMS):
        value = columns + value - times(times(value, x), k)
    left_side = stacked(times(value, x))
    terms = dot(left_side, masked)
    terms = terms[: 2 * share] + terms[2 * share :]
    cross = dot(left_side, links[...])
    cross = cross[: 2 * share] + cross[2 * share :]
    next_terms[:, :link] = terms[:share, :link]
    next_terms[:, link:] = cross[:share]
    off_terms[...] = terms[:share, link:]
    own_terms[:, :link] = terms[share:, link:]
    own_terms[:, link:] = cross[share:]


def start_kernel(s_own, y_own, y_core, far, cross, start, scaled, s_rows, y_rows):
    rows, group = y_own.shape
    width = s_rows.shape[1]
    half = width // 2
    part, near, core = place()
    top, bottom = at(near * half, half), at((1 - near) * half, half)
    left, right = at(near * half, half, 128), at((1 - near) * half, half, 128)
    low_left, low_right = (at(width + v * half, half, 128) for v in (near, 1 - near))

    def put(rows, cols, low_cols, value):
        start[rows, cols], start[rows, low_cols] = halves(value)

    for i in range(width // group):
        first, cols = i * group, slice(i * group, (i + 1) * group)
        put_rows(
            s_own.at[first : first + group, :],
            y_core.at[rows + first : rows + first + group, :],
            s_rows.at[:, cols],
        )
    put(top, left, low_left, s_rows[:, left])
    side = s_rows[:, right]
    put(top, right, low_right, side)
    put(bottom, left, low_left, side.T)
    for i in range(half // group):
        first = slice(2 * rows + i * group, 2 * rows + (i + 1) * group)
        put_rows(far.at[first, :], cross.at[first, :], s_rows.at[:, i * group : (i + 1) * group])
    put(bottom, right, low_right, s_rows[:, :half])
    for ref, mask in ((y_own, 0), (y_core, 1), (far, 2), (cross.at[rows:, :], 3)):
        y_rows[:, at((part ^ mask) * group, group, 128)] = ref[:rows, :]
    scaled[...] = times_wide(y_rows[...], start)


def back_kernel(*refs):
    sums, (start, scaled, schur, back, whole, parts) = refs[:8], refs[8:]
    part = place()[0]
    side = lax.axis_index("tm") % 2
    size = sums[0].shape[0]
    group, width = schur.shape
    span = 2 * size
    for mask in range(4):
        for half in range(2):
            rows = at((part ^ mask) * span + (side ^ half) * size, size, 8)
            whole[rows, :] = sums[2 * mask + half][...]

    def put(row, col, value):
        rows = slice(row * group, (row + 1) * group)
        high, low = halves(value)
        parts[rows, col * group : (col + 1) * group] = high
        parts[rows, width + col * group : width + (col + 1) * group] = low

    def across(row):
        first, other = row * span + 2 * group, (row + 2) * span + 2 * group
        return jnp.concatenate(
            [whole[at(first, group // 2, 8), :], whole[at(other, group // 2, 8), :]], axis=0
        )

    for row in range(4):
        first = row * span
        put(row, row, whole[first : first + group, :])
        value = whole[first + group : first + 2 * group, :]
        put(row, (row + 1) % 4, value)
        put((row + 1) % 4, row, value.T)
        if row < 2:
            value = across(row)
            put(row, row + 2, value)
            put(row + 2, row, value.T)
    before = (part + 3) % 4
    value = across(part % 2)
    for col, value in (
        (part, whole[at(part * span, group, 8), :]),
        ((part + 1) % 4, whole[at(part * span + group, group, 8), :]),
        ((part + 2) % 4, jnp.where(part < 2, value, value.T)),
        (before, whole[at(before * span + group, group, 8), :].T),
    ):
        schur[:, at(col * group, group, 128)] = value
    value = scaled[...]
    back[...] = 2.0 * value - times_wide(times_wide(value, parts), start)


def finish_kernel(own_terms, came, link_diag, link_cross):
    link = link_diag.shape[1]
    there = lax.axis_index("tm") + 1 < lax.axis_size("tm")
    link_diag[...] = own_terms[:, :link] + jnp.where(there, came[:, :link], 0.0)
    link_cross[...] = own_terms[:, link:] + jnp.where(there, came[:, link:], 0.0)


def call(kernel, outs, scratch, *args, sizes=None, whole=False, alias={}, flops=0):
    vmem = pl.BlockSpec(memory_space=pltpu.VMEM)
    specs = [pl.BlockSpec(memory_space=pltpu.HBM) if whole else vmem] * len(args)
    if whole:
        args = [pltpu.with_memory_space_constraint(arg, pltpu.HBM) for arg in args]
    if sizes is not None:
        specs, args = [pl.BlockSpec(memory_space=pltpu.SMEM), *specs], (sizes, *args)
    return pl.pallas_call(
        kernel,
        out_shape=[jax.ShapeDtypeStruct(shape, dtype) for shape, dtype in outs],
        in_specs=specs,
        out_specs=[vmem] * len(outs),
        scratch_shapes=scratch,
        input_output_aliases=alias,
        compiler_params=pltpu.CompilerParams(vmem_limit_bytes=VMEM_BYTES),
        cost_estimate=pl.CostEstimate(flops=flops, bytes_accessed=0, transcendentals=0),
        name=kernel.__name__,
    )(*args)


def after(value, *others):
    return lax.optimization_barrier((value, *others))[0]


def shards(
    blocks, operator, initial, block_sizes, link_index, link_pair, link_global, schur_base,
    schur_start,
):
    operator, initial = operator[0], initial[0]
    pair, glob = link_pair[0], link_global[0]
    rows, order = operator.shape
    half = order // 2
    unit = half // 3
    link, width = pair.shape[1] // 2, glob.shape[1]
    group, share = width // 4, link // 4
    size = group + group // 4

    def tile_swap(value, mask):
        return lax.ppermute(value, "tile", [(i, i ^ mask) for i in range(4)])

    def block_swap(value, mask):
        return lax.ppermute(value, "tm", [(i, i ^ mask) for i in range(blocks)])

    def diagonal_swap(value):
        pairs = [
            (b * 4 + i, (b ^ 1) * 4 + (i ^ 2)) for b in range(blocks) for i in range(4)
        ]
        return lax.ppermute(value, ("tm", "tile"), pairs)

    vmem, matrix = pltpu.VMEM, ((2 * order, order), BF16)

    g_far = tile_swap(glob, 2)
    x_sent, k_sent, x_own, k_own, g_own, s_own, index = call(
        pack_kernel,
        [((3 * unit + SPARE, unit), F32), ((3 * unit + 2 * SPARE, unit), F32),
         ((rows, order), F32), ((rows, order), F32), ((rows, width), BF16),
         ((width, group), F32), (link_index.shape, jnp.int32)],
        [pltpu.SemaphoreType.DMA((8,))],
        initial, operator, glob, schur_start, link_index, whole=True,
    )
    x_far, k_far = tile_swap(x_sent, 2), tile_swap(k_sent, 2)
    g_far = after(g_far, x_sent)
    g_cross = tile_swap(g_far, 1)
    x_far, g_cross = lax.optimization_barrier((x_far, g_cross))
    x, k, links, live_rows, live_cols, columns, first = call(
        prepare_kernel,
        [matrix, matrix, ((order, width), BF16), ((order, 1), F32), ((1, order), F32),
         ((group, order), F32), ((group, order), F32)],
        [vmem((half, order), F32), vmem((order, width), BF16)],
        x_own, k_own, tile_swap(x_own, 1), tile_swap(k_own, 1), g_own, tile_swap(g_own, 1),
        g_far, g_cross, index,
        x_far, tile_swap(x_far, 1), sizes=block_sizes,
    )
    k_far = after(k_far, first)
    p_core, p_far = (tile_swap(after(pair, first), m) for m in (1, 2))
    keep, send, y_own, y_core, y_far, k = call(
        global_kernel,
        [((size, group), F32)] * 2 + [((rows, group), F32), ((rows + width, group), F32)]
        + [((2 * rows + 2 * group, group), F32), matrix],
        [vmem((2 * size, group), F32), vmem((order, group), F32)],
        live_cols, k_far, tile_swap(k_far, 1), x, k, links, columns, first, schur_base, s_own,
        alias={4: 5},
    )

    y_all = (y_own, tile_swap(y_core, 1), tile_swap(y_far, 2))
    if blocks > 2:
        parts = [block_swap(send, 1), block_swap(keep, 2), block_swap(send, 3)]
        total = (keep + parts[1]) + (parts[0] + parts[2])
    else:
        total = keep + block_swap(send, 1)
    p_far = after(p_far, keep)
    own_terms, off_terms, next_terms = call(
        pair_kernel,
        [((share, link + width), F32), ((share, link), F32), ((share, link + width), F32)],
        [vmem((order, 2 * link), BF16)],
        live_rows, pair, p_core, p_far, tile_swap(p_far, 1), x, k, after(links, total),
    )
    step = 4
    while step < blocks:
        other = block_swap(total, step)
        if step == 4:
            other, off_terms, *y_all = lax.optimization_barrier((other, off_terms, *y_all))
        total = total + other
        step *= 2
    cross = tile_swap(after(y_all[2], total), 1)
    start, scaled = call(
        start_kernel,
        [((width, 2 * width), BF16), ((rows, width), F32)],
        [vmem((2 * group, width), F32), vmem((rows, width), F32)],
        s_own, *y_all, cross,
    )

    here = (total, after(block_swap(total, 1), scaled))
    there = (after(tile_swap(total, 2), scaled), after(diagonal_swap(total), scaled))
    sums = []
    for pieces in (here, there):
        sums += [*pieces, *(tile_swap(piece, 1) for piece in pieces)]
    global_schur, back_cols = call(
        back_kernel,
        [((group, width), F32), ((rows, width), F32)],
        [vmem((8 * size, group), F32), vmem((width, 2 * width), BF16)],
        *sums, start, scaled,
        flops=int(4 * rows * order * order),
    )
    next_terms = after(next_terms, cross)
    came = lax.ppermute(next_terms, "tm", [(i, (i - 1) % blocks) for i in range(blocks)])
    link_diag, link_cross = call(
        finish_kernel,
        [((share, link), F32), ((share, width), F32)],
        [],
        own_terms, came,
    )
    return (
        link_diag[None], off_terms[None], link_cross[None], global_schur, back_cols[None],
    )


def solution(mesh):
    return jax.shard_map(
        functools.partial(shards, mesh.shape["tm"]),
        mesh=mesh,
        in_specs=(
            P("tm", "tile", None),
            P("tm", "tile", None),
            P("tm"),
            P("tm", None),
            P("tm", "tile", None),
            P("tm", "tile", None),
            P("tile", None),
            P("tile", None),
        ),
        out_specs=(
            P("tm", "tile", None),
            P("tm", "tile", None),
            P("tm", "tile", None),
            P("tile", None),
            P("tm", "tile", None),
        ),
        check_vma=False,
    )
```

```python
import functools

import jax
import jax.numpy as jnp
from jax import lax
from jax.experimental import pallas as pl
from jax.experimental.pallas import tpu as pltpu
from jax.sharding import PartitionSpec as P

BF16 = jnp.bfloat16
F32 = jnp.float32
STEPS = 2
TERMS = 2**STEPS - 1
SPARE = 8
VMEM_BYTES = 32 * 2**20


def halves(value):
    high = value.astype(BF16)
    return high, (value - high.astype(F32)).astype(BF16)


def dot(left_side, right_side):
    return jnp.dot(left_side, right_side, preferred_element_type=F32)


def both(value):
    return jnp.concatenate(halves(value), axis=1)


def stacked(value):
    return jnp.concatenate(halves(value), axis=0)


def at(start, size, unit=16):
    return pl.ds(pl.multiple_of(start, unit), size)


def place():
    part = lax.axis_index("tile")
    return part, part // 2, part % 2


def put_rows(own, other, target, offset=0):
    rows = own.shape[0]
    core = place()[2]
    target[at(offset + core * rows, rows), :] = own[...]
    target[at(offset + (1 - core) * rows, rows), :] = other[...]


def started(*pairs, sems):
    copies = [
        pltpu.make_async_copy(source, target, sems.at[i])
        for i, (source, target) in enumerate(pairs)
    ]
    for copy in copies:
        copy.start()
    return copies


def pack_kernel(
    x_rows, k_rows, g_rows, s_rows, index,
    x_out, k_out, x_own, k_own, g_own, s_out, index_out, sems,
):
    rows, order = x_rows.shape
    half = order // 2
    unit = half // 3
    group = s_rows.shape[0]
    _, near, core = place()
    copies = started(
        (x_rows, x_own),
        (k_rows, k_own),
        (g_rows, g_own),
        (index, index_out),
        *[
            (s_rows.at[:, first : first + group], s_out.at[first : first + group, :])
            for first in range(0, s_out.shape[0], group)
        ],
        sems=sems,
    )
    edge = at(near * half + core * 2 * unit, unit, 128)
    middle = at(near * half + unit, unit, 128)
    opposite = at(near * half + (1 - core) * 2 * unit, unit, 128)
    large = at(core * (rows - unit), unit, 8)
    small = at((1 - core) * unit, rows - unit, 8)
    for copy, own, out in zip(copies, (x_own, k_own), (x_out, k_out)):
        copy.wait()
        out[0:unit, :] = own[large, edge]
        out[unit : 2 * unit, :] = own[large, middle]
        out[2 * unit : unit + rows, :] = own[small, middle]
        block = own[large, opposite]
        out[unit + rows : 3 * unit, :] = jnp.where(
            core == 0, block[: unit // 2, :], block.T[unit // 2 :, :]
        )
        out[3 * unit :, :] = jnp.zeros((out.shape[0] - 3 * unit, unit), F32)
    for copy in copies[2:]:
        copy.wait()


def corner(far, cross, target, live):
    order = target.shape[1]
    half = order // 2
    unit = half // 3
    core = place()[2]

    def joined(first, last):
        mine, theirs = far[first:last, :], cross[first:last, :]
        return jnp.where(core == 0, mine, theirs), jnp.where(core == 0, theirs, mine)

    def put(row, col, value):
        first = half + row * unit
        cols = slice(half + col * unit, half + (col + 1) * unit)
        high, low = halves(value * live[:, cols])
        target[first : first + unit, cols] = high
        target[order + first : order + first + unit, cols] = low

    zero, one = joined(0, unit)
    put(0, 0, zero)
    put(2, 2, one)
    zero, one = joined(unit, 2 * unit)
    put(0, 1, zero)
    put(1, 0, zero.T)
    put(2, 1, one)
    put(1, 2, one.T)
    put(1, 1, jnp.concatenate(joined(2 * unit, 2 * unit + unit // 2), axis=0))
    side = jnp.concatenate(joined(2 * unit + unit // 2, 3 * unit), axis=0)
    put(0, 2, side)
    put(2, 0, side.T)


def spread(whole, target, live):
    half, order = whole.shape
    for rows, cols, value in (
        (slice(0, half), slice(0, order), whole[...]),
        (slice(half, order), slice(0, half), whole[:, half:].T),
    ):
        high, low = halves(value * live[:, cols])
        target[rows, cols] = high
        target[order + rows.start : order + rows.stop, cols] = low


def times(rows, matrix):
    count, order = rows.shape
    high = rows.astype(BF16)
    parts = stacked(rows)
    result = []
    for first in range(0, order, 256):
        cols = slice(first, min(first + 256, order))
        product = dot(parts, matrix[:order, cols])
        result.append((product[:count] + product[count:]) + dot(high, matrix[order:, cols]))
    return jnp.concatenate(result, axis=1)


def times_wide(left_side, right_side):
    width = right_side.shape[1] // 2
    high, low = halves(left_side)
    product = dot(high, right_side[...])
    return (product[:, :width] + product[:, width:]) + dot(low, right_side[:, :width])


def prepare_kernel(
    sizes, x_own, k_own, x_core, k_core, g_own, g_core, g_far, g_cross, index, far, cross,
    x, k, links, live_rows, live_cols, columns, first, whole, gathered,
):
    half, order = whole.shape
    rows = half // 2
    width = links.shape[1]
    group = width // 4
    part, near, core = place()
    for out, axis in ((live_rows, 0), (live_cols, 1)):
        ids = lax.broadcasted_iota(jnp.int32, out.shape, axis)
        ids = jnp.where(ids < half, ids + near * half, ids - near * half)
        out[...] = jnp.where(ids < sizes[0], 1.0, 0.0)
    for own, other, target in ((x_own, x_core, x), (k_own, k_core, k)):
        for side, col in enumerate((near * half, (1 - near) * half)):
            cols = slice(side * half, (side + 1) * half)
            whole[at(core * rows, rows), cols] = own[:, at(col, half, 128)]
            whole[at((1 - core) * rows, rows), cols] = other[:, at(col, half, 128)]
        spread(whole, target, live_cols)
    put_rows(g_own, g_core, gathered)
    put_rows(g_far, g_cross, gathered, half)
    hot = lax.broadcasted_iota(jnp.int32, (width, width), 0) == index[...]
    chosen = dot(gathered[...], hot.astype(F32).astype(BF16))
    links[...] = (chosen * live_rows[...]).astype(BF16)
    corner(far, cross, x, live_cols)
    value = links[:, at(part * group, group, 128)].astype(F32).T
    columns[...] = value
    high = value.astype(BF16)
    first[...] = dot(high, x[:order, :]) + dot(high, x[order:, :])


def global_kernel(
    live, far, cross, x, k_in, links, columns, first, base, s_own,
    keep, send, y_own, y_core, y_far, k, pack, solved,
):
    del k_in
    order, width = links.shape
    half = order // 2
    rows = half // 2
    group = width // 4
    part, near, core = place()
    block = lax.axis_index("tm")
    corner(far, cross, k, live)
    value = 2.0 * columns[...] - times(first[...], k)
    for step in range(TERMS - 1):
        value = columns[...] + value - times(times(value, x), k)
    result = times(value, x)
    left_side = stacked(result)
    solved[...] = result.T
    y_own[...] = solved[at(core * rows, rows), :]
    y_core[:rows, :] = solved[at((1 - core) * rows, rows), :]
    y_core[rows:, :] = s_own[...]
    y_far[:rows, :] = solved[at(half + core * rows, rows), :]
    y_far[rows : 2 * rows, :] = solved[at(half + (1 - core) * rows, rows), :]
    y_far[2 * rows :, :] = s_own[at(2 * near * group, 2 * group, 8), :]

    def square(shift):
        cols = at(((part + shift) % 4) * group, group, 128)
        parts = dot(left_side, links[:, cols])
        added = jnp.where(block == 0, base[:, cols], 0.0)
        return parts[:group] + parts[group:] + added

    pack[0:group, :] = square(0)
    pack[group : 2 * group, :] = square(1)
    across = square(2)
    pack[2 * group :, :] = jnp.where(
        part < 2, across[: group // 2, :], across.T[group // 2 :, :]
    )
    size = keep.shape[0]
    side = block % 2
    keep[...] = pack[at(side * size, size, 8), :]
    send[...] = pack[at((1 - side) * size, size, 8), :]


def pair_kernel(
    live, p_own, p_core, p_far, p_cross, x, k, links,
    own_terms, off_terms, next_terms, gathered,
):
    half = x.shape[1] // 2
    rows, width = p_far.shape
    link = width // 2
    share = link // 4
    put_rows(p_own, p_core, gathered)
    put_rows(p_far, p_cross, gathered, half)
    masked = gathered[...] * live[...].astype(BF16)
    source = lax.broadcasted_iota(jnp.int32, (width, 2 * share), 0)
    target = lax.broadcasted_iota(jnp.int32, (width, 2 * share), 1)
    wanted = place()[0] * share + target + jnp.where(target < share, 0, link - share)
    columns = dot(masked, (source == wanted).astype(F32).astype(BF16)).T
    value = columns
    for step in range(TERMS):
        value = columns + value - times(times(value, x), k)
    left_side = stacked(times(value, x))
    terms = dot(left_side, masked)
    terms = terms[: 2 * share] + terms[2 * share :]
    cross = dot(left_side, links[...])
    cross = cross[: 2 * share] + cross[2 * share :]
    next_terms[:, :link] = terms[:share, :link]
    next_terms[:, link:] = cross[:share]
    off_terms[...] = terms[:share, link:]
    own_terms[:, :link] = terms[share:, link:]
    own_terms[:, link:] = cross[share:]


def start_kernel(s_own, y_own, y_core, far, cross, start, scaled, s_rows, y_rows):
    rows, group = y_own.shape
    width = s_rows.shape[1]
    half = width // 2
    part, near, core = place()
    top, bottom = at(near * half, half), at((1 - near) * half, half)
    left, right = at(near * half, half, 128), at((1 - near) * half, half, 128)
    low_left, low_right = (at(width + v * half, half, 128) for v in (near, 1 - near))

    def put(rows, cols, low_cols, value):
        start[rows, cols], start[rows, low_cols] = halves(value)

    for i in range(width // group):
        first, cols = i * group, slice(i * group, (i + 1) * group)
        put_rows(
            s_own.at[first : first + group, :],
            y_core.at[rows + first : rows + first + group, :],
            s_rows.at[:, cols],
        )
    put(top, left, low_left, s_rows[:, left])
    side = s_rows[:, right]
    put(top, right, low_right, side)
    put(bottom, left, low_left, side.T)
    for i in range(half // group):
        first = slice(2 * rows + i * group, 2 * rows + (i + 1) * group)
        put_rows(far.at[first, :], cross.at[first, :], s_rows.at[:, i * group : (i + 1) * group])
    put(bottom, right, low_right, s_rows[:, :half])
    for ref, mask in ((y_own, 0), (y_core, 1), (far, 2), (cross.at[rows:, :], 3)):
        y_rows[:, at((part ^ mask) * group, group, 128)] = ref[:rows, :]
    scaled[...] = times_wide(y_rows[...], start)


def back_kernel(*refs):
    sums, (start, scaled, schur, back, whole, parts) = refs[:8], refs[8:]
    part = place()[0]
    side = lax.axis_index("tm") % 2
    size = sums[0].shape[0]
    group, width = schur.shape
    span = 2 * size
    for mask in range(4):
        for half in range(2):
            rows = at((part ^ mask) * span + (side ^ half) * size, size, 8)
            whole[rows, :] = sums[2 * mask + half][...]

    def put(row, col, value):
        rows = slice(row * group, (row + 1) * group)
        high, low = halves(value)
        parts[rows, col * group : (col + 1) * group] = high
        parts[rows, width + col * group : width + (col + 1) * group] = low

    def across(row):
        first, other = row * span + 2 * group, (row + 2) * span + 2 * group
        return jnp.concatenate(
            [whole[at(first, group // 2, 8), :], whole[at(other, group // 2, 8), :]], axis=0
        )

    for row in range(4):
        first = row * span
        put(row, row, whole[first : first + group, :])
        value = whole[first + group : first + 2 * group, :]
        put(row, (row + 1) % 4, value)
        put((row + 1) % 4, row, value.T)
        if row < 2:
            value = across(row)
            put(row, row + 2, value)
            put(row + 2, row, value.T)
    before = (part + 3) % 4
    value = across(part % 2)
    for col, value in (
        (part, whole[at(part * span, group, 8), :]),
        ((part + 1) % 4, whole[at(part * span + group, group, 8), :]),
        ((part + 2) % 4, jnp.where(part < 2, value, value.T)),
        (before, whole[at(before * span + group, group, 8), :].T),
    ):
        schur[:, at(col * group, group, 128)] = value
    value = scaled[...]
    back[...] = 2.0 * value - times_wide(times_wide(value, parts), start)


def finish_kernel(own_terms, came, link_diag, link_cross):
    link = link_diag.shape[1]
    there = lax.axis_index("tm") + 1 < lax.axis_size("tm")
    link_diag[...] = own_terms[:, :link] + jnp.where(there, came[:, :link], 0.0)
    link_cross[...] = own_terms[:, link:] + jnp.where(there, came[:, link:], 0.0)


def call(kernel, outs, scratch, *args, sizes=None, whole=False, alias={}, flops=0):
    vmem = pl.BlockSpec(memory_space=pltpu.VMEM)
    specs = [pl.BlockSpec(memory_space=pltpu.HBM) if whole else vmem] * len(args)
    if whole:
        args = [pltpu.with_memory_space_constraint(arg, pltpu.HBM) for arg in args]
    if sizes is not None:
        specs, args = [pl.BlockSpec(memory_space=pltpu.SMEM), *specs], (sizes, *args)
    return pl.pallas_call(
        kernel,
        out_shape=[jax.ShapeDtypeStruct(shape, dtype) for shape, dtype in outs],
        in_specs=specs,
        out_specs=[vmem] * len(outs),
        scratch_shapes=scratch,
        input_output_aliases=alias,
        compiler_params=pltpu.CompilerParams(vmem_limit_bytes=VMEM_BYTES),
        cost_estimate=pl.CostEstimate(flops=flops, bytes_accessed=0, transcendentals=0),
        name=kernel.__name__,
    )(*args)


def after(value, *others):
    return lax.optimization_barrier((value, *others))[0]


def shards(
    blocks, operator, initial, block_sizes, link_index, link_pair, link_global, schur_base,
    schur_start,
):
    operator, initial = operator[0], initial[0]
    pair, glob = link_pair[0], link_global[0]
    rows, order = operator.shape
    half = order // 2
    unit = half // 3
    link, width = pair.shape[1] // 2, glob.shape[1]
    group, share = width // 4, link // 4
    size = group + group // 4

    def tile_swap(value, mask):
        return lax.ppermute(value, "tile", [(i, i ^ mask) for i in range(4)])

    def block_swap(value, mask):
        return lax.ppermute(value, "tm", [(i, i ^ mask) for i in range(blocks)])

    def diagonal_swap(value):
        pairs = [
            (b * 4 + i, (b ^ 1) * 4 + (i ^ 2)) for b in range(blocks) for i in range(4)
        ]
        return lax.ppermute(value, ("tm", "tile"), pairs)

    vmem, matrix = pltpu.VMEM, ((2 * order, order), BF16)

    g_far = tile_swap(glob, 2)
    x_sent, k_sent, x_own, k_own, g_own, s_own, index = call(
        pack_kernel,
        [((3 * unit + SPARE, unit), F32), ((3 * unit + 2 * SPARE, unit), F32),
         ((rows, order), F32), ((rows, order), F32), ((rows, width), BF16),
         ((width, group), F32), (link_index.shape, jnp.int32)],
        [pltpu.SemaphoreType.DMA((8,))],
        initial, operator, glob, schur_start, link_index, whole=True,
    )
    x_far, k_far = tile_swap(x_sent, 2), tile_swap(k_sent, 2)
    g_far = after(g_far, x_sent)
    g_cross = tile_swap(g_far, 1)
    x_far, g_cross = lax.optimization_barrier((x_far, g_cross))
    x, k, links, live_rows, live_cols, columns, first = call(
        prepare_kernel,
        [matrix, matrix, ((order, width), BF16), ((order, 1), F32), ((1, order), F32),
         ((group, order), F32), ((group, order), F32)],
        [vmem((half, order), F32), vmem((order, width), BF16)],
        x_own, k_own, tile_swap(x_own, 1), tile_swap(k_own, 1), g_own, tile_swap(g_own, 1),
        g_far, g_cross, index,
        x_far, tile_swap(x_far, 1), sizes=block_sizes,
    )
    k_far = after(k_far, first)
    p_core, p_far = (tile_swap(after(pair, first), m) for m in (1, 2))
    keep, send, y_own, y_core, y_far, k = call(
        global_kernel,
        [((size, group), F32)] * 2 + [((rows, group), F32), ((rows + width, group), F32)]
        + [((2 * rows + 2 * group, group), F32), matrix],
        [vmem((2 * size, group), F32), vmem((order, group), F32)],
        live_cols, k_far, tile_swap(k_far, 1), x, k, links, columns, first, schur_base, s_own,
        alias={4: 5},
    )

    y_all = (y_own, tile_swap(y_core, 1), tile_swap(y_far, 2))
    if blocks > 2:
        parts = [block_swap(send, 1), block_swap(keep, 2), block_swap(send, 3)]
        total = (keep + parts[1]) + (parts[0] + parts[2])
    else:
        total = keep + block_swap(send, 1)
    p_far = after(p_far, keep)
    own_terms, off_terms, next_terms = call(
        pair_kernel,
        [((share, link + width), F32), ((share, link), F32), ((share, link + width), F32)],
        [vmem((order, 2 * link), BF16)],
        live_rows, pair, p_core, p_far, tile_swap(p_far, 1), x, k, after(links, total),
    )
    step = 4
    while step < blocks:
        other = block_swap(total, step)
        if step == 4:
            other, off_terms, *y_all = lax.optimization_barrier((other, off_terms, *y_all))
        total = total + other
        step *= 2
    cross = tile_swap(after(y_all[2], total), 1)
    start, scaled = call(
        start_kernel,
        [((width, 2 * width), BF16), ((rows, width), F32)],
        [vmem((2 * group, width), F32), vmem((rows, width), F32)],
        s_own, *y_all, cross,
    )

    near = after(block_swap(total, 1), scaled)
    here = (total, near)
    there = (after(tile_swap(total, 2), near), after(diagonal_swap(total), near))
    sums = []
    for pieces in (here, there):
        sums += [*pieces, *(tile_swap(piece, 1) for piece in pieces)]
    global_schur, back_cols = call(
        back_kernel,
        [((group, width), F32), ((rows, width), F32)],
        [vmem((8 * size, group), F32), vmem((width, 2 * width), BF16)],
        *sums, start, scaled,
        flops=int(4 * rows * order * order),
    )
    next_terms = after(next_terms, cross)
    came = lax.ppermute(next_terms, "tm", [(i, (i - 1) % blocks) for i in range(blocks)])
    link_diag, link_cross = call(
        finish_kernel,
        [((share, link), F32), ((share, width), F32)],
        [],
        own_terms, came,
    )
    return (
        link_diag[None], off_terms[None], link_cross[None], global_schur, back_cols[None],
    )


def solution(mesh):
    return jax.shard_map(
        functools.partial(shards, mesh.shape["tm"]),
        mesh=mesh,
        in_specs=(
            P("tm", "tile", None),
            P("tm", "tile", None),
            P("tm"),
            P("tm", None),
            P("tm", "tile", None),
            P("tm", "tile", None),
            P("tile", None),
            P("tile", None),
        ),
        out_specs=(
            P("tm", "tile", None),
            P("tm", "tile", None),
            P("tm", "tile", None),
            P("tile", None),
            P("tm", "tile", None),
        ),
        check_vma=False,
    )
```

```python
import functools

import jax
import jax.numpy as jnp
from jax import lax
from jax.experimental import pallas as pl
from jax.experimental.pallas import tpu as pltpu
from jax.sharding import PartitionSpec as P

BF16 = jnp.bfloat16
F32 = jnp.float32
STEPS = 2
TERMS = 2**STEPS - 1
SPARE = 8
VMEM_BYTES = 32 * 2**20


def halves(value):
    high = value.astype(BF16)
    return high, (value - high.astype(F32)).astype(BF16)


def dot(left_side, right_side):
    return jnp.dot(left_side, right_side, preferred_element_type=F32)


def both(value):
    return jnp.concatenate(halves(value), axis=1)


def stacked(value):
    return jnp.concatenate(halves(value), axis=0)


def at(start, size, unit=16):
    return pl.ds(pl.multiple_of(start, unit), size)


def place():
    part = lax.axis_index("tile")
    return part, part // 2, part % 2


def folded(square):
    half = square.shape[0] // 2
    last = square[half:, half:]
    last = jnp.concatenate([last[: half // 2, :], last[half // 2 :, :]], axis=1)
    return jnp.concatenate([square[:half, :], last], axis=0)


def unfolded(rows):
    half = rows.shape[1] // 2
    upper, last = rows[:half, :], rows[half:, :]
    last = jnp.concatenate([last[:, :half], last[:, half:]], axis=0)
    return jnp.concatenate(
        [upper, jnp.concatenate([upper[:, half:].T, last], axis=1)], axis=0
    )


def put_rows(own, other, target, offset=0):
    rows = own.shape[0]
    core = place()[2]
    target[at(offset + core * rows, rows), :] = own[...]
    target[at(offset + (1 - core) * rows, rows), :] = other[...]


def started(*pairs, sems):
    copies = [
        pltpu.make_async_copy(source, target, sems.at[i])
        for i, (source, target) in enumerate(pairs)
    ]
    for copy in copies:
        copy.start()
    return copies


def pack_kernel(
    x_rows, k_rows, g_rows, s_rows, index,
    x_out, k_out, x_own, k_own, g_own, s_out, index_out, sems,
):
    rows, order = x_rows.shape
    half = order // 2
    unit = half // 3
    group = s_rows.shape[0]
    _, near, core = place()
    copies = started(
        (x_rows, x_own),
        (k_rows, k_own),
        (g_rows, g_own),
        (index, index_out),
        *[
            (s_rows.at[:, first : first + group], s_out.at[first : first + group, :])
            for first in range(0, s_out.shape[0], group)
        ],
        sems=sems,
    )
    edge = at(near * half + core * 2 * unit, unit, 128)
    middle = at(near * half + unit, unit, 128)
    opposite = at(near * half + (1 - core) * 2 * unit, unit, 128)
    large = at(core * (rows - unit), unit, 8)
    small = at((1 - core) * unit, rows - unit, 8)
    for copy, own, out in zip(copies, (x_own, k_own), (x_out, k_out)):
        copy.wait()
        out[0:unit, :] = own[large, edge]
        out[unit : 2 * unit, :] = own[large, middle]
        out[2 * unit : unit + rows, :] = own[small, middle]
        block = own[large, opposite]
        out[unit + rows : 3 * unit, :] = jnp.where(
            core == 0, block[: unit // 2, :], block.T[unit // 2 :, :]
        )
        out[3 * unit :, :] = jnp.zeros((out.shape[0] - 3 * unit, unit), F32)
    for copy in copies[2:]:
        copy.wait()


def corner(far, cross, target, live):
    order = target.shape[1]
    half = order // 2
    unit = half // 3
    core = place()[2]

    def joined(first, last):
        mine, theirs = far[first:last, :], cross[first:last, :]
        return jnp.where(core == 0, mine, theirs), jnp.where(core == 0, theirs, mine)

    def put(row, col, value):
        first = half + row * unit
        cols = slice(half + col * unit, half + (col + 1) * unit)
        high, low = halves(value * live[:, cols])
        target[first : first + unit, cols] = high
        target[order + first : order + first + unit, cols] = low

    zero, one = joined(0, unit)
    put(0, 0, zero)
    put(2, 2, one)
    zero, one = joined(unit, 2 * unit)
    put(0, 1, zero)
    put(1, 0, zero.T)
    put(2, 1, one)
    put(1, 2, one.T)
    put(1, 1, jnp.concatenate(joined(2 * unit, 2 * unit + unit // 2), axis=0))
    side = jnp.concatenate(joined(2 * unit + unit // 2, 3 * unit), axis=0)
    put(0, 2, side)
    put(2, 0, side.T)


def spread(whole, target, live):
    half, order = whole.shape
    for rows, cols, value in (
        (slice(0, half), slice(0, order), whole[...]),
        (slice(half, order), slice(0, half), whole[:, half:].T),
    ):
        high, low = halves(value * live[:, cols])
        target[rows, cols] = high
        target[order + rows.start : order + rows.stop, cols] = low


def times(rows, matrix):
    count, order = rows.shape
    high = rows.astype(BF16)
    parts = stacked(rows)
    result = []
    for first in range(0, order, 256):
        cols = slice(first, min(first + 256, order))
        product = dot(parts, matrix[:order, cols])
        result.append((product[:count] + product[count:]) + dot(high, matrix[order:, cols]))
    return jnp.concatenate(result, axis=1)


def times_wide(left_side, right_side):
    width = right_side.shape[1] // 2
    high, low = halves(left_side)
    product = dot(high, right_side[...])
    return (product[:, :width] + product[:, width:]) + dot(low, right_side[:, :width])


def prepare_kernel(
    sizes, x_own, k_own, x_core, k_core, g_own, g_core, g_far, g_cross, index, far, cross,
    x, k, links, live_rows, live_cols, columns, first, whole, gathered,
):
    half, order = whole.shape
    rows = half // 2
    width = links.shape[1]
    group = width // 4
    part, near, core = place()
    for out, axis in ((live_rows, 0), (live_cols, 1)):
        ids = lax.broadcasted_iota(jnp.int32, out.shape, axis)
        ids = jnp.where(ids < half, ids + near * half, ids - near * half)
        out[...] = jnp.where(ids < sizes[0], 1.0, 0.0)
    for own, other, target in ((x_own, x_core, x), (k_own, k_core, k)):
        for side, col in enumerate((near * half, (1 - near) * half)):
            cols = slice(side * half, (side + 1) * half)
            whole[at(core * rows, rows), cols] = own[:, at(col, half, 128)]
            whole[at((1 - core) * rows, rows), cols] = other[:, at(col, half, 128)]
        spread(whole, target, live_cols)
    put_rows(g_own, g_core, gathered)
    put_rows(g_far, g_cross, gathered, half)
    hot = lax.broadcasted_iota(jnp.int32, (width, width), 0) == index[...]
    chosen = dot(gathered[...], hot.astype(F32).astype(BF16))
    links[...] = (chosen * live_rows[...]).astype(BF16)
    corner(far, cross, x, live_cols)
    value = links[:, at(part * group, group, 128)].astype(F32).T
    columns[...] = value
    high = value.astype(BF16)
    first[...] = dot(high, x[:order, :]) + dot(high, x[order:, :])


def global_kernel(
    live, far, cross, x, k_in, links, columns, product, base, s_own,
    keep, send, y_own, y_core, y_far, k, pack, solved,
):
    del k_in
    order, width = links.shape
    half = order // 2
    rows = half // 2
    group = width // 4
    part, near, core = place()
    block = lax.axis_index("tm")
    corner(far, cross, k, live)
    value = 2.0 * columns[...] - times(product[...], k)
    for step in range(TERMS - 1):
        value = columns[...] + value - times(times(value, x), k)
    result = times(value, x)
    left_side = stacked(result)
    solved[...] = result.T
    y_own[...] = solved[at(core * rows, rows), :]
    y_core[:rows, :] = solved[at((1 - core) * rows, rows), :]
    y_core[rows:, :] = s_own[...]
    y_far[:rows, :] = solved[at(half + core * rows, rows), :]
    y_far[rows : 2 * rows, :] = solved[at(half + (1 - core) * rows, rows), :]
    y_far[2 * rows :, :] = s_own[at(2 * near * group, 2 * group, 8), :]

    def square(shift):
        cols = at(((part + shift) % 4) * group, group, 128)
        parts = dot(left_side, links[:, cols])
        added = jnp.where(block == 0, base[:, cols], 0.0)
        return parts[:group] + parts[group:] + added

    first = group * 3 // 4
    pack[0:first, :] = folded(square(0))
    pack[first : first + group, :] = square(1)
    across = square(2)
    pack[first + group :, :] = jnp.where(
        part < 2, across[: group // 2, :], across.T[group // 2 :, :]
    )
    size = keep.shape[0]
    side = block % 2
    keep[...] = pack[at(side * size, size, 8), :]
    send[...] = pack[at((1 - side) * size, size, 8), :]


def pair_kernel(
    live, p_own, p_core, p_far, p_cross, x, k, links,
    own_terms, off_terms, next_terms, gathered,
):
    half = x.shape[1] // 2
    rows, width = p_far.shape
    link = width // 2
    share = link // 4
    put_rows(p_own, p_core, gathered)
    put_rows(p_far, p_cross, gathered, half)
    masked = gathered[...] * live[...].astype(BF16)
    source = lax.broadcasted_iota(jnp.int32, (width, 2 * share), 0)
    target = lax.broadcasted_iota(jnp.int32, (width, 2 * share), 1)
    wanted = place()[0] * share + target + jnp.where(target < share, 0, link - share)
    columns = dot(masked, (source == wanted).astype(F32).astype(BF16)).T
    value = columns
    for step in range(TERMS):
        value = columns + value - times(times(value, x), k)
    left_side = stacked(times(value, x))
    terms = dot(left_side, masked)
    terms = terms[: 2 * share] + terms[2 * share :]
    cross = dot(left_side, links[...])
    cross = cross[: 2 * share] + cross[2 * share :]
    next_terms[:, :link] = terms[:share, :link]
    next_terms[:, link:] = cross[:share]
    off_terms[...] = terms[:share, link:]
    own_terms[:, :link] = terms[share:, link:]
    own_terms[:, link:] = cross[share:]


def start_kernel(s_own, y_own, y_core, far, cross, start, scaled, s_rows, y_rows):
    rows, group = y_own.shape
    width = s_rows.shape[1]
    half = width // 2
    part, near, core = place()
    top, bottom = at(near * half, half), at((1 - near) * half, half)
    left, right = at(near * half, half, 128), at((1 - near) * half, half, 128)
    low_left, low_right = (at(width + v * half, half, 128) for v in (near, 1 - near))

    def put(rows, cols, low_cols, value):
        start[rows, cols], start[rows, low_cols] = halves(value)

    for i in range(width // group):
        first, cols = i * group, slice(i * group, (i + 1) * group)
        put_rows(
            s_own.at[first : first + group, :],
            y_core.at[rows + first : rows + first + group, :],
            s_rows.at[:, cols],
        )
    put(top, left, low_left, s_rows[:, left])
    side = s_rows[:, right]
    put(top, right, low_right, side)
    put(bottom, left, low_left, side.T)
    for i in range(half // group):
        first = slice(2 * rows + i * group, 2 * rows + (i + 1) * group)
        put_rows(far.at[first, :], cross.at[first, :], s_rows.at[:, i * group : (i + 1) * group])
    put(bottom, right, low_right, s_rows[:, :half])
    for ref, mask in ((y_own, 0), (y_core, 1), (far, 2), (cross.at[rows:, :], 3)):
        y_rows[:, at((part ^ mask) * group, group, 128)] = ref[:rows, :]
    scaled[...] = times_wide(y_rows[...], start)


def back_kernel(*refs):
    sums, (start, scaled, schur, back, whole, parts) = refs[:8], refs[8:]
    part = place()[0]
    side = lax.axis_index("tm") % 2
    size = sums[0].shape[0]
    group, width = schur.shape
    span, diagonal = 2 * size, group * 3 // 4
    for mask in range(4):
        for half in range(2):
            rows = at((part ^ mask) * span + (side ^ half) * size, size, 8)
            whole[rows, :] = sums[2 * mask + half][...]

    def put(row, col, value):
        rows = slice(row * group, (row + 1) * group)
        high, low = halves(value)
        parts[rows, col * group : (col + 1) * group] = high
        parts[rows, width + col * group : width + (col + 1) * group] = low

    def across(row):
        first = row * span + diagonal + group
        other = first + 2 * span
        return jnp.concatenate(
            [whole[at(first, group // 2, 8), :], whole[at(other, group // 2, 8), :]], axis=0
        )

    for row in range(4):
        first = row * span
        put(row, row, unfolded(whole[first : first + diagonal, :]))
        value = whole[first + diagonal : first + diagonal + group, :]
        put(row, (row + 1) % 4, value)
        put((row + 1) % 4, row, value.T)
        if row < 2:
            value = across(row)
            put(row, row + 2, value)
            put(row + 2, row, value.T)
    before = (part + 3) % 4
    value = across(part % 2)
    for col, value in (
        (part, unfolded(whole[at(part * span, diagonal, 8), :])),
        ((part + 1) % 4, whole[at(part * span + diagonal, group, 8), :]),
        ((part + 2) % 4, jnp.where(part < 2, value, value.T)),
        (before, whole[at(before * span + diagonal, group, 8), :].T),
    ):
        schur[:, at(col * group, group, 128)] = value
    value = scaled[...]
    back[...] = 2.0 * value - times_wide(times_wide(value, parts), start)


def finish_kernel(own_terms, came, link_diag, link_cross):
    link = link_diag.shape[1]
    there = lax.axis_index("tm") + 1 < lax.axis_size("tm")
    link_diag[...] = own_terms[:, :link] + jnp.where(there, came[:, :link], 0.0)
    link_cross[...] = own_terms[:, link:] + jnp.where(there, came[:, link:], 0.0)


def call(kernel, outs, scratch, *args, sizes=None, whole=False, alias={}, flops=0):
    vmem = pl.BlockSpec(memory_space=pltpu.VMEM)
    specs = [pl.BlockSpec(memory_space=pltpu.HBM) if whole else vmem] * len(args)
    if whole:
        args = [pltpu.with_memory_space_constraint(arg, pltpu.HBM) for arg in args]
    if sizes is not None:
        specs, args = [pl.BlockSpec(memory_space=pltpu.SMEM), *specs], (sizes, *args)
    return pl.pallas_call(
        kernel,
        out_shape=[jax.ShapeDtypeStruct(shape, dtype) for shape, dtype in outs],
        in_specs=specs,
        out_specs=[vmem] * len(outs),
        scratch_shapes=scratch,
        input_output_aliases=alias,
        compiler_params=pltpu.CompilerParams(vmem_limit_bytes=VMEM_BYTES),
        cost_estimate=pl.CostEstimate(flops=flops, bytes_accessed=0, transcendentals=0),
        name=kernel.__name__,
    )(*args)


def after(value, *others):
    return lax.optimization_barrier((value, *others))[0]


def shards(
    blocks, operator, initial, block_sizes, link_index, link_pair, link_global, schur_base,
    schur_start,
):
    operator, initial = operator[0], initial[0]
    pair, glob = link_pair[0], link_global[0]
    rows, order = operator.shape
    half = order // 2
    unit = half // 3
    link, width = pair.shape[1] // 2, glob.shape[1]
    group, share = width // 4, link // 4
    size = group * 9 // 8

    def tile_swap(value, mask):
        return lax.ppermute(value, "tile", [(i, i ^ mask) for i in range(4)])

    def block_swap(value, mask):
        return lax.ppermute(value, "tm", [(i, i ^ mask) for i in range(blocks)])

    def diagonal_swap(value):
        pairs = [
            (b * 4 + i, (b ^ 1) * 4 + (i ^ 2)) for b in range(blocks) for i in range(4)
        ]
        return lax.ppermute(value, ("tm", "tile"), pairs)

    vmem, matrix = pltpu.VMEM, ((2 * order, order), BF16)

    g_far = tile_swap(glob, 2)
    x_sent, k_sent, x_own, k_own, g_own, s_own, index = call(
        pack_kernel,
        [((3 * unit + SPARE, unit), F32), ((3 * unit + 2 * SPARE, unit), F32),
         ((rows, order), F32), ((rows, order), F32), ((rows, width), BF16),
         ((width, group), F32), (link_index.shape, jnp.int32)],
        [pltpu.SemaphoreType.DMA((8,))],
        initial, operator, glob, schur_start, link_index, whole=True,
    )
    x_far, k_far = tile_swap(x_sent, 2), tile_swap(k_sent, 2)
    g_far = after(g_far, x_sent)
    g_cross = tile_swap(g_far, 1)
    x_far, g_cross = lax.optimization_barrier((x_far, g_cross))
    x, k, links, live_rows, live_cols, columns, first = call(
        prepare_kernel,
        [matrix, matrix, ((order, width), BF16), ((order, 1), F32), ((1, order), F32),
         ((group, order), F32), ((group, order), F32)],
        [vmem((half, order), F32), vmem((order, width), BF16)],
        x_own, k_own, tile_swap(x_own, 1), tile_swap(k_own, 1), g_own, tile_swap(g_own, 1),
        g_far, g_cross, index,
        x_far, tile_swap(x_far, 1), sizes=block_sizes,
    )
    k_far = after(k_far, first)
    p_core, p_far = (tile_swap(after(pair, first), m) for m in (1, 2))
    k_cross, p_core = lax.optimization_barrier((tile_swap(k_far, 1), p_core))
    keep, send, y_own, y_core, y_far, k = call(
        global_kernel,
        [((size, group), F32)] * 2 + [((rows, group), F32), ((rows + width, group), F32)]
        + [((2 * rows + 2 * group, group), F32), matrix],
        [vmem((2 * size, group), F32), vmem((order, group), F32)],
        live_cols, k_far, k_cross, x, k, links, columns, first, schur_base, s_own,
        alias={4: 5},
    )

    y_all = (y_own, tile_swap(y_core, 1), tile_swap(y_far, 2))
    if blocks > 2:
        parts = [block_swap(send, 1), block_swap(keep, 2), block_swap(send, 3)]
        total = (keep + parts[1]) + (parts[0] + parts[2])
    else:
        total = keep + block_swap(send, 1)
    p_far = after(p_far, keep)
    own_terms, off_terms, next_terms = call(
        pair_kernel,
        [((share, link + width), F32), ((share, link), F32), ((share, link + width), F32)],
        [vmem((order, 2 * link), BF16)],
        live_rows, pair, p_core, p_far, tile_swap(p_far, 1), x, k, after(links, total),
    )
    step = 4
    while step < blocks:
        other = block_swap(total, step)
        if step == 4:
            other, off_terms, *y_all = lax.optimization_barrier((other, off_terms, *y_all))
        total = total + other
        step *= 2
    cross = tile_swap(after(y_all[2], total), 1)
    start, scaled = call(
        start_kernel,
        [((width, 2 * width), BF16), ((rows, width), F32)],
        [vmem((2 * group, width), F32), vmem((rows, width), F32)],
        s_own, *y_all, cross,
    )

    near = after(block_swap(total, 1), scaled)
    here = (total, near)
    there = (after(tile_swap(total, 2), near), after(diagonal_swap(total), near))
    sums = []
    for pieces in (here, there):
        sums += [*pieces, *(tile_swap(piece, 1) for piece in pieces)]
    global_schur, back_cols = call(
        back_kernel,
        [((group, width), F32), ((rows, width), F32)],
        [vmem((8 * size, group), F32), vmem((width, 2 * width), BF16)],
        *sums, start, scaled,
        flops=int(6 * rows * order * order),
    )
    next_terms = after(next_terms, cross)
    came = lax.ppermute(next_terms, "tm", [(i, (i - 1) % blocks) for i in range(blocks)])
    link_diag, link_cross = call(
        finish_kernel,
        [((share, link), F32), ((share, width), F32)],
        [],
        own_terms, came,
    )
    return (
        link_diag[None], off_terms[None], link_cross[None], global_schur, back_cols[None],
    )


def solution(mesh):
    return jax.shard_map(
        functools.partial(shards, mesh.shape["tm"]),
        mesh=mesh,
        in_specs=(
            P("tm", "tile", None),
            P("tm", "tile", None),
            P("tm"),
            P("tm", None),
            P("tm", "tile", None),
            P("tm", "tile", None),
            P("tile", None),
            P("tile", None),
        ),
        out_specs=(
            P("tm", "tile", None),
            P("tm", "tile", None),
            P("tm", "tile", None),
            P("tile", None),
            P("tm", "tile", None),
        ),
        check_vma=False,
    )
```

```python
import functools

import jax
import jax.numpy as jnp
from jax import lax
from jax.experimental import pallas as pl
from jax.experimental.pallas import tpu as pltpu
from jax.sharding import PartitionSpec as P

BF16 = jnp.bfloat16
F32 = jnp.float32
STEPS = 2
TERMS = 2**STEPS - 1
SPARE = 8
VMEM_BYTES = 32 * 2**20


def halves(value):
    high = value.astype(BF16)
    return high, (value - high.astype(F32)).astype(BF16)


def dot(left_side, right_side):
    return jnp.dot(left_side, right_side, preferred_element_type=F32)


def both(value):
    return jnp.concatenate(halves(value), axis=1)


def stacked(value):
    return jnp.concatenate(halves(value), axis=0)


def at(start, size, unit=16):
    return pl.ds(pl.multiple_of(start, unit), size)


def place():
    part = lax.axis_index("tile")
    return part, part // 2, part % 2


def folded(square):
    half = square.shape[0] // 2
    last = square[half:, half:]
    last = jnp.concatenate([last[: half // 2, :], last[half // 2 :, :]], axis=1)
    return jnp.concatenate([square[:half, :], last], axis=0)


def unfolded(rows):
    half = rows.shape[1] // 2
    upper, last = rows[:half, :], rows[half:, :]
    last = jnp.concatenate([last[:, :half], last[:, half:]], axis=0)
    return jnp.concatenate(
        [upper, jnp.concatenate([upper[:, half:].T, last], axis=1)], axis=0
    )


def put_rows(own, other, target, offset=0):
    rows = own.shape[0]
    core = place()[2]
    target[at(offset + core * rows, rows), :] = own[...]
    target[at(offset + (1 - core) * rows, rows), :] = other[...]


def started(*pairs, sems):
    copies = [
        pltpu.make_async_copy(source, target, sems.at[i])
        for i, (source, target) in enumerate(pairs)
    ]
    for copy in copies:
        copy.start()
    return copies


def pack_kernel(
    x_rows, k_rows, g_rows, s_rows, index,
    x_out, k_out, x_own, k_own, g_own, s_out, index_out, sems,
):
    rows, order = x_rows.shape
    half = order // 2
    unit = half // 3
    group = s_rows.shape[0]
    _, near, core = place()
    copies = started(
        (x_rows, x_own),
        (k_rows, k_own),
        (g_rows, g_own),
        (index, index_out),
        *[
            (s_rows.at[:, first : first + group], s_out.at[first : first + group, :])
            for first in range(0, s_out.shape[0], group)
        ],
        sems=sems,
    )
    edge = at(near * half + core * 2 * unit, unit, 128)
    middle = at(near * half + unit, unit, 128)
    opposite = at(near * half + (1 - core) * 2 * unit, unit, 128)
    large = at(core * (rows - unit), unit, 8)
    small = at((1 - core) * unit, rows - unit, 8)
    for copy, own, out in zip(copies, (x_own, k_own), (x_out, k_out)):
        copy.wait()
        out[0:unit, :] = own[large, edge]
        out[unit : 2 * unit, :] = own[large, middle]
        out[2 * unit : unit + rows, :] = own[small, middle]
        block = own[large, opposite]
        out[unit + rows : 3 * unit, :] = jnp.where(
            core == 0, block[: unit // 2, :], block.T[unit // 2 :, :]
        )
        out[3 * unit :, :] = jnp.zeros((out.shape[0] - 3 * unit, unit), F32)
    for copy in copies[2:]:
        copy.wait()


def corner(far, cross, target, live):
    order = target.shape[1]
    half = order // 2
    unit = half // 3
    core = place()[2]

    def joined(first, last):
        mine, theirs = far[first:last, :], cross[first:last, :]
        return jnp.where(core == 0, mine, theirs), jnp.where(core == 0, theirs, mine)

    def put(row, col, value):
        first = half + row * unit
        cols = slice(half + col * unit, half + (col + 1) * unit)
        high, low = halves(value * live[:, cols])
        target[first : first + unit, cols] = high
        target[order + first : order + first + unit, cols] = low

    zero, one = joined(0, unit)
    put(0, 0, zero)
    put(2, 2, one)
    zero, one = joined(unit, 2 * unit)
    put(0, 1, zero)
    put(1, 0, zero.T)
    put(2, 1, one)
    put(1, 2, one.T)
    put(1, 1, jnp.concatenate(joined(2 * unit, 2 * unit + unit // 2), axis=0))
    side = jnp.concatenate(joined(2 * unit + unit // 2, 3 * unit), axis=0)
    put(0, 2, side)
    put(2, 0, side.T)


def spread(whole, target, live):
    half, order = whole.shape
    for rows, cols, value in (
        (slice(0, half), slice(0, order), whole[...]),
        (slice(half, order), slice(0, half), whole[:, half:].T),
    ):
        high, low = halves(value * live[:, cols])
        target[rows, cols] = high
        target[order + rows.start : order + rows.stop, cols] = low


def times(rows, matrix):
    count, order = rows.shape
    high = rows.astype(BF16)
    parts = stacked(rows)
    result = []
    for first in range(0, order, 256):
        cols = slice(first, min(first + 256, order))
        product = dot(parts, matrix[:order, cols])
        result.append((product[:count] + product[count:]) + dot(high, matrix[order:, cols]))
    return jnp.concatenate(result, axis=1)


def times_wide(left_side, right_side):
    width = right_side.shape[1] // 2
    high, low = halves(left_side)
    product = dot(high, right_side[...])
    return (product[:, :width] + product[:, width:]) + dot(low, right_side[:, :width])


def prepare_kernel(
    sizes, x_own, k_own, x_core, k_core, g_own, g_core, g_far, g_cross, index, far, cross,
    x, k, links, live_rows, live_cols, columns, first, whole, gathered,
):
    half, order = whole.shape
    rows = half // 2
    width = links.shape[1]
    group = width // 4
    part, near, core = place()
    for out, axis in ((live_rows, 0), (live_cols, 1)):
        ids = lax.broadcasted_iota(jnp.int32, out.shape, axis)
        ids = jnp.where(ids < half, ids + near * half, ids - near * half)
        out[...] = jnp.where(ids < sizes[0], 1.0, 0.0)
    for own, other, target in ((x_own, x_core, x), (k_own, k_core, k)):
        for side, col in enumerate((near * half, (1 - near) * half)):
            cols = slice(side * half, (side + 1) * half)
            whole[at(core * rows, rows), cols] = own[:, at(col, half, 128)]
            whole[at((1 - core) * rows, rows), cols] = other[:, at(col, half, 128)]
        spread(whole, target, live_cols)
    put_rows(g_own, g_core, gathered)
    put_rows(g_far, g_cross, gathered, half)
    hot = lax.broadcasted_iota(jnp.int32, (width, width), 0) == index[...]
    chosen = dot(gathered[...], hot.astype(F32).astype(BF16))
    links[...] = (chosen * live_rows[...]).astype(BF16)
    corner(far, cross, x, live_cols)
    value = links[:, at(part * group, group, 128)].astype(F32).T
    columns[...] = value
    high = value.astype(BF16)
    first[...] = dot(high, x[:order, :]) + dot(high, x[order:, :])


def global_kernel(
    live, far, cross, x, k_in, links, columns, product, base, s_own,
    keep, send, y_own, y_core, y_far, k, pack, solved,
):
    del k_in
    order, width = links.shape
    half = order // 2
    rows = half // 2
    group = width // 4
    part, near, core = place()
    time = lax.axis_index("tm")
    corner(far, cross, k, live)
    value = 2.0 * columns[...] - times(product[...], k)
    for step in range(TERMS - 1):
        value = columns[...] + value - times(times(value, x), k)
    result = times(value, x)
    left_side = stacked(result)
    solved[...] = result.T
    y_own[...] = solved[at(core * rows, rows), :]
    y_core[:rows, :] = solved[at((1 - core) * rows, rows), :]
    for i, block in enumerate((part, 2 * (1 - near), 2 * (1 - near) + 1)):
        first = rows + i * group
        y_core[first : first + group, :] = s_own[at(block * group, group, 8), :]
    y_far[:rows, :] = solved[at(half + core * rows, rows), :]
    y_far[rows : 2 * rows, :] = solved[at(half + (1 - core) * rows, rows), :]
    y_far[2 * rows :, :] = s_own[at(2 * near * group, 2 * group, 8), :]

    def square(shift):
        cols = at(((part + shift) % 4) * group, group, 128)
        parts = dot(left_side, links[:, cols])
        added = jnp.where(time == 0, base[:, cols], 0.0)
        return parts[:group] + parts[group:] + added

    first = group * 3 // 4
    pack[0:first, :] = folded(square(0))
    pack[first : first + group, :] = square(1)
    across = square(2)
    pack[first + group :, :] = jnp.where(
        part < 2, across[: group // 2, :], across.T[group // 2 :, :]
    )
    size = keep.shape[0]
    side = time % 2
    keep[...] = pack[at(side * size, size, 8), :]
    send[...] = pack[at((1 - side) * size, size, 8), :]


def pair_kernel(
    live, p_own, p_core, p_far, p_cross, x, k, links,
    own_terms, off_terms, next_terms, gathered,
):
    half = x.shape[1] // 2
    rows, width = p_far.shape
    link = width // 2
    share = link // 4
    put_rows(p_own, p_core, gathered)
    put_rows(p_far, p_cross, gathered, half)
    masked = gathered[...] * live[...].astype(BF16)
    source = lax.broadcasted_iota(jnp.int32, (width, 2 * share), 0)
    target = lax.broadcasted_iota(jnp.int32, (width, 2 * share), 1)
    wanted = place()[0] * share + target + jnp.where(target < share, 0, link - share)
    columns = dot(masked, (source == wanted).astype(F32).astype(BF16)).T
    value = columns
    for step in range(TERMS):
        value = columns + value - times(times(value, x), k)
    left_side = stacked(times(value, x))
    terms = dot(left_side, masked)
    terms = terms[: 2 * share] + terms[2 * share :]
    cross = dot(left_side, links[...])
    cross = cross[: 2 * share] + cross[2 * share :]
    next_terms[:, :link] = terms[:share, :link]
    next_terms[:, link:] = cross[:share]
    off_terms[...] = terms[:share, link:]
    own_terms[:, :link] = terms[share:, link:]
    own_terms[:, link:] = cross[share:]


def start_kernel(s_own, y_own, y_core, far, cross, start, scaled, s_rows, y_rows):
    rows, group = y_own.shape
    width = s_rows.shape[1]
    half = width // 2
    part, near, core = place()
    top, bottom = at(near * half, half), at((1 - near) * half, half)
    left, right = at(near * half, half, 128), at((1 - near) * half, half, 128)
    low_left, low_right = (at(width + v * half, half, 128) for v in (near, 1 - near))

    def put(rows, cols, low_cols, value):
        start[rows, cols], start[rows, low_cols] = halves(value)

    mine, theirs = at(core * group, group), at((1 - core) * group, group)
    for i in range(width // group):
        first = i * group
        s_rows[mine, first : first + group] = s_own[first : first + group, :]
    for i, block in enumerate((part ^ 1, 2 * (1 - near), 2 * (1 - near) + 1)):
        first = rows + i * group
        s_rows[theirs, at(block * group, group, 128)] = y_core[first : first + group, :]
    s_rows[theirs, at(part * group, group, 128)] = s_own[at((part ^ 1) * group, group, 8), :].T
    put(top, left, low_left, s_rows[:, left])
    side = s_rows[:, right]
    put(top, right, low_right, side)
    put(bottom, left, low_left, side.T)
    for i in range(half // group):
        first = slice(2 * rows + i * group, 2 * rows + (i + 1) * group)
        put_rows(far.at[first, :], cross.at[first, :], s_rows.at[:, i * group : (i + 1) * group])
    put(bottom, right, low_right, s_rows[:, :half])
    for ref, mask in ((y_own, 0), (y_core, 1), (far, 2), (cross.at[rows:, :], 3)):
        y_rows[:, at((part ^ mask) * group, group, 128)] = ref[:rows, :]
    scaled[...] = times_wide(y_rows[...], start)


def back_kernel(*refs):
    sums, (start, scaled, schur, back, whole, parts) = refs[:8], refs[8:]
    part = place()[0]
    side = lax.axis_index("tm") % 2
    size = sums[0].shape[0]
    group, width = schur.shape
    span, diagonal = 2 * size, group * 3 // 4
    for mask in range(4):
        for half in range(2):
            rows = at((part ^ mask) * span + (side ^ half) * size, size, 8)
            whole[rows, :] = sums[2 * mask + half][...]

    def put(row, col, value):
        rows = slice(row * group, (row + 1) * group)
        high, low = halves(value)
        parts[rows, col * group : (col + 1) * group] = high
        parts[rows, width + col * group : width + (col + 1) * group] = low

    def across(row):
        first = row * span + diagonal + group
        other = first + 2 * span
        return jnp.concatenate(
            [whole[at(first, group // 2, 8), :], whole[at(other, group // 2, 8), :]], axis=0
        )

    for row in range(4):
        first = row * span
        put(row, row, unfolded(whole[first : first + diagonal, :]))
        value = whole[first + diagonal : first + diagonal + group, :]
        put(row, (row + 1) % 4, value)
        put((row + 1) % 4, row, value.T)
        if row < 2:
            value = across(row)
            put(row, row + 2, value)
            put(row + 2, row, value.T)
    before = (part + 3) % 4
    value = across(part % 2)
    for col, value in (
        (part, unfolded(whole[at(part * span, diagonal, 8), :])),
        ((part + 1) % 4, whole[at(part * span + diagonal, group, 8), :]),
        ((part + 2) % 4, jnp.where(part < 2, value, value.T)),
        (before, whole[at(before * span + diagonal, group, 8), :].T),
    ):
        schur[:, at(col * group, group, 128)] = value
    value = scaled[...]
    back[...] = 2.0 * value - times_wide(times_wide(value, parts), start)


def finish_kernel(own_terms, came, link_diag, link_cross):
    link = link_diag.shape[1]
    there = lax.axis_index("tm") + 1 < lax.axis_size("tm")
    link_diag[...] = own_terms[:, :link] + jnp.where(there, came[:, :link], 0.0)
    link_cross[...] = own_terms[:, link:] + jnp.where(there, came[:, link:], 0.0)


def call(kernel, outs, scratch, *args, sizes=None, whole=False, alias={}, flops=0):
    vmem = pl.BlockSpec(memory_space=pltpu.VMEM)
    specs = [pl.BlockSpec(memory_space=pltpu.HBM) if whole else vmem] * len(args)
    if whole:
        args = [pltpu.with_memory_space_constraint(arg, pltpu.HBM) for arg in args]
    if sizes is not None:
        specs, args = [pl.BlockSpec(memory_space=pltpu.SMEM), *specs], (sizes, *args)
    return pl.pallas_call(
        kernel,
        out_shape=[jax.ShapeDtypeStruct(shape, dtype) for shape, dtype in outs],
        in_specs=specs,
        out_specs=[vmem] * len(outs),
        scratch_shapes=scratch,
        input_output_aliases=alias,
        compiler_params=pltpu.CompilerParams(vmem_limit_bytes=VMEM_BYTES),
        cost_estimate=pl.CostEstimate(flops=flops, bytes_accessed=0, transcendentals=0),
        name=kernel.__name__,
    )(*args)


def after(value, *others):
    return lax.optimization_barrier((value, *others))[0]


def shards(
    blocks, operator, initial, block_sizes, link_index, link_pair, link_global, schur_base,
    schur_start,
):
    operator, initial = operator[0], initial[0]
    pair, glob = link_pair[0], link_global[0]
    rows, order = operator.shape
    half = order // 2
    unit = half // 3
    link, width = pair.shape[1] // 2, glob.shape[1]
    group, share = width // 4, link // 4
    size = group * 9 // 8

    def tile_swap(value, mask):
        return lax.ppermute(value, "tile", [(i, i ^ mask) for i in range(4)])

    def block_swap(value, mask):
        return lax.ppermute(value, "tm", [(i, i ^ mask) for i in range(blocks)])

    def diagonal_swap(value):
        pairs = [
            (b * 4 + i, (b ^ 1) * 4 + (i ^ 2)) for b in range(blocks) for i in range(4)
        ]
        return lax.ppermute(value, ("tm", "tile"), pairs)

    vmem, matrix = pltpu.VMEM, ((2 * order, order), BF16)

    g_far = tile_swap(glob, 2)
    x_sent, k_sent, x_own, k_own, g_own, s_own, index = call(
        pack_kernel,
        [((3 * unit + SPARE, unit), F32), ((3 * unit + 2 * SPARE, unit), F32),
         ((rows, order), F32), ((rows, order), F32), ((rows, width), BF16),
         ((width, group), F32), (link_index.shape, jnp.int32)],
        [pltpu.SemaphoreType.DMA((8,))],
        initial, operator, glob, schur_start, link_index, whole=True,
    )
    x_far, k_far = tile_swap(x_sent, 2), tile_swap(k_sent, 2)
    g_far = after(g_far, x_sent)
    g_cross = tile_swap(g_far, 1)
    x_far, g_cross = lax.optimization_barrier((x_far, g_cross))
    x, k, links, live_rows, live_cols, columns, first = call(
        prepare_kernel,
        [matrix, matrix, ((order, width), BF16), ((order, 1), F32), ((1, order), F32),
         ((group, order), F32), ((group, order), F32)],
        [vmem((half, order), F32), vmem((order, width), BF16)],
        x_own, k_own, tile_swap(x_own, 1), tile_swap(k_own, 1), g_own, tile_swap(g_own, 1),
        g_far, g_cross, index,
        x_far, tile_swap(x_far, 1), sizes=block_sizes,
    )
    k_far = after(k_far, first)
    p_core, p_far = (tile_swap(after(pair, first), m) for m in (1, 2))
    k_cross, p_core = lax.optimization_barrier((tile_swap(k_far, 1), p_core))
    keep, send, y_own, y_core, y_far, k = call(
        global_kernel,
        [((size, group), F32)] * 2 + [((rows, group), F32), ((rows + 3 * group, group), F32)]
        + [((2 * rows + 2 * group, group), F32), matrix],
        [vmem((2 * size, group), F32), vmem((order, group), F32)],
        live_cols, k_far, k_cross, x, k, links, columns, first, schur_base, s_own,
        alias={4: 5},
    )

    y_all = (y_own, tile_swap(y_core, 1), tile_swap(y_far, 2))
    if blocks > 2:
        parts = [block_swap(send, 1), block_swap(keep, 2), block_swap(send, 3)]
        total = (keep + parts[1]) + (parts[0] + parts[2])
    else:
        total = keep + block_swap(send, 1)
    p_far = after(p_far, keep)
    own_terms, off_terms, next_terms = call(
        pair_kernel,
        [((share, link + width), F32), ((share, link), F32), ((share, link + width), F32)],
        [vmem((order, 2 * link), BF16)],
        live_rows, pair, p_core, p_far, tile_swap(p_far, 1), x, k, after(links, total),
    )
    step = 4
    while step < blocks:
        other = block_swap(total, step)
        if step == 4:
            other, off_terms, *y_all = lax.optimization_barrier((other, off_terms, *y_all))
        total = total + other
        step *= 2
    cross = tile_swap(after(y_all[2], total), 1)
    start, scaled = call(
        start_kernel,
        [((width, 2 * width), BF16), ((rows, width), F32)],
        [vmem((2 * group, width), F32), vmem((rows, width), F32)],
        s_own, *y_all, cross,
    )

    near = after(block_swap(total, 1), scaled)
    here = (total, near)
    there = (after(tile_swap(total, 2), near), after(diagonal_swap(total), near))
    sums = []
    for pieces in (here, there):
        sums += [*pieces, *(tile_swap(piece, 1) for piece in pieces)]
    global_schur, back_cols = call(
        back_kernel,
        [((group, width), F32), ((rows, width), F32)],
        [vmem((8 * size, group), F32), vmem((width, 2 * width), BF16)],
        *sums, start, scaled,
        flops=int(6 * rows * order * order),
    )
    next_terms = after(next_terms, cross)
    came = lax.ppermute(next_terms, "tm", [(i, (i - 1) % blocks) for i in range(blocks)])
    link_diag, link_cross = call(
        finish_kernel,
        [((share, link), F32), ((share, width), F32)],
        [],
        own_terms, came,
    )
    return (
        link_diag[None], off_terms[None], link_cross[None], global_schur, back_cols[None],
    )


def solution(mesh):
    return jax.shard_map(
        functools.partial(shards, mesh.shape["tm"]),
        mesh=mesh,
        in_specs=(
            P("tm", "tile", None),
            P("tm", "tile", None),
            P("tm"),
            P("tm", None),
            P("tm", "tile", None),
            P("tm", "tile", None),
            P("tile", None),
            P("tile", None),
        ),
        out_specs=(
            P("tm", "tile", None),
            P("tm", "tile", None),
            P("tm", "tile", None),
            P("tile", None),
            P("tm", "tile", None),
        ),
        check_vma=False,
    )
```

```python
import functools

import jax
import jax.numpy as jnp
from jax import lax
from jax.experimental import pallas as pl
from jax.experimental.pallas import tpu as pltpu
from jax.sharding import PartitionSpec as P

BF16 = jnp.bfloat16
F32 = jnp.float32
STEPS = 2
TERMS = 2**STEPS - 1
SPARE = 8
VMEM_BYTES = 32 * 2**20


def halves(value):
    high = value.astype(BF16)
    return high, (value - high.astype(F32)).astype(BF16)


def dot(left_side, right_side):
    return jnp.dot(left_side, right_side, preferred_element_type=F32)


def both(value):
    return jnp.concatenate(halves(value), axis=1)


def stacked(value):
    return jnp.concatenate(halves(value), axis=0)


def at(start, size, unit=16):
    return pl.ds(pl.multiple_of(start, unit), size)


def place():
    part = lax.axis_index("tile")
    return part, part // 2, part % 2


def folded(square):
    half = square.shape[0] // 2
    last = square[half:, half:]
    last = jnp.concatenate([last[: half // 2, :], last[half // 2 :, :]], axis=1)
    return jnp.concatenate([square[:half, :], last], axis=0)


def unfolded(rows):
    half = rows.shape[1] // 2
    upper, last = rows[:half, :], rows[half:, :]
    last = jnp.concatenate([last[:, :half], last[:, half:]], axis=0)
    return jnp.concatenate(
        [upper, jnp.concatenate([upper[:, half:].T, last], axis=1)], axis=0
    )


def put_rows(own, other, target, offset=0):
    rows = own.shape[0]
    core = place()[2]
    target[at(offset + core * rows, rows), :] = own[...]
    target[at(offset + (1 - core) * rows, rows), :] = other[...]


def started(*pairs, sems):
    copies = [
        pltpu.make_async_copy(source, target, sems.at[i])
        for i, (source, target) in enumerate(pairs)
    ]
    for copy in copies:
        copy.start()
    return copies


def pack_kernel(
    x_rows, k_rows, g_rows, s_rows, index,
    x_out, k_out, x_own, k_own, g_own, s_out, index_out, sems,
):
    rows, order = x_rows.shape
    half = order // 2
    unit = half // 3
    group = s_rows.shape[0]
    _, near, core = place()
    copies = started(
        (x_rows, x_own),
        (k_rows, k_own),
        (g_rows, g_own),
        (index, index_out),
        *[
            (s_rows.at[:, first : first + group], s_out.at[first : first + group, :])
            for first in range(0, s_out.shape[0], group)
        ],
        sems=sems,
    )
    edge = at(near * half + core * 2 * unit, unit, 128)
    middle = at(near * half + unit, unit, 128)
    opposite = at(near * half + (1 - core) * 2 * unit, unit, 128)
    large = at(core * (rows - unit), unit, 8)
    small = at((1 - core) * unit, rows - unit, 8)
    for copy, own, out in zip(copies, (x_own, k_own), (x_out, k_out)):
        copy.wait()
        out[0:unit, :] = own[large, edge]
        out[unit : 2 * unit, :] = own[large, middle]
        out[2 * unit : unit + rows, :] = own[small, middle]
        block = own[large, opposite]
        out[unit + rows : 3 * unit, :] = jnp.where(
            core == 0, block[: unit // 2, :], block.T[unit // 2 :, :]
        )
        out[3 * unit :, :] = jnp.zeros((out.shape[0] - 3 * unit, unit), F32)
    for copy in copies[2:]:
        copy.wait()


def corner(far, cross, target, live):
    order = target.shape[1]
    half = order // 2
    unit = half // 3
    core = place()[2]

    def joined(first, last):
        mine, theirs = far[first:last, :], cross[first:last, :]
        return jnp.where(core == 0, mine, theirs), jnp.where(core == 0, theirs, mine)

    def put(row, col, value):
        first = half + row * unit
        cols = slice(half + col * unit, half + (col + 1) * unit)
        high, low = halves(value * live[:, cols])
        target[first : first + unit, cols] = high
        target[order + first : order + first + unit, cols] = low

    zero, one = joined(0, unit)
    put(0, 0, zero)
    put(2, 2, one)
    zero, one = joined(unit, 2 * unit)
    put(0, 1, zero)
    put(1, 0, zero.T)
    put(2, 1, one)
    put(1, 2, one.T)
    put(1, 1, jnp.concatenate(joined(2 * unit, 2 * unit + unit // 2), axis=0))
    side = jnp.concatenate(joined(2 * unit + unit // 2, 3 * unit), axis=0)
    put(0, 2, side)
    put(2, 0, side.T)


def spread(whole, target, live):
    half, order = whole.shape
    for rows, cols, value in (
        (slice(0, half), slice(0, order), whole[...]),
        (slice(half, order), slice(0, half), whole[:, half:].T),
    ):
        high, low = halves(value * live[:, cols])
        target[rows, cols] = high
        target[order + rows.start : order + rows.stop, cols] = low


def times(rows, matrix):
    count, order = rows.shape
    high = rows.astype(BF16)
    parts = stacked(rows)
    result = []
    for first in range(0, order, 256):
        cols = slice(first, min(first + 256, order))
        product = dot(parts, matrix[:order, cols])
        result.append((product[:count] + product[count:]) + dot(high, matrix[order:, cols]))
    return jnp.concatenate(result, axis=1)


def times_wide(left_side, right_side):
    width = right_side.shape[1] // 2
    high, low = halves(left_side)
    product = dot(high, right_side[...])
    return (product[:, :width] + product[:, width:]) + dot(low, right_side[:, :width])


def prepare_kernel(
    sizes, x_own, k_own, x_core, k_core, g_own, g_core, g_far, g_cross, index, far, cross,
    x, k, links, live_rows, live_cols, columns, first, whole, gathered,
):
    half, order = whole.shape
    rows = half // 2
    width = links.shape[1]
    group = width // 4
    part, near, core = place()
    for out, axis in ((live_rows, 0), (live_cols, 1)):
        ids = lax.broadcasted_iota(jnp.int32, out.shape, axis)
        ids = jnp.where(ids < half, ids + near * half, ids - near * half)
        out[...] = jnp.where(ids < sizes[0], 1.0, 0.0)
    for own, other, target in ((x_own, x_core, x), (k_own, k_core, k)):
        for side, col in enumerate((near * half, (1 - near) * half)):
            cols = slice(side * half, (side + 1) * half)
            whole[at(core * rows, rows), cols] = own[:, at(col, half, 128)]
            whole[at((1 - core) * rows, rows), cols] = other[:, at(col, half, 128)]
        spread(whole, target, live_cols)
    put_rows(g_own, g_core, gathered)
    put_rows(g_far, g_cross, gathered, half)
    hot = lax.broadcasted_iota(jnp.int32, (width, width), 0) == index[...]
    chosen = dot(gathered[...], hot.astype(F32).astype(BF16))
    links[...] = (chosen * live_rows[...]).astype(BF16)
    corner(far, cross, x, live_cols)
    value = links[:, at(part * group, group, 128)].astype(F32).T
    columns[...] = value
    high = value.astype(BF16)
    first[...] = dot(high, x[:order, :]) + dot(high, x[order:, :])


def global_kernel(
    live, far, cross, x, k_in, links, columns, product, base, s_own,
    keep, send, y_own, y_core, y_far, k, pack, solved,
):
    del k_in
    order, width = links.shape
    half = order // 2
    rows = half // 2
    group = width // 4
    part, near, core = place()
    time = lax.axis_index("tm")
    corner(far, cross, k, live)
    value = 2.0 * columns[...] - times(product[...], k)
    for step in range(TERMS - 1):
        value = columns[...] + value - times(times(value, x), k)
    result = times(value, x)
    left_side = stacked(result)
    solved[...] = result.T
    y_own[...] = solved[at(core * rows, rows), :]
    y_core[:rows, :] = solved[at((1 - core) * rows, rows), :]
    for i, block in enumerate((part, 2 * (1 - near), 2 * (1 - near) + 1)):
        first = rows + i * group
        y_core[first : first + group, :] = s_own[at(block * group, group, 8), :]
    y_far[:rows, :] = solved[at(half + core * rows, rows), :]
    y_far[rows : 2 * rows, :] = solved[at(half + (1 - core) * rows, rows), :]
    y_far[2 * rows :, :] = s_own[at(2 * near * group, 2 * group, 8), :]

    def square(shift):
        cols = at(((part + shift) % 4) * group, group, 128)
        parts = dot(left_side, links[:, cols])
        added = jnp.where(time == 0, base[:, cols], 0.0)
        return parts[:group] + parts[group:] + added

    first = group * 3 // 4
    pack[0:first, :] = folded(square(0))
    pack[first : first + group, :] = square(1)
    across = square(2)
    pack[first + group :, :] = jnp.where(
        part < 2, across[: group // 2, :], across.T[group // 2 :, :]
    )
    size = keep.shape[0]
    side = time % 2
    keep[...] = pack[at(side * size, size, 8), :]
    send[...] = pack[at((1 - side) * size, size, 8), :]


def pair_kernel(
    live, p_own, p_core, p_far, p_cross, x, k, links,
    own_terms, off_terms, next_terms, gathered,
):
    half = x.shape[1] // 2
    rows, width = p_far.shape
    link = width // 2
    share = link // 4
    put_rows(p_own, p_core, gathered)
    put_rows(p_far, p_cross, gathered, half)
    masked = gathered[...] * live[...].astype(BF16)
    source = lax.broadcasted_iota(jnp.int32, (width, 2 * share), 0)
    target = lax.broadcasted_iota(jnp.int32, (width, 2 * share), 1)
    wanted = place()[0] * share + target + jnp.where(target < share, 0, link - share)
    columns = dot(masked, (source == wanted).astype(F32).astype(BF16)).T
    value = columns
    for step in range(TERMS):
        value = columns + value - times(times(value, x), k)
    left_side = stacked(times(value, x))
    terms = dot(left_side, masked)
    terms = terms[: 2 * share] + terms[2 * share :]
    cross = dot(left_side, links[...])
    cross = cross[: 2 * share] + cross[2 * share :]
    next_terms[:, :link] = terms[:share, :link]
    next_terms[:, link:] = cross[:share]
    off_terms[...] = terms[:share, link:]
    own_terms[:, :link] = terms[share:, link:]
    own_terms[:, link:] = cross[share:]


def start_kernel(s_own, y_own, y_core, far, cross, start, scaled, s_rows, y_rows):
    rows, group = y_own.shape
    width = s_rows.shape[1]
    half = width // 2
    part, near, core = place()
    top, bottom = at(near * half, half), at((1 - near) * half, half)
    left, right = at(near * half, half, 128), at((1 - near) * half, half, 128)
    low_left, low_right = (at(width + v * half, half, 128) for v in (near, 1 - near))

    def put(rows, cols, low_cols, value):
        start[rows, cols], start[rows, low_cols] = halves(value)

    mine, theirs = at(core * group, group), at((1 - core) * group, group)
    for i in range(width // group):
        first = i * group
        s_rows[mine, first : first + group] = s_own[first : first + group, :]
    for i, block in enumerate((part ^ 1, 2 * (1 - near), 2 * (1 - near) + 1)):
        first = rows + i * group
        s_rows[theirs, at(block * group, group, 128)] = y_core[first : first + group, :]
    s_rows[theirs, at(part * group, group, 128)] = s_own[at((part ^ 1) * group, group, 8), :].T
    put(top, left, low_left, s_rows[:, left])
    side = s_rows[:, right]
    put(top, right, low_right, side)
    put(bottom, left, low_left, side.T)
    for i in range(half // group):
        first = slice(2 * rows + i * group, 2 * rows + (i + 1) * group)
        put_rows(far.at[first, :], cross.at[first, :], s_rows.at[:, i * group : (i + 1) * group])
    put(bottom, right, low_right, s_rows[:, :half])
    for ref, mask in ((y_own, 0), (y_core, 1), (far, 2), (cross.at[rows:, :], 3)):
        y_rows[:, at((part ^ mask) * group, group, 128)] = ref[:rows, :]
    scaled[...] = times_wide(y_rows[...], start)


def back_kernel(*refs):
    sums, (start, scaled, schur, back, whole, parts) = refs[:8], refs[8:]
    part = place()[0]
    side = lax.axis_index("tm") % 2
    size = sums[0].shape[0]
    group, width = schur.shape
    span, diagonal = 2 * size, group * 3 // 4
    for mask in range(4):
        for half in range(2):
            rows = at((part ^ mask) * span + (side ^ half) * size, size, 8)
            whole[rows, :] = sums[2 * mask + half][...]

    def put(row, col, value):
        rows = slice(row * group, (row + 1) * group)
        high, low = halves(value)
        parts[rows, col * group : (col + 1) * group] = high
        parts[rows, width + col * group : width + (col + 1) * group] = low

    def across(row):
        first = row * span + diagonal + group
        other = first + 2 * span
        return jnp.concatenate(
            [whole[at(first, group // 2, 8), :], whole[at(other, group // 2, 8), :]], axis=0
        )

    for row in range(4):
        first = row * span
        put(row, row, unfolded(whole[first : first + diagonal, :]))
        value = whole[first + diagonal : first + diagonal + group, :]
        put(row, (row + 1) % 4, value)
        put((row + 1) % 4, row, value.T)
        if row < 2:
            value = across(row)
            put(row, row + 2, value)
            put(row + 2, row, value.T)
    before = (part + 3) % 4
    value = across(part % 2)
    for col, value in (
        (part, unfolded(whole[at(part * span, diagonal, 8), :])),
        ((part + 1) % 4, whole[at(part * span + diagonal, group, 8), :]),
        ((part + 2) % 4, jnp.where(part < 2, value, value.T)),
        (before, whole[at(before * span + diagonal, group, 8), :].T),
    ):
        schur[:, at(col * group, group, 128)] = value
    value = scaled[...]
    back[...] = 2.0 * value - times_wide(times_wide(value, parts), start)


def finish_kernel(own_terms, came, link_diag, link_cross):
    link = link_diag.shape[1]
    there = lax.axis_index("tm") + 1 < lax.axis_size("tm")
    link_diag[...] = own_terms[:, :link] + jnp.where(there, came[:, :link], 0.0)
    link_cross[...] = own_terms[:, link:] + jnp.where(there, came[:, link:], 0.0)


def call(kernel, outs, scratch, *args, sizes=None, whole=False, alias={}, flops=0):
    vmem = pl.BlockSpec(memory_space=pltpu.VMEM)
    specs = [pl.BlockSpec(memory_space=pltpu.HBM) if whole else vmem] * len(args)
    if whole:
        args = [pltpu.with_memory_space_constraint(arg, pltpu.HBM) for arg in args]
    if sizes is not None:
        specs, args = [pl.BlockSpec(memory_space=pltpu.SMEM), *specs], (sizes, *args)
    return pl.pallas_call(
        kernel,
        out_shape=[jax.ShapeDtypeStruct(shape, dtype) for shape, dtype in outs],
        in_specs=specs,
        out_specs=[vmem] * len(outs),
        scratch_shapes=scratch,
        input_output_aliases=alias,
        compiler_params=pltpu.CompilerParams(vmem_limit_bytes=VMEM_BYTES),
        cost_estimate=pl.CostEstimate(flops=flops, bytes_accessed=0, transcendentals=0),
        name=kernel.__name__,
    )(*args)


def after(value, *others):
    return lax.optimization_barrier((value, *others))[0]


def shards(
    blocks, operator, initial, block_sizes, link_index, link_pair, link_global, schur_base,
    schur_start,
):
    operator, initial = operator[0], initial[0]
    pair, glob = link_pair[0], link_global[0]
    rows, order = operator.shape
    half = order // 2
    unit = half // 3
    link, width = pair.shape[1] // 2, glob.shape[1]
    group, share = width // 4, link // 4
    size = group * 9 // 8

    def tile_swap(value, mask):
        return lax.ppermute(value, "tile", [(i, i ^ mask) for i in range(4)])

    def block_swap(value, mask):
        return lax.ppermute(value, "tm", [(i, i ^ mask) for i in range(blocks)])

    def diagonal_swap(value):
        pairs = [
            (b * 4 + i, (b ^ 1) * 4 + (i ^ 2)) for b in range(blocks) for i in range(4)
        ]
        return lax.ppermute(value, ("tm", "tile"), pairs)

    vmem, matrix = pltpu.VMEM, ((2 * order, order), BF16)

    g_far = tile_swap(glob, 2)
    x_sent, k_sent, x_own, k_own, g_own, s_own, index = call(
        pack_kernel,
        [((3 * unit + SPARE, unit), F32), ((3 * unit + 2 * SPARE, unit), F32),
         ((rows, order), F32), ((rows, order), F32), ((rows, width), BF16),
         ((width, group), F32), (link_index.shape, jnp.int32)],
        [pltpu.SemaphoreType.DMA((8,))],
        initial, operator, glob, schur_start, link_index, whole=True,
    )
    x_far, k_far = tile_swap(x_sent, 2), tile_swap(k_sent, 2)
    g_far = after(g_far, x_sent)
    g_cross = tile_swap(g_far, 1)
    x_far, g_cross = lax.optimization_barrier((x_far, g_cross))
    x, k, links, live_rows, live_cols, columns, first = call(
        prepare_kernel,
        [matrix, matrix, ((order, width), BF16), ((order, 1), F32), ((1, order), F32),
         ((group, order), F32), ((group, order), F32)],
        [vmem((half, order), F32), vmem((order, width), BF16)],
        x_own, k_own, tile_swap(x_own, 1), tile_swap(k_own, 1), g_own, tile_swap(g_own, 1),
        g_far, g_cross, index,
        x_far, tile_swap(x_far, 1), sizes=block_sizes,
    )
    k_far = after(k_far, first)
    p_core, p_far = (tile_swap(after(pair, first), m) for m in (1, 2))
    k_cross, p_core = lax.optimization_barrier((tile_swap(k_far, 1), p_core))
    keep, send, y_own, y_core, y_far, k = call(
        global_kernel,
        [((size, group), F32)] * 2 + [((rows, group), F32), ((rows + 3 * group, group), F32)]
        + [((2 * rows + 2 * group, group), F32), matrix],
        [vmem((2 * size, group), F32), vmem((order, group), F32)],
        live_cols, k_far, k_cross, x, k, links, columns, first, schur_base, s_own,
        alias={4: 5},
    )

    y_all = (y_own, tile_swap(y_core, 1), tile_swap(y_far, 2))
    if blocks > 2:
        parts = [block_swap(send, 1), block_swap(keep, 2), block_swap(send, 3)]
        total = (parts[2] + parts[0]) + (parts[1] + keep)
    else:
        total = keep + block_swap(send, 1)
    p_far = after(p_far, keep)
    own_terms, off_terms, next_terms = call(
        pair_kernel,
        [((share, link + width), F32), ((share, link), F32), ((share, link + width), F32)],
        [vmem((order, 2 * link), BF16)],
        live_rows, pair, p_core, p_far, tile_swap(p_far, 1), x, k, after(links, total),
    )
    step = 4
    while step < blocks:
        other = block_swap(total, step)
        if step == 4:
            other, off_terms, *y_all = lax.optimization_barrier((other, off_terms, *y_all))
        total = total + other
        step *= 2
    cross = tile_swap(after(y_all[2], total), 1)
    start, scaled = call(
        start_kernel,
        [((width, 2 * width), BF16), ((rows, width), F32)],
        [vmem((2 * group, width), F32), vmem((rows, width), F32)],
        s_own, *y_all, cross,
    )

    near = after(block_swap(total, 1), scaled)
    here = (total, near)
    there = (after(tile_swap(total, 2), near), after(diagonal_swap(total), near))
    sums = []
    for pieces in (here, there):
        sums += [*pieces, *(tile_swap(piece, 1) for piece in pieces)]
    global_schur, back_cols = call(
        back_kernel,
        [((group, width), F32), ((rows, width), F32)],
        [vmem((8 * size, group), F32), vmem((width, 2 * width), BF16)],
        *sums, start, scaled,
        flops=int(6 * rows * order * order),
    )
    next_terms = after(next_terms, cross)
    came = lax.ppermute(next_terms, "tm", [(i, (i - 1) % blocks) for i in range(blocks)])
    link_diag, link_cross = call(
        finish_kernel,
        [((share, link), F32), ((share, width), F32)],
        [],
        own_terms, came,
    )
    return (
        link_diag[None], off_terms[None], link_cross[None], global_schur, back_cols[None],
    )


def solution(mesh):
    return jax.shard_map(
        functools.partial(shards, mesh.shape["tm"]),
        mesh=mesh,
        in_specs=(
            P("tm", "tile", None),
            P("tm", "tile", None),
            P("tm"),
            P("tm", None),
            P("tm", "tile", None),
            P("tm", "tile", None),
            P("tile", None),
            P("tile", None),
        ),
        out_specs=(
            P("tm", "tile", None),
            P("tm", "tile", None),
            P("tm", "tile", None),
            P("tile", None),
            P("tm", "tile", None),
        ),
        check_vma=False,
    )
```

```python
import functools

import jax
import jax.numpy as jnp
from jax import lax
from jax.experimental import pallas as pl
from jax.experimental.pallas import tpu as pltpu
from jax.sharding import PartitionSpec as P

BF16 = jnp.bfloat16
F32 = jnp.float32
STEPS = 2
TERMS = 2**STEPS - 1
SPARE = 8
VMEM_BYTES = 32 * 2**20


def halves(value):
    high = value.astype(BF16)
    return high, (value - high.astype(F32)).astype(BF16)


def dot(left_side, right_side):
    return jnp.dot(left_side, right_side, preferred_element_type=F32)


def both(value):
    return jnp.concatenate(halves(value), axis=1)


def stacked(value):
    return jnp.concatenate(halves(value), axis=0)


def at(start, size, unit=16):
    return pl.ds(pl.multiple_of(start, unit), size)


def place():
    part = lax.axis_index("tile")
    return part, part // 2, part % 2


def folded(square):
    half = square.shape[0] // 2
    last = square[half:, half:]
    last = jnp.concatenate([last[: half // 2, :], last[half // 2 :, :]], axis=1)
    return jnp.concatenate([square[:half, :], last], axis=0)


def unfolded(rows):
    half = rows.shape[1] // 2
    upper, last = rows[:half, :], rows[half:, :]
    last = jnp.concatenate([last[:, :half], last[:, half:]], axis=0)
    return jnp.concatenate(
        [upper, jnp.concatenate([upper[:, half:].T, last], axis=1)], axis=0
    )


def put_rows(own, other, target, offset=0):
    rows = own.shape[0]
    core = place()[2]
    target[at(offset + core * rows, rows), :] = own[...]
    target[at(offset + (1 - core) * rows, rows), :] = other[...]


def started(*pairs, sems):
    copies = [
        pltpu.make_async_copy(source, target, sems.at[i])
        for i, (source, target) in enumerate(pairs)
    ]
    for copy in copies:
        copy.start()
    return copies


def pack_kernel(
    x_rows, k_rows, g_rows, s_rows, index,
    x_out, k_out, x_own, k_own, g_own, s_out, index_out, sems,
):
    rows, order = x_rows.shape
    half = order // 2
    unit = half // 3
    group = s_rows.shape[0]
    _, near, core = place()
    copies = started(
        (x_rows, x_own),
        (k_rows, k_own),
        (g_rows, g_own),
        (index, index_out),
        *[
            (s_rows.at[:, first : first + group], s_out.at[first : first + group, :])
            for first in range(0, s_out.shape[0], group)
        ],
        sems=sems,
    )
    edge = at(near * half + core * 2 * unit, unit, 128)
    middle = at(near * half + unit, unit, 128)
    opposite = at(near * half + (1 - core) * 2 * unit, unit, 128)
    large = at(core * (rows - unit), unit, 8)
    small = at((1 - core) * unit, rows - unit, 8)
    for copy, own, out in zip(copies, (x_own, k_own), (x_out, k_out)):
        copy.wait()
        out[0:unit, :] = own[large, edge]
        out[unit : 2 * unit, :] = own[large, middle]
        out[2 * unit : unit + rows, :] = own[small, middle]
        block = own[large, opposite]
        out[unit + rows : 3 * unit, :] = jnp.where(
            core == 0, block[: unit // 2, :], block.T[unit // 2 :, :]
        )
        out[3 * unit :, :] = jnp.zeros((out.shape[0] - 3 * unit, unit), F32)
    for copy in copies[2:]:
        copy.wait()


def corner(far, cross, target, live):
    order = target.shape[1]
    half = order // 2
    unit = half // 3
    core = place()[2]

    def joined(first, last):
        mine, theirs = far[first:last, :], cross[first:last, :]
        return jnp.where(core == 0, mine, theirs), jnp.where(core == 0, theirs, mine)

    def put(row, col, value):
        first = half + row * unit
        cols = slice(half + col * unit, half + (col + 1) * unit)
        high, low = halves(value * live[:, cols])
        target[first : first + unit, cols] = high
        target[order + first : order + first + unit, cols] = low

    zero, one = joined(0, unit)
    put(0, 0, zero)
    put(2, 2, one)
    zero, one = joined(unit, 2 * unit)
    put(0, 1, zero)
    put(1, 0, zero.T)
    put(2, 1, one)
    put(1, 2, one.T)
    put(1, 1, jnp.concatenate(joined(2 * unit, 2 * unit + unit // 2), axis=0))
    side = jnp.concatenate(joined(2 * unit + unit // 2, 3 * unit), axis=0)
    put(0, 2, side)
    put(2, 0, side.T)


def spread(whole, target, live):
    half, order = whole.shape
    for rows, cols, value in (
        (slice(0, half), slice(0, order), whole[...]),
        (slice(half, order), slice(0, half), whole[:, half:].T),
    ):
        high, low = halves(value * live[:, cols])
        target[rows, cols] = high
        target[order + rows.start : order + rows.stop, cols] = low


def times(rows, matrix):
    count, order = rows.shape
    high = rows.astype(BF16)
    parts = stacked(rows)
    result = []
    for first in range(0, order, 256):
        cols = slice(first, min(first + 256, order))
        product = dot(parts, matrix[:order, cols])
        result.append((product[:count] + product[count:]) + dot(high, matrix[order:, cols]))
    return jnp.concatenate(result, axis=1)


def times_wide(left_side, right_side):
    width = right_side.shape[1] // 2
    high, low = halves(left_side)
    product = dot(high, right_side[...])
    return (product[:, :width] + product[:, width:]) + dot(low, right_side[:, :width])


def prepare_kernel(
    sizes, x_own, k_own, x_core, k_core, g_own, g_core, g_far, g_cross, index, far, cross,
    x, k, links, live_rows, live_cols, columns, first, whole, gathered,
):
    half, order = whole.shape
    rows = half // 2
    width = links.shape[1]
    group = width // 4
    part, near, core = place()
    for out, axis in ((live_rows, 0), (live_cols, 1)):
        ids = lax.broadcasted_iota(jnp.int32, out.shape, axis)
        ids = jnp.where(ids < half, ids + near * half, ids - near * half)
        out[...] = jnp.where(ids < sizes[0], 1.0, 0.0)
    for own, other, target in ((x_own, x_core, x), (k_own, k_core, k)):
        for side, col in enumerate((near * half, (1 - near) * half)):
            cols = slice(side * half, (side + 1) * half)
            whole[at(core * rows, rows), cols] = own[:, at(col, half, 128)]
            whole[at((1 - core) * rows, rows), cols] = other[:, at(col, half, 128)]
        spread(whole, target, live_cols)
    put_rows(g_own, g_core, gathered)
    put_rows(g_far, g_cross, gathered, half)
    hot = lax.broadcasted_iota(jnp.int32, (width, width), 0) == index[...]
    chosen = dot(gathered[...], hot.astype(F32).astype(BF16))
    links[...] = (chosen * live_rows[...]).astype(BF16)
    corner(far, cross, x, live_cols)
    value = links[:, at(part * group, group, 128)].astype(F32).T
    columns[...] = value
    high = value.astype(BF16)
    first[...] = dot(high, x[:order, :]) + dot(high, x[order:, :])


def global_kernel(
    live, far, cross, x, k_in, links, columns, product, base, s_own,
    keep, send, y_own, y_core, y_far, k, pack, solved,
):
    del k_in
    order, width = links.shape
    half = order // 2
    rows = half // 2
    group = width // 4
    part, near, core = place()
    time = lax.axis_index("tm")
    corner(far, cross, k, live)
    value = 2.0 * columns[...] - times(product[...], k)
    for step in range(TERMS - 1):
        value = columns[...] + value - times(times(value, x), k)
    result = times(value, x)
    left_side = stacked(result)
    solved[...] = result.T
    y_own[...] = solved[at(core * rows, rows), :]
    y_core[:rows, :] = solved[at((1 - core) * rows, rows), :]
    for i, block in enumerate((part, 2 * (1 - near), 2 * (1 - near) + 1)):
        first = rows + i * group
        y_core[first : first + group, :] = s_own[at(block * group, group, 8), :]
    y_far[:rows, :] = solved[at(half + core * rows, rows), :]
    y_far[rows : 2 * rows, :] = solved[at(half + (1 - core) * rows, rows), :]
    y_far[2 * rows :, :] = s_own[at(2 * near * group, 2 * group, 8), :]

    def square(shift):
        cols = at(((part + shift) % 4) * group, group, 128)
        parts = dot(left_side, links[:, cols])
        added = jnp.where(time == 0, base[:, cols], 0.0)
        return parts[:group] + parts[group:] + added

    first = group * 3 // 4
    pack[0:first, :] = folded(square(0))
    pack[first : first + group, :] = square(1)
    across = square(2)
    pack[first + group :, :] = jnp.where(
        part < 2, across[: group // 2, :], across.T[group // 2 :, :]
    )
    size = keep.shape[0]
    side = time % 2
    keep[...] = pack[at(side * size, size, 8), :]
    send[...] = pack[at((1 - side) * size, size, 8), :]


def pair_kernel(
    live, p_own, p_core, p_far, p_cross, x, k, links,
    own_terms, off_terms, next_terms, gathered,
):
    half = x.shape[1] // 2
    rows, width = p_far.shape
    link = width // 2
    share = link // 4
    put_rows(p_own, p_core, gathered)
    put_rows(p_far, p_cross, gathered, half)
    masked = gathered[...] * live[...].astype(BF16)
    source = lax.broadcasted_iota(jnp.int32, (width, 2 * share), 0)
    target = lax.broadcasted_iota(jnp.int32, (width, 2 * share), 1)
    wanted = place()[0] * share + target + jnp.where(target < share, 0, link - share)
    columns = dot(masked, (source == wanted).astype(F32).astype(BF16)).T
    value = columns
    for step in range(TERMS):
        value = columns + value - times(times(value, x), k)
    left_side = stacked(times(value, x))
    terms = dot(left_side, masked)
    terms = terms[: 2 * share] + terms[2 * share :]
    cross = dot(left_side, links[...])
    cross = cross[: 2 * share] + cross[2 * share :]
    next_terms[:, :link] = terms[:share, :link]
    next_terms[:, link:] = cross[:share]
    off_terms[...] = terms[:share, link:]
    own_terms[:, :link] = terms[share:, link:]
    own_terms[:, link:] = cross[share:]


def start_kernel(s_own, y_own, y_core, far, cross, start, scaled, s_rows, y_rows):
    rows, group = y_own.shape
    width = s_rows.shape[1]
    half = width // 2
    part, near, core = place()
    top, bottom = at(near * half, half), at((1 - near) * half, half)
    left, right = at(near * half, half, 128), at((1 - near) * half, half, 128)
    low_left, low_right = (at(width + v * half, half, 128) for v in (near, 1 - near))

    def put(rows, cols, low_cols, value):
        start[rows, cols], start[rows, low_cols] = halves(value)

    mine, theirs = at(core * group, group), at((1 - core) * group, group)
    for i in range(width // group):
        first = i * group
        s_rows[mine, first : first + group] = s_own[first : first + group, :]
    for i, block in enumerate((part ^ 1, 2 * (1 - near), 2 * (1 - near) + 1)):
        first = rows + i * group
        s_rows[theirs, at(block * group, group, 128)] = y_core[first : first + group, :]
    s_rows[theirs, at(part * group, group, 128)] = s_own[at((part ^ 1) * group, group, 8), :].T
    put(top, left, low_left, s_rows[:, left])
    side = s_rows[:, right]
    put(top, right, low_right, side)
    put(bottom, left, low_left, side.T)
    for i in range(half // group):
        first = slice(2 * rows + i * group, 2 * rows + (i + 1) * group)
        put_rows(far.at[first, :], cross.at[first, :], s_rows.at[:, i * group : (i + 1) * group])
    put(bottom, right, low_right, s_rows[:, :half])
    for ref, mask in ((y_own, 0), (y_core, 1), (far, 2), (cross.at[rows:, :], 3)):
        y_rows[:, at((part ^ mask) * group, group, 128)] = ref[:rows, :]
    scaled[...] = times_wide(y_rows[...], start)


def back_kernel(*refs):
    sums, (start, scaled, schur_out, back_out) = refs[:8], refs[8:12]
    whole, parts, schur, back, sems = refs[12:]
    part = place()[0]
    side = lax.axis_index("tm") % 2
    size = sums[0].shape[0]
    group, width = schur.shape
    span, diagonal = 2 * size, group * 3 // 4
    for mask in range(4):
        for half in range(2):
            rows = at((part ^ mask) * span + (side ^ half) * size, size, 8)
            whole[rows, :] = sums[2 * mask + half][...]

    def put(row, col, value):
        rows = slice(row * group, (row + 1) * group)
        high, low = halves(value)
        parts[rows, col * group : (col + 1) * group] = high
        parts[rows, width + col * group : width + (col + 1) * group] = low

    def across(row):
        first = row * span + diagonal + group
        other = first + 2 * span
        return jnp.concatenate(
            [whole[at(first, group // 2, 8), :], whole[at(other, group // 2, 8), :]], axis=0
        )

    for row in range(4):
        first = row * span
        put(row, row, unfolded(whole[first : first + diagonal, :]))
        value = whole[first + diagonal : first + diagonal + group, :]
        put(row, (row + 1) % 4, value)
        put((row + 1) % 4, row, value.T)
        if row < 2:
            value = across(row)
            put(row, row + 2, value)
            put(row + 2, row, value.T)
    before = (part + 3) % 4
    value = across(part % 2)
    for col, value in (
        (part, unfolded(whole[at(part * span, diagonal, 8), :])),
        ((part + 1) % 4, whole[at(part * span + diagonal, group, 8), :]),
        ((part + 2) % 4, jnp.where(part < 2, value, value.T)),
        (before, whole[at(before * span + diagonal, group, 8), :].T),
    ):
        schur[:, at(col * group, group, 128)] = value
    copies = [pltpu.make_async_copy(schur, schur_out, sems.at[0])]
    copies[0].start()
    value = scaled[...]
    high, low = halves(times_wide(value, parts))
    half = width // 2
    for i, first in enumerate((0, half)):
        cols = slice(first, first + half)
        right_side = start[:, cols]
        product = dot(high, right_side) + dot(high, start[:, width + first : width + first + half])
        back[:, cols] = 2.0 * value[:, cols] - (product + dot(low, right_side))
        copies.append(
            pltpu.make_async_copy(back.at[:, cols], back_out.at[:, cols], sems.at[1 + i])
        )
        copies[-1].start()
    for copy in copies:
        copy.wait()


def finish_kernel(own_terms, came, link_diag, link_cross):
    link = link_diag.shape[1]
    there = lax.axis_index("tm") + 1 < lax.axis_size("tm")
    link_diag[...] = own_terms[:, :link] + jnp.where(there, came[:, :link], 0.0)
    link_cross[...] = own_terms[:, link:] + jnp.where(there, came[:, link:], 0.0)


def call(kernel, outs, scratch, *args, sizes=None, whole=False, out_whole=False, alias={}, flops=0):
    vmem = pl.BlockSpec(memory_space=pltpu.VMEM)
    specs = [pl.BlockSpec(memory_space=pltpu.HBM) if whole else vmem] * len(args)
    if whole:
        args = [pltpu.with_memory_space_constraint(arg, pltpu.HBM) for arg in args]
    if sizes is not None:
        specs, args = [pl.BlockSpec(memory_space=pltpu.SMEM), *specs], (sizes, *args)
    return pl.pallas_call(
        kernel,
        out_shape=[jax.ShapeDtypeStruct(shape, dtype) for shape, dtype in outs],
        in_specs=specs,
        out_specs=[pl.BlockSpec(memory_space=pltpu.HBM) if out_whole else vmem] * len(outs),
        scratch_shapes=scratch,
        input_output_aliases=alias,
        compiler_params=pltpu.CompilerParams(vmem_limit_bytes=VMEM_BYTES),
        cost_estimate=pl.CostEstimate(flops=flops, bytes_accessed=0, transcendentals=0),
        name=kernel.__name__,
    )(*args)


def after(value, *others):
    return lax.optimization_barrier((value, *others))[0]


def shards(
    blocks, operator, initial, block_sizes, link_index, link_pair, link_global, schur_base,
    schur_start,
):
    operator, initial = operator[0], initial[0]
    pair, glob = link_pair[0], link_global[0]
    rows, order = operator.shape
    half = order // 2
    unit = half // 3
    link, width = pair.shape[1] // 2, glob.shape[1]
    group, share = width // 4, link // 4
    size = group * 9 // 8

    def tile_swap(value, mask):
        return lax.ppermute(value, "tile", [(i, i ^ mask) for i in range(4)])

    def block_swap(value, mask):
        return lax.ppermute(value, "tm", [(i, i ^ mask) for i in range(blocks)])

    def diagonal_swap(value):
        pairs = [
            (b * 4 + i, (b ^ 1) * 4 + (i ^ 2)) for b in range(blocks) for i in range(4)
        ]
        return lax.ppermute(value, ("tm", "tile"), pairs)

    vmem, matrix = pltpu.VMEM, ((2 * order, order), BF16)

    g_far = tile_swap(glob, 2)
    x_sent, k_sent, x_own, k_own, g_own, s_own, index = call(
        pack_kernel,
        [((3 * unit + SPARE, unit), F32), ((3 * unit + 2 * SPARE, unit), F32),
         ((rows, order), F32), ((rows, order), F32), ((rows, width), BF16),
         ((width, group), F32), (link_index.shape, jnp.int32)],
        [pltpu.SemaphoreType.DMA((8,))],
        initial, operator, glob, schur_start, link_index, whole=True,
    )
    x_far, k_far = tile_swap(x_sent, 2), tile_swap(k_sent, 2)
    g_far = after(g_far, x_sent)
    g_cross = tile_swap(g_far, 1)
    x_far, g_cross = lax.optimization_barrier((x_far, g_cross))
    x, k, links, live_rows, live_cols, columns, first = call(
        prepare_kernel,
        [matrix, matrix, ((order, width), BF16), ((order, 1), F32), ((1, order), F32),
         ((group, order), F32), ((group, order), F32)],
        [vmem((half, order), F32), vmem((order, width), BF16)],
        x_own, k_own, tile_swap(x_own, 1), tile_swap(k_own, 1), g_own, tile_swap(g_own, 1),
        g_far, g_cross, index,
        x_far, tile_swap(x_far, 1), sizes=block_sizes,
    )
    k_far = after(k_far, first)
    p_core, p_far = (tile_swap(after(pair, first), m) for m in (1, 2))
    k_cross, p_core = lax.optimization_barrier((tile_swap(k_far, 1), p_core))
    keep, send, y_own, y_core, y_far, k = call(
        global_kernel,
        [((size, group), F32)] * 2 + [((rows, group), F32), ((rows + 3 * group, group), F32)]
        + [((2 * rows + 2 * group, group), F32), matrix],
        [vmem((2 * size, group), F32), vmem((order, group), F32)],
        live_cols, k_far, k_cross, x, k, links, columns, first, schur_base, s_own,
        alias={4: 5},
    )

    y_all = (y_own, tile_swap(y_core, 1), tile_swap(y_far, 2))
    if blocks > 2:
        parts = [block_swap(send, 1), block_swap(keep, 2), block_swap(send, 3)]
        total = (parts[2] + parts[0]) + (parts[1] + keep)
    else:
        total = keep + block_swap(send, 1)
    p_far = after(p_far, keep)
    own_terms, off_terms, next_terms = call(
        pair_kernel,
        [((share, link + width), F32), ((share, link), F32), ((share, link + width), F32)],
        [vmem((order, 2 * link), BF16)],
        live_rows, pair, p_core, p_far, tile_swap(p_far, 1), x, k, after(links, total),
    )
    step = 4
    while step < blocks:
        other = block_swap(total, step)
        if step == 4:
            other, off_terms, *y_all = lax.optimization_barrier((other, off_terms, *y_all))
        total = total + other
        step *= 2
    cross = tile_swap(after(y_all[2], total), 1)
    start, scaled = call(
        start_kernel,
        [((width, 2 * width), BF16), ((rows, width), F32)],
        [vmem((2 * group, width), F32), vmem((rows, width), F32)],
        s_own, *y_all, cross,
    )

    near = after(block_swap(total, 1), scaled)
    here = (total, near)
    there = (after(tile_swap(total, 2), near), after(diagonal_swap(total), near))
    sums = []
    for pieces in (here, there):
        sums += [*pieces, *(tile_swap(piece, 1) for piece in pieces)]
    global_schur, back_cols = call(
        back_kernel,
        [((group, width), F32), ((rows, width), F32)],
        [vmem((8 * size, group), F32), vmem((width, 2 * width), BF16), vmem((group, width), F32),
         vmem((rows, width), F32), pltpu.SemaphoreType.DMA((3,))],
        *sums, start, scaled, out_whole=True,
        flops=int(6 * rows * order * order),
    )
    next_terms = after(next_terms, cross)
    came = lax.ppermute(next_terms, "tm", [(i, (i - 1) % blocks) for i in range(blocks)])
    link_diag, link_cross = call(
        finish_kernel,
        [((share, link), F32), ((share, width), F32)],
        [],
        own_terms, came,
    )
    return (
        link_diag[None], off_terms[None], link_cross[None], global_schur, back_cols[None],
    )


def solution(mesh):
    return jax.shard_map(
        functools.partial(shards, mesh.shape["tm"]),
        mesh=mesh,
        in_specs=(
            P("tm", "tile", None),
            P("tm", "tile", None),
            P("tm"),
            P("tm", None),
            P("tm", "tile", None),
            P("tm", "tile", None),
            P("tile", None),
            P("tile", None),
        ),
        out_specs=(
            P("tm", "tile", None),
            P("tm", "tile", None),
            P("tm", "tile", None),
            P("tile", None),
            P("tm", "tile", None),
        ),
        check_vma=False,
    )
```

```python
import functools

import jax
import jax.numpy as jnp
from jax import lax
from jax.experimental import pallas as pl
from jax.experimental.pallas import tpu as pltpu
from jax.sharding import PartitionSpec as P

BF16 = jnp.bfloat16
F32 = jnp.float32
STEPS = 2
TERMS = 2**STEPS - 1
SPARE = 8
VMEM_BYTES = 32 * 2**20


def halves(value):
    high = value.astype(BF16)
    return high, (value - high.astype(F32)).astype(BF16)


def dot(left_side, right_side):
    return jnp.dot(left_side, right_side, preferred_element_type=F32)


def both(value):
    return jnp.concatenate(halves(value), axis=1)


def stacked(value):
    return jnp.concatenate(halves(value), axis=0)


def at(start, size, unit=16):
    return pl.ds(pl.multiple_of(start, unit), size)


def place():
    part = lax.axis_index("tile")
    return part, part // 2, part % 2


def folded(square):
    half = square.shape[0] // 2
    last = square[half:, half:]
    last = jnp.concatenate([last[: half // 2, :], last[half // 2 :, :]], axis=1)
    return jnp.concatenate([square[:half, :], last], axis=0)


def unfolded(rows):
    half = rows.shape[1] // 2
    upper, last = rows[:half, :], rows[half:, :]
    last = jnp.concatenate([last[:, :half], last[:, half:]], axis=0)
    return jnp.concatenate(
        [upper, jnp.concatenate([upper[:, half:].T, last], axis=1)], axis=0
    )


def put_rows(own, other, target, offset=0):
    rows = own.shape[0]
    core = place()[2]
    target[at(offset + core * rows, rows), :] = own[...]
    target[at(offset + (1 - core) * rows, rows), :] = other[...]


def started(*pairs, sems):
    copies = [
        pltpu.make_async_copy(source, target, sems.at[i])
        for i, (source, target) in enumerate(pairs)
    ]
    for copy in copies:
        copy.start()
    return copies


def pack_kernel(
    x_rows, k_rows, g_rows, s_rows, index,
    x_out, k_out, x_own, k_own, g_own, s_out, index_out, sems,
):
    rows, order = x_rows.shape
    half = order // 2
    unit = half // 3
    group = s_rows.shape[0]
    _, near, core = place()
    copies = started(
        (x_rows, x_own),
        (k_rows, k_own),
        (g_rows, g_own),
        (index, index_out),
        *[
            (s_rows.at[:, first : first + group], s_out.at[first : first + group, :])
            for first in range(0, s_out.shape[0], group)
        ],
        sems=sems,
    )
    edge = at(near * half + core * 2 * unit, unit, 128)
    middle = at(near * half + unit, unit, 128)
    opposite = at(near * half + (1 - core) * 2 * unit, unit, 128)
    large = at(core * (rows - unit), unit, 8)
    small = at((1 - core) * unit, rows - unit, 8)
    for copy, own, out in zip(copies, (x_own, k_own), (x_out, k_out)):
        copy.wait()
        out[0:unit, :] = own[large, edge]
        out[unit : 2 * unit, :] = own[large, middle]
        out[2 * unit : unit + rows, :] = own[small, middle]
        block = own[large, opposite]
        out[unit + rows : 3 * unit, :] = jnp.where(
            core == 0, block[: unit // 2, :], block.T[unit // 2 :, :]
        )
        out[3 * unit :, :] = jnp.zeros((out.shape[0] - 3 * unit, unit), F32)
    for copy in copies[2:]:
        copy.wait()


def corner(far, cross, target, live):
    order = target.shape[1]
    half = order // 2
    unit = half // 3
    core = place()[2]

    def joined(first, last):
        mine, theirs = far[first:last, :], cross[first:last, :]
        return jnp.where(core == 0, mine, theirs), jnp.where(core == 0, theirs, mine)

    def put(row, col, value):
        first = half + row * unit
        cols = slice(half + col * unit, half + (col + 1) * unit)
        high, low = halves(value * live[:, cols])
        target[first : first + unit, cols] = high
        target[order + first : order + first + unit, cols] = low

    zero, one = joined(0, unit)
    put(0, 0, zero)
    put(2, 2, one)
    zero, one = joined(unit, 2 * unit)
    put(0, 1, zero)
    put(1, 0, zero.T)
    put(2, 1, one)
    put(1, 2, one.T)
    put(1, 1, jnp.concatenate(joined(2 * unit, 2 * unit + unit // 2), axis=0))
    side = jnp.concatenate(joined(2 * unit + unit // 2, 3 * unit), axis=0)
    put(0, 2, side)
    put(2, 0, side.T)


def spread(whole, target, live):
    half, order = whole.shape
    for rows, cols, value in (
        (slice(0, half), slice(0, order), whole[...]),
        (slice(half, order), slice(0, half), whole[:, half:].T),
    ):
        high, low = halves(value * live[:, cols])
        target[rows, cols] = high
        target[order + rows.start : order + rows.stop, cols] = low


def times(rows, matrix):
    count, order = rows.shape
    high = rows.astype(BF16)
    parts = stacked(rows)
    result = []
    for first in range(0, order, 256):
        cols = slice(first, min(first + 256, order))
        product = dot(parts, matrix[:order, cols])
        result.append((product[:count] + product[count:]) + dot(high, matrix[order:, cols]))
    return jnp.concatenate(result, axis=1)


def times_wide(left_side, right_side, first, last):
    count, width = left_side.shape[0], right_side.shape[1] // 2
    parts = stacked(left_side)
    product = dot(parts, right_side[:, first:last])
    return (product[:count] + product[count:]) + dot(
        parts[:count], right_side[:, width + first : width + last]
    )


def prepare_kernel(
    sizes, x_own, k_own, x_core, k_core, g_own, g_core, g_far, g_cross, index, far, cross,
    x, k, links, live_rows, live_cols, columns, first, whole, gathered,
):
    half, order = whole.shape
    rows = half // 2
    width = links.shape[1]
    group = width // 4
    part, near, core = place()
    for out, axis in ((live_rows, 0), (live_cols, 1)):
        ids = lax.broadcasted_iota(jnp.int32, out.shape, axis)
        ids = jnp.where(ids < half, ids + near * half, ids - near * half)
        out[...] = jnp.where(ids < sizes[0], 1.0, 0.0)
    for own, other, target in ((x_own, x_core, x), (k_own, k_core, k)):
        for side, col in enumerate((near * half, (1 - near) * half)):
            cols = slice(side * half, (side + 1) * half)
            whole[at(core * rows, rows), cols] = own[:, at(col, half, 128)]
            whole[at((1 - core) * rows, rows), cols] = other[:, at(col, half, 128)]
        spread(whole, target, live_cols)
    put_rows(g_own, g_core, gathered)
    put_rows(g_far, g_cross, gathered, half)
    hot = lax.broadcasted_iota(jnp.int32, (width, width), 0) == index[...]
    chosen = dot(gathered[...], hot.astype(F32).astype(BF16))
    links[...] = (chosen * live_rows[...]).astype(BF16)
    corner(far, cross, x, live_cols)
    value = links[:, at(part * group, group, 128)].astype(F32).T
    columns[...] = value
    high = value.astype(BF16)
    first[...] = dot(high, x[:order, :]) + dot(high, x[order:, :])


def global_kernel(
    live, far, cross, x, k_in, links, columns, product, base, s_own,
    keep, send, y_own, y_core, y_far, k, pack, solved,
):
    del k_in
    order, width = links.shape
    half = order // 2
    rows = half // 2
    group = width // 4
    part, near, core = place()
    time = lax.axis_index("tm")
    corner(far, cross, k, live)
    value = 2.0 * columns[...] - times(product[...], k)
    for step in range(TERMS - 1):
        value = columns[...] + value - times(times(value, x), k)
    result = times(value, x)
    left_side = stacked(result)
    solved[...] = result.T
    y_own[...] = solved[at(core * rows, rows), :]
    y_core[:rows, :] = solved[at((1 - core) * rows, rows), :]
    for i, block in enumerate((part, 2 * (1 - near), 2 * (1 - near) + 1)):
        first = rows + i * group
        y_core[first : first + group, :] = s_own[at(block * group, group, 8), :]
    y_far[:rows, :] = solved[at(half + core * rows, rows), :]
    y_far[rows : 2 * rows, :] = solved[at(half + (1 - core) * rows, rows), :]
    y_far[2 * rows :, :] = s_own[at(2 * near * group, 2 * group, 8), :]

    def square(shift):
        cols = at(((part + shift) % 4) * group, group, 128)
        parts = dot(left_side, links[:, cols])
        added = jnp.where(time == 0, base[:, cols], 0.0)
        return parts[:group] + parts[group:] + added

    first = group * 3 // 4
    pack[0:first, :] = folded(square(0))
    pack[first : first + group, :] = square(1)
    across = square(2)
    pack[first + group :, :] = jnp.where(
        part < 2, across[: group // 2, :], across.T[group // 2 :, :]
    )
    size = keep.shape[0]
    side = time % 2
    keep[...] = pack[at(side * size, size, 8), :]
    send[...] = pack[at((1 - side) * size, size, 8), :]


def pair_kernel(
    live, p_own, p_core, p_far, p_cross, x, k, links,
    own_terms, off_terms, next_terms, gathered,
):
    half = x.shape[1] // 2
    rows, width = p_far.shape
    link = width // 2
    share = link // 4
    put_rows(p_own, p_core, gathered)
    put_rows(p_far, p_cross, gathered, half)
    masked = gathered[...] * live[...].astype(BF16)
    source = lax.broadcasted_iota(jnp.int32, (width, 2 * share), 0)
    target = lax.broadcasted_iota(jnp.int32, (width, 2 * share), 1)
    wanted = place()[0] * share + target + jnp.where(target < share, 0, link - share)
    columns = dot(masked, (source == wanted).astype(F32).astype(BF16)).T
    value = columns
    for step in range(TERMS):
        value = columns + value - times(times(value, x), k)
    left_side = stacked(times(value, x))
    terms = dot(left_side, masked)
    terms = terms[: 2 * share] + terms[2 * share :]
    cross = dot(left_side, links[...])
    cross = cross[: 2 * share] + cross[2 * share :]
    next_terms[:, :link] = terms[:share, :link]
    next_terms[:, link:] = cross[:share]
    off_terms[...] = terms[:share, link:]
    own_terms[:, :link] = terms[share:, link:]
    own_terms[:, link:] = cross[share:]


def start_kernel(s_own, y_own, y_core, far, cross, start, scaled, s_rows, y_rows):
    rows, group = y_own.shape
    width = s_rows.shape[1]
    half = width // 2
    part, near, core = place()
    top, bottom = at(near * half, half), at((1 - near) * half, half)
    left, right = at(near * half, half, 128), at((1 - near) * half, half, 128)
    low_left, low_right = (at(width + v * half, half, 128) for v in (near, 1 - near))

    def put(rows, cols, low_cols, value):
        start[rows, cols], start[rows, low_cols] = halves(value)

    mine, theirs = at(core * group, group), at((1 - core) * group, group)
    for i in range(width // group):
        first = i * group
        s_rows[mine, first : first + group] = s_own[first : first + group, :]
    for i, block in enumerate((part ^ 1, 2 * (1 - near), 2 * (1 - near) + 1)):
        first = rows + i * group
        s_rows[theirs, at(block * group, group, 128)] = y_core[first : first + group, :]
    s_rows[theirs, at(part * group, group, 128)] = s_own[at((part ^ 1) * group, group, 8), :].T
    put(top, left, low_left, s_rows[:, left])
    side = s_rows[:, right]
    put(top, right, low_right, side)
    put(bottom, left, low_left, side.T)
    for i in range(half // group):
        first = slice(2 * rows + i * group, 2 * rows + (i + 1) * group)
        put_rows(far.at[first, :], cross.at[first, :], s_rows.at[:, i * group : (i + 1) * group])
    put(bottom, right, low_right, s_rows[:, :half])
    for ref, mask in ((y_own, 0), (y_core, 1), (far, 2), (cross.at[rows:, :], 3)):
        y_rows[:, at((part ^ mask) * group, group, 128)] = ref[:rows, :]
    for first in range(0, width, half):
        scaled[:, first : first + half] = times_wide(y_rows[...], start, first, first + half)


def back_kernel(*refs):
    sums, (start, scaled, schur_out, back_out) = refs[:8], refs[8:12]
    whole, parts, schur, back, sems = refs[12:]
    part = place()[0]
    side = lax.axis_index("tm") % 2
    size = sums[0].shape[0]
    group, width = schur.shape
    span, diagonal = 2 * size, group * 3 // 4
    for mask in range(4):
        for half in range(2):
            rows = at((part ^ mask) * span + (side ^ half) * size, size, 8)
            whole[rows, :] = sums[2 * mask + half][...]

    def put(row, col, value):
        rows = slice(row * group, (row + 1) * group)
        high, low = halves(value)
        parts[rows, col * group : (col + 1) * group] = high
        parts[rows, width + col * group : width + (col + 1) * group] = low

    def across(row):
        first = row * span + diagonal + group
        other = first + 2 * span
        return jnp.concatenate(
            [whole[at(first, group // 2, 8), :], whole[at(other, group // 2, 8), :]], axis=0
        )

    for row in range(4):
        first = row * span
        put(row, row, unfolded(whole[first : first + diagonal, :]))
        value = whole[first + diagonal : first + diagonal + group, :]
        put(row, (row + 1) % 4, value)
        put((row + 1) % 4, row, value.T)
        if row < 2:
            value = across(row)
            put(row, row + 2, value)
            put(row + 2, row, value.T)
    before = (part + 3) % 4
    value = across(part % 2)
    for col, value in (
        (part, unfolded(whole[at(part * span, diagonal, 8), :])),
        ((part + 1) % 4, whole[at(part * span + diagonal, group, 8), :]),
        ((part + 2) % 4, jnp.where(part < 2, value, value.T)),
        (before, whole[at(before * span + diagonal, group, 8), :].T),
    ):
        schur[:, at(col * group, group, 128)] = value
    copies = [pltpu.make_async_copy(schur, schur_out, sems.at[0])]
    copies[0].start()
    value = scaled[...]
    half = width // 2
    result = jnp.concatenate(
        [times_wide(value, parts, first, first + half) for first in (0, half)], axis=1
    )
    for i, first in enumerate((0, half)):
        cols = slice(first, first + half)
        back[:, cols] = 2.0 * value[:, cols] - times_wide(result, start, first, first + half)
        copies.append(
            pltpu.make_async_copy(back.at[:, cols], back_out.at[:, cols], sems.at[1 + i])
        )
        copies[-1].start()
    for copy in copies:
        copy.wait()


def finish_kernel(own_terms, came, link_diag, link_cross):
    link = link_diag.shape[1]
    there = lax.axis_index("tm") + 1 < lax.axis_size("tm")
    link_diag[...] = own_terms[:, :link] + jnp.where(there, came[:, :link], 0.0)
    link_cross[...] = own_terms[:, link:] + jnp.where(there, came[:, link:], 0.0)


def call(kernel, outs, scratch, *args, sizes=None, whole=False, out_whole=False, alias={}, flops=0):
    vmem = pl.BlockSpec(memory_space=pltpu.VMEM)
    specs = [pl.BlockSpec(memory_space=pltpu.HBM) if whole else vmem] * len(args)
    if whole:
        args = [pltpu.with_memory_space_constraint(arg, pltpu.HBM) for arg in args]
    if sizes is not None:
        specs, args = [pl.BlockSpec(memory_space=pltpu.SMEM), *specs], (sizes, *args)
    return pl.pallas_call(
        kernel,
        out_shape=[jax.ShapeDtypeStruct(shape, dtype) for shape, dtype in outs],
        in_specs=specs,
        out_specs=[pl.BlockSpec(memory_space=pltpu.HBM) if out_whole else vmem] * len(outs),
        scratch_shapes=scratch,
        input_output_aliases=alias,
        compiler_params=pltpu.CompilerParams(vmem_limit_bytes=VMEM_BYTES),
        cost_estimate=pl.CostEstimate(flops=flops, bytes_accessed=0, transcendentals=0),
        name=kernel.__name__,
    )(*args)


def after(value, *others):
    return lax.optimization_barrier((value, *others))[0]


def shards(
    blocks, operator, initial, block_sizes, link_index, link_pair, link_global, schur_base,
    schur_start,
):
    operator, initial = operator[0], initial[0]
    pair, glob = link_pair[0], link_global[0]
    rows, order = operator.shape
    half = order // 2
    unit = half // 3
    link, width = pair.shape[1] // 2, glob.shape[1]
    group, share = width // 4, link // 4
    size = group * 9 // 8

    def tile_swap(value, mask):
        return lax.ppermute(value, "tile", [(i, i ^ mask) for i in range(4)])

    def block_swap(value, mask):
        return lax.ppermute(value, "tm", [(i, i ^ mask) for i in range(blocks)])

    def diagonal_swap(value):
        pairs = [
            (b * 4 + i, (b ^ 1) * 4 + (i ^ 2)) for b in range(blocks) for i in range(4)
        ]
        return lax.ppermute(value, ("tm", "tile"), pairs)

    vmem, matrix = pltpu.VMEM, ((2 * order, order), BF16)

    g_far = tile_swap(glob, 2)
    x_sent, k_sent, x_own, k_own, g_own, s_own, index = call(
        pack_kernel,
        [((3 * unit + SPARE, unit), F32), ((3 * unit + 2 * SPARE, unit), F32),
         ((rows, order), F32), ((rows, order), F32), ((rows, width), BF16),
         ((width, group), F32), (link_index.shape, jnp.int32)],
        [pltpu.SemaphoreType.DMA((8,))],
        initial, operator, glob, schur_start, link_index, whole=True,
    )
    x_far, k_far = tile_swap(x_sent, 2), tile_swap(k_sent, 2)
    g_far = after(g_far, x_sent)
    g_cross = tile_swap(g_far, 1)
    x_far, g_cross = lax.optimization_barrier((x_far, g_cross))
    x, k, links, live_rows, live_cols, columns, first = call(
        prepare_kernel,
        [matrix, matrix, ((order, width), BF16), ((order, 1), F32), ((1, order), F32),
         ((group, order), F32), ((group, order), F32)],
        [vmem((half, order), F32), vmem((order, width), BF16)],
        x_own, k_own, tile_swap(x_own, 1), tile_swap(k_own, 1), g_own, tile_swap(g_own, 1),
        g_far, g_cross, index,
        x_far, tile_swap(x_far, 1), sizes=block_sizes,
    )
    k_far = after(k_far, first)
    p_core, p_far = (tile_swap(after(pair, first), m) for m in (1, 2))
    k_cross, p_core = lax.optimization_barrier((tile_swap(k_far, 1), p_core))
    keep, send, y_own, y_core, y_far, k = call(
        global_kernel,
        [((size, group), F32)] * 2 + [((rows, group), F32), ((rows + 3 * group, group), F32)]
        + [((2 * rows + 2 * group, group), F32), matrix],
        [vmem((2 * size, group), F32), vmem((order, group), F32)],
        live_cols, k_far, k_cross, x, k, links, columns, first, schur_base, s_own,
        alias={4: 5},
    )

    y_all = (y_own, tile_swap(y_core, 1), tile_swap(y_far, 2))
    if blocks > 2:
        parts = [block_swap(send, 1), block_swap(keep, 2), block_swap(send, 3)]
        total = (parts[2] + parts[0]) + (parts[1] + keep)
    else:
        total = keep + block_swap(send, 1)
    p_far = after(p_far, keep)
    own_terms, off_terms, next_terms = call(
        pair_kernel,
        [((share, link + width), F32), ((share, link), F32), ((share, link + width), F32)],
        [vmem((order, 2 * link), BF16)],
        live_rows, pair, p_core, p_far, tile_swap(p_far, 1), x, k, after(links, total),
    )
    step = 4
    while step < blocks:
        other = block_swap(total, step)
        if step == 4:
            other, off_terms, *y_all = lax.optimization_barrier((other, off_terms, *y_all))
        total = total + other
        step *= 2
    cross = tile_swap(after(y_all[2], total), 1)
    start, scaled = call(
        start_kernel,
        [((width, 2 * width), BF16), ((rows, width), F32)],
        [vmem((2 * group, width), F32), vmem((rows, width), F32)],
        s_own, *y_all, cross,
    )

    near = after(block_swap(total, 1), scaled)
    here = (total, near)
    there = (after(tile_swap(total, 2), near), after(diagonal_swap(total), near))
    sums = []
    for pieces in (here, there):
        sums += [*pieces, *(tile_swap(piece, 1) for piece in pieces)]
    global_schur, back_cols = call(
        back_kernel,
        [((group, width), F32), ((rows, width), F32)],
        [vmem((8 * size, group), F32), vmem((width, 2 * width), BF16), vmem((group, width), F32),
         vmem((rows, width), F32), pltpu.SemaphoreType.DMA((3,))],
        *sums, start, scaled, out_whole=True,
        flops=int(6 * rows * order * order),
    )
    next_terms = after(next_terms, cross)
    came = lax.ppermute(next_terms, "tm", [(i, (i - 1) % blocks) for i in range(blocks)])
    link_diag, link_cross = call(
        finish_kernel,
        [((share, link), F32), ((share, width), F32)],
        [],
        own_terms, came,
    )
    return (
        link_diag[None], off_terms[None], link_cross[None], global_schur, back_cols[None],
    )


def solution(mesh):
    return jax.shard_map(
        functools.partial(shards, mesh.shape["tm"]),
        mesh=mesh,
        in_specs=(
            P("tm", "tile", None),
            P("tm", "tile", None),
            P("tm"),
            P("tm", None),
            P("tm", "tile", None),
            P("tm", "tile", None),
            P("tile", None),
            P("tile", None),
        ),
        out_specs=(
            P("tm", "tile", None),
            P("tm", "tile", None),
            P("tm", "tile", None),
            P("tile", None),
            P("tm", "tile", None),
        ),
        check_vma=False,
    )
```

```python
import functools

import jax
import jax.numpy as jnp
from jax import lax
from jax.experimental import pallas as pl
from jax.experimental.pallas import tpu as pltpu
from jax.sharding import PartitionSpec as P

BF16 = jnp.bfloat16
F32 = jnp.float32
STEPS = 2
TERMS = 2**STEPS - 1
SPARE = 8
VMEM_BYTES = 32 * 2**20


def halves(value):
    high = value.astype(BF16)
    return high, (value - high.astype(F32)).astype(BF16)


def dot(left_side, right_side):
    return jnp.dot(left_side, right_side, preferred_element_type=F32)


def both(value):
    return jnp.concatenate(halves(value), axis=1)


def stacked(value):
    return jnp.concatenate(halves(value), axis=0)


def at(start, size, unit=16):
    return pl.ds(pl.multiple_of(start, unit), size)


def place():
    part = lax.axis_index("tile")
    return part, part // 2, part % 2


def folded(square):
    half = square.shape[0] // 2
    last = square[half:, half:]
    last = jnp.concatenate([last[: half // 2, :], last[half // 2 :, :]], axis=1)
    return jnp.concatenate([square[:half, :], last], axis=0)


def unfolded(rows):
    half = rows.shape[1] // 2
    upper, last = rows[:half, :], rows[half:, :]
    last = jnp.concatenate([last[:, :half], last[:, half:]], axis=0)
    return jnp.concatenate(
        [upper, jnp.concatenate([upper[:, half:].T, last], axis=1)], axis=0
    )


def put_rows(own, other, target, offset=0):
    rows = own.shape[0]
    core = place()[2]
    target[at(offset + core * rows, rows), :] = own[...]
    target[at(offset + (1 - core) * rows, rows), :] = other[...]


def started(*pairs, sems):
    copies = [
        pltpu.make_async_copy(source, target, sems.at[i])
        for i, (source, target) in enumerate(pairs)
    ]
    for copy in copies:
        copy.start()
    return copies


def pack_kernel(
    x_rows, k_rows, g_rows, s_rows, index,
    x_out, k_out, x_own, k_own, g_own, s_out, index_out, sems,
):
    rows, order = x_rows.shape
    half = order // 2
    unit = half // 3
    group = s_rows.shape[0]
    _, near, core = place()
    copies = started(
        (x_rows, x_own),
        (k_rows, k_own),
        (g_rows, g_own),
        (index, index_out),
        *[
            (s_rows.at[:, first : first + group], s_out.at[first : first + group, :])
            for first in range(0, s_out.shape[0], group)
        ],
        sems=sems,
    )
    edge = at(near * half + core * 2 * unit, unit, 128)
    middle = at(near * half + unit, unit, 128)
    opposite = at(near * half + (1 - core) * 2 * unit, unit, 128)
    large = at(core * (rows - unit), unit, 8)
    small = at((1 - core) * unit, rows - unit, 8)
    for copy, own, out in zip(copies, (x_own, k_own), (x_out, k_out)):
        copy.wait()
        out[0:unit, :] = own[large, edge]
        out[unit : 2 * unit, :] = own[large, middle]
        out[2 * unit : unit + rows, :] = own[small, middle]
        block = own[large, opposite]
        out[unit + rows : 3 * unit, :] = jnp.where(
            core == 0, block[: unit // 2, :], block.T[unit // 2 :, :]
        )
        out[3 * unit :, :] = jnp.zeros((out.shape[0] - 3 * unit, unit), F32)
    for copy in copies[2:]:
        copy.wait()


def corner(far, cross, target, live):
    order = target.shape[1]
    half = order // 2
    unit = half // 3
    core = place()[2]

    def joined(first, last):
        mine, theirs = far[first:last, :], cross[first:last, :]
        return jnp.where(core == 0, mine, theirs), jnp.where(core == 0, theirs, mine)

    def put(row, col, value):
        first = half + row * unit
        cols = slice(half + col * unit, half + (col + 1) * unit)
        high, low = halves(value * live[:, cols])
        target[first : first + unit, cols] = high
        target[order + first : order + first + unit, cols] = low

    zero, one = joined(0, unit)
    put(0, 0, zero)
    put(2, 2, one)
    zero, one = joined(unit, 2 * unit)
    put(0, 1, zero)
    put(1, 0, zero.T)
    put(2, 1, one)
    put(1, 2, one.T)
    put(1, 1, jnp.concatenate(joined(2 * unit, 2 * unit + unit // 2), axis=0))
    side = jnp.concatenate(joined(2 * unit + unit // 2, 3 * unit), axis=0)
    put(0, 2, side)
    put(2, 0, side.T)


def spread(whole, target, live):
    half, order = whole.shape
    for rows, cols, value in (
        (slice(0, half), slice(0, order), whole[...]),
        (slice(half, order), slice(0, half), whole[:, half:].T),
    ):
        high, low = halves(value * live[:, cols])
        target[rows, cols] = high
        target[order + rows.start : order + rows.stop, cols] = low


def times(rows, matrix):
    count, order = rows.shape
    high = rows.astype(BF16)
    parts = stacked(rows)
    result = []
    for first in range(0, order, 256):
        cols = slice(first, min(first + 256, order))
        product = dot(parts, matrix[:order, cols])
        result.append((product[:count] + product[count:]) + dot(high, matrix[order:, cols]))
    return jnp.concatenate(result, axis=1)


def times_wide(left_side, right_side, first, last):
    count, width = left_side.shape[0], right_side.shape[1] // 2
    parts = stacked(left_side)
    product = dot(parts, right_side[:, first:last])
    return (product[:count] + product[count:]) + dot(
        parts[:count], right_side[:, width + first : width + last]
    )


def prepare_kernel(
    sizes, x_own, k_own, x_core, k_core, g_own, g_core, g_far, g_cross, index, far, cross,
    x, k, links, live_rows, live_cols, columns, first, whole, gathered,
):
    half, order = whole.shape
    rows = half // 2
    width = links.shape[1]
    group = width // 4
    part, near, core = place()
    for out, axis in ((live_rows, 0), (live_cols, 1)):
        ids = lax.broadcasted_iota(jnp.int32, out.shape, axis)
        ids = jnp.where(ids < half, ids + near * half, ids - near * half)
        out[...] = jnp.where(ids < sizes[0], 1.0, 0.0)
    for own, other, target in ((x_own, x_core, x), (k_own, k_core, k)):
        for side, col in enumerate((near * half, (1 - near) * half)):
            cols = slice(side * half, (side + 1) * half)
            whole[at(core * rows, rows), cols] = own[:, at(col, half, 128)]
            whole[at((1 - core) * rows, rows), cols] = other[:, at(col, half, 128)]
        spread(whole, target, live_cols)
    put_rows(g_own, g_core, gathered)
    put_rows(g_far, g_cross, gathered, half)
    hot = lax.broadcasted_iota(jnp.int32, (width, width), 0) == index[...]
    chosen = dot(gathered[...], hot.astype(F32).astype(BF16))
    links[...] = (chosen * live_rows[...]).astype(BF16)
    corner(far, cross, x, live_cols)
    value = links[:, at(part * group, group, 128)].astype(F32).T
    columns[...] = value
    high = value.astype(BF16)
    first[...] = dot(high, x[:order, :]) + dot(high, x[order:, :])


def global_kernel(
    live, far, cross, x, k_in, links, columns, product, base, s_own,
    keep, send, y_own, y_core, y_far, k, pack, solved,
):
    del k_in
    order, width = links.shape
    half = order // 2
    rows = half // 2
    group = width // 4
    part, near, core = place()
    time = lax.axis_index("tm")
    corner(far, cross, k, live)
    value = 2.0 * columns[...] - times(product[...], k)
    for step in range(TERMS - 1):
        value = columns[...] + value - times(times(value, x), k)
    result = times(value, x)
    left_side = stacked(result)
    solved[...] = result.T
    y_own[...] = solved[at(core * rows, rows), :]
    y_core[:rows, :] = solved[at((1 - core) * rows, rows), :]
    for i, block in enumerate((part, 2 * (1 - near), 2 * (1 - near) + 1)):
        first = rows + i * group
        y_core[first : first + group, :] = s_own[at(block * group, group, 8), :]
    y_far[:rows, :] = solved[at(half + core * rows, rows), :]
    y_far[rows : 2 * rows, :] = solved[at(half + (1 - core) * rows, rows), :]
    y_far[2 * rows :, :] = s_own[at(2 * near * group, 2 * group, 8), :]

    def square(shift):
        cols = at(((part + shift) % 4) * group, group, 128)
        parts = dot(left_side, links[:, cols])
        added = jnp.where(time == 0, base[:, cols], 0.0)
        return parts[:group] + parts[group:] + added

    first = group * 3 // 4
    pack[0:first, :] = folded(square(0))
    pack[first : first + group, :] = square(1)
    across = square(2)
    pack[first + group :, :] = jnp.where(
        part < 2, across[: group // 2, :], across.T[group // 2 :, :]
    )
    size = keep.shape[0]
    side = time % 2
    keep[...] = pack[at(side * size, size, 8), :]
    send[...] = pack[at((1 - side) * size, size, 8), :]


def pair_kernel(
    live, p_own, p_core, p_far, p_cross, x, k, links,
    own_terms, off_terms, next_terms, gathered, turned, columns,
):
    half = x.shape[1] // 2
    rows, width = p_far.shape
    link = width // 2
    share = link // 4
    put_rows(p_own, p_core, gathered)
    put_rows(p_far, p_cross, gathered, half)
    masked = gathered[...] * live[...].astype(BF16)
    gathered[...] = masked
    part = place()[0]
    for first in (0, link):
        block = gathered[:, at(first + (part // 2) * 2 * share, 2 * share, 128)]
        turned[...] = block.astype(F32).T
        half = first * share // link
        columns[half : half + share, :] = turned[at((part % 2) * share, share, 8), :]
    value = columns[...]
    order = x.shape[1]
    high = value.astype(BF16)
    product = dot(high, x[:order, :]) + dot(high, x[order:, :])
    value = 2.0 * value - times(product, k)
    for step in range(TERMS - 1):
        value = columns[...] + value - times(times(value, x), k)
    left_side = stacked(times(value, x))
    terms = dot(left_side, masked)
    terms = terms[: 2 * share] + terms[2 * share :]
    cross = dot(left_side, links[...])
    cross = cross[: 2 * share] + cross[2 * share :]
    next_terms[:, :link] = terms[:share, :link]
    next_terms[:, link:] = cross[:share]
    off_terms[...] = terms[:share, link:]
    own_terms[:, :link] = terms[share:, link:]
    own_terms[:, link:] = cross[share:]


def start_kernel(s_own, y_own, y_core, far, cross, start, scaled, s_rows, y_rows):
    rows, group = y_own.shape
    width = s_rows.shape[1]
    half = width // 2
    part, near, core = place()
    top, bottom = at(near * half, half), at((1 - near) * half, half)
    left, right = at(near * half, half, 128), at((1 - near) * half, half, 128)
    low_left, low_right = (at(width + v * half, half, 128) for v in (near, 1 - near))

    def put(rows, cols, low_cols, value):
        start[rows, cols], start[rows, low_cols] = halves(value)

    mine, theirs = at(core * group, group), at((1 - core) * group, group)
    for i in range(width // group):
        first = i * group
        s_rows[mine, first : first + group] = s_own[first : first + group, :]
    for i, block in enumerate((part ^ 1, 2 * (1 - near), 2 * (1 - near) + 1)):
        first = rows + i * group
        s_rows[theirs, at(block * group, group, 128)] = y_core[first : first + group, :]
    s_rows[theirs, at(part * group, group, 128)] = s_own[at((part ^ 1) * group, group, 8), :].T
    put(top, left, low_left, s_rows[:, left])
    side = s_rows[:, right]
    put(top, right, low_right, side)
    put(bottom, left, low_left, side.T)
    for i in range(half // group):
        first = slice(2 * rows + i * group, 2 * rows + (i + 1) * group)
        put_rows(far.at[first, :], cross.at[first, :], s_rows.at[:, i * group : (i + 1) * group])
    put(bottom, right, low_right, s_rows[:, :half])
    for ref, mask in ((y_own, 0), (y_core, 1), (far, 2), (cross.at[rows:, :], 3)):
        y_rows[:, at((part ^ mask) * group, group, 128)] = ref[:rows, :]
    for first in range(0, width, half):
        scaled[:, first : first + half] = times_wide(y_rows[...], start, first, first + half)


def back_kernel(*refs):
    sums, (start, scaled, schur_out, back_out) = refs[:8], refs[8:12]
    whole, parts, schur, back, sems = refs[12:]
    part = place()[0]
    side = lax.axis_index("tm") % 2
    size = sums[0].shape[0]
    group, width = schur.shape
    span, diagonal = 2 * size, group * 3 // 4
    for mask in range(4):
        for half in range(2):
            rows = at((part ^ mask) * span + (side ^ half) * size, size, 8)
            whole[rows, :] = sums[2 * mask + half][...]

    def put(row, col, value):
        rows = slice(row * group, (row + 1) * group)
        high, low = halves(value)
        parts[rows, col * group : (col + 1) * group] = high
        parts[rows, width + col * group : width + (col + 1) * group] = low

    def across(row):
        first = row * span + diagonal + group
        other = first + 2 * span
        return jnp.concatenate(
            [whole[at(first, group // 2, 8), :], whole[at(other, group // 2, 8), :]], axis=0
        )

    for row in range(4):
        first = row * span
        put(row, row, unfolded(whole[first : first + diagonal, :]))
        value = whole[first + diagonal : first + diagonal + group, :]
        put(row, (row + 1) % 4, value)
        put((row + 1) % 4, row, value.T)
        if row < 2:
            value = across(row)
            put(row, row + 2, value)
            put(row + 2, row, value.T)
    before = (part + 3) % 4
    value = across(part % 2)
    for col, value in (
        (part, unfolded(whole[at(part * span, diagonal, 8), :])),
        ((part + 1) % 4, whole[at(part * span + diagonal, group, 8), :]),
        ((part + 2) % 4, jnp.where(part < 2, value, value.T)),
        (before, whole[at(before * span + diagonal, group, 8), :].T),
    ):
        schur[:, at(col * group, group, 128)] = value
    copies = [pltpu.make_async_copy(schur, schur_out, sems.at[0])]
    copies[0].start()
    value = scaled[...]
    half = width // 2
    result = jnp.concatenate(
        [times_wide(value, parts, first, first + half) for first in (0, half)], axis=1
    )
    for i, first in enumerate((0, half)):
        cols = slice(first, first + half)
        back[:, cols] = 2.0 * value[:, cols] - times_wide(result, start, first, first + half)
        copies.append(
            pltpu.make_async_copy(back.at[:, cols], back_out.at[:, cols], sems.at[1 + i])
        )
        copies[-1].start()
    for copy in copies:
        copy.wait()


def finish_kernel(own_terms, came, link_diag, link_cross):
    link = link_diag.shape[1]
    there = lax.axis_index("tm") + 1 < lax.axis_size("tm")
    link_diag[...] = own_terms[:, :link] + jnp.where(there, came[:, :link], 0.0)
    link_cross[...] = own_terms[:, link:] + jnp.where(there, came[:, link:], 0.0)


def call(kernel, outs, scratch, *args, sizes=None, whole=False, out_whole=False, alias={}, flops=0):
    vmem = pl.BlockSpec(memory_space=pltpu.VMEM)
    specs = [pl.BlockSpec(memory_space=pltpu.HBM) if whole else vmem] * len(args)
    if whole:
        args = [pltpu.with_memory_space_constraint(arg, pltpu.HBM) for arg in args]
    if sizes is not None:
        specs, args = [pl.BlockSpec(memory_space=pltpu.SMEM), *specs], (sizes, *args)
    return pl.pallas_call(
        kernel,
        out_shape=[jax.ShapeDtypeStruct(shape, dtype) for shape, dtype in outs],
        in_specs=specs,
        out_specs=[pl.BlockSpec(memory_space=pltpu.HBM) if out_whole else vmem] * len(outs),
        scratch_shapes=scratch,
        input_output_aliases=alias,
        compiler_params=pltpu.CompilerParams(vmem_limit_bytes=VMEM_BYTES),
        cost_estimate=pl.CostEstimate(flops=flops, bytes_accessed=0, transcendentals=0),
        name=kernel.__name__,
    )(*args)


def after(value, *others):
    return lax.optimization_barrier((value, *others))[0]


def shards(
    blocks, operator, initial, block_sizes, link_index, link_pair, link_global, schur_base,
    schur_start,
):
    operator, initial = operator[0], initial[0]
    pair, glob = link_pair[0], link_global[0]
    rows, order = operator.shape
    half = order // 2
    unit = half // 3
    link, width = pair.shape[1] // 2, glob.shape[1]
    group, share = width // 4, link // 4
    size = group * 9 // 8

    def tile_swap(value, mask):
        return lax.ppermute(value, "tile", [(i, i ^ mask) for i in range(4)])

    def block_swap(value, mask):
        return lax.ppermute(value, "tm", [(i, i ^ mask) for i in range(blocks)])

    def diagonal_swap(value):
        pairs = [
            (b * 4 + i, (b ^ 1) * 4 + (i ^ 2)) for b in range(blocks) for i in range(4)
        ]
        return lax.ppermute(value, ("tm", "tile"), pairs)

    vmem, matrix = pltpu.VMEM, ((2 * order, order), BF16)

    g_far = tile_swap(glob, 2)
    x_sent, k_sent, x_own, k_own, g_own, s_own, index = call(
        pack_kernel,
        [((3 * unit + SPARE, unit), F32), ((3 * unit + 2 * SPARE, unit), F32),
         ((rows, order), F32), ((rows, order), F32), ((rows, width), BF16),
         ((width, group), F32), (link_index.shape, jnp.int32)],
        [pltpu.SemaphoreType.DMA((8,))],
        initial, operator, glob, schur_start, link_index, whole=True,
    )
    x_far, k_far = tile_swap(x_sent, 2), tile_swap(k_sent, 2)
    g_far = after(g_far, x_sent)
    g_cross = tile_swap(g_far, 1)
    x_far, g_cross = lax.optimization_barrier((x_far, g_cross))
    x, k, links, live_rows, live_cols, columns, first = call(
        prepare_kernel,
        [matrix, matrix, ((order, width), BF16), ((order, 1), F32), ((1, order), F32),
         ((group, order), F32), ((group, order), F32)],
        [vmem((half, order), F32), vmem((order, width), BF16)],
        x_own, k_own, tile_swap(x_own, 1), tile_swap(k_own, 1), g_own, tile_swap(g_own, 1),
        g_far, g_cross, index,
        x_far, tile_swap(x_far, 1), sizes=block_sizes,
    )
    k_far = after(k_far, first)
    p_core, p_far = (tile_swap(after(pair, first), m) for m in (1, 2))
    k_cross, p_core = lax.optimization_barrier((tile_swap(k_far, 1), p_core))
    keep, send, y_own, y_core, y_far, k = call(
        global_kernel,
        [((size, group), F32)] * 2 + [((rows, group), F32), ((rows + 3 * group, group), F32)]
        + [((2 * rows + 2 * group, group), F32), matrix],
        [vmem((2 * size, group), F32), vmem((order, group), F32)],
        live_cols, k_far, k_cross, x, k, links, columns, first, schur_base, s_own,
        alias={4: 5},
    )

    y_all = (y_own, tile_swap(y_core, 1), tile_swap(y_far, 2))
    if blocks > 2:
        parts = [block_swap(send, 1), block_swap(keep, 2), block_swap(send, 3)]
        total = (parts[2] + parts[0]) + (parts[1] + keep)
    else:
        total = keep + block_swap(send, 1)
    p_far = after(p_far, keep)
    own_terms, off_terms, next_terms = call(
        pair_kernel,
        [((share, link + width), F32), ((share, link), F32), ((share, link + width), F32)],
        [vmem((order, 2 * link), BF16), vmem((2 * share, order), F32),
         vmem((2 * share, order), F32)],
        live_rows, pair, p_core, p_far, tile_swap(p_far, 1), x, k, after(links, total),
    )
    step = 4
    while step < blocks:
        other = block_swap(total, step)
        if step == 4:
            other, off_terms, *y_all = lax.optimization_barrier((other, off_terms, *y_all))
        total = total + other
        step *= 2
    cross = tile_swap(after(y_all[2], total), 1)
    start, scaled = call(
        start_kernel,
        [((width, 2 * width), BF16), ((rows, width), F32)],
        [vmem((2 * group, width), F32), vmem((rows, width), F32)],
        s_own, *y_all, cross,
    )

    near = after(block_swap(total, 1), scaled)
    here = (total, near)
    there = (after(tile_swap(total, 2), near), after(diagonal_swap(total), near))
    sums = []
    for pieces in (here, there):
        sums += [*pieces, *(tile_swap(piece, 1) for piece in pieces)]
    global_schur, back_cols = call(
        back_kernel,
        [((group, width), F32), ((rows, width), F32)],
        [vmem((8 * size, group), F32), vmem((width, 2 * width), BF16), vmem((group, width), F32),
         vmem((rows, width), F32), pltpu.SemaphoreType.DMA((3,))],
        *sums, start, scaled, out_whole=True,
        flops=int(6 * rows * order * order),
    )
    next_terms = after(next_terms, cross)
    came = lax.ppermute(next_terms, "tm", [(i, (i - 1) % blocks) for i in range(blocks)])
    link_diag, link_cross = call(
        finish_kernel,
        [((share, link), F32), ((share, width), F32)],
        [],
        own_terms, came,
    )
    return (
        link_diag[None], off_terms[None], link_cross[None], global_schur, back_cols[None],
    )


def solution(mesh):
    return jax.shard_map(
        functools.partial(shards, mesh.shape["tm"]),
        mesh=mesh,
        in_specs=(
            P("tm", "tile", None),
            P("tm", "tile", None),
            P("tm"),
            P("tm", None),
            P("tm", "tile", None),
            P("tm", "tile", None),
            P("tile", None),
            P("tile", None),
        ),
        out_specs=(
            P("tm", "tile", None),
            P("tm", "tile", None),
            P("tm", "tile", None),
            P("tile", None),
            P("tm", "tile", None),
        ),
        check_vma=False,
    )
```

```python
import functools

import jax
import jax.numpy as jnp
from jax import lax
from jax.experimental import pallas as pl
from jax.experimental.pallas import tpu as pltpu
from jax.sharding import PartitionSpec as P

BF16 = jnp.bfloat16
F32 = jnp.float32
STEPS = 2
TERMS = 2**STEPS - 1
SPARE = 8
VMEM_BYTES = 32 * 2**20


def halves(value):
    high = value.astype(BF16)
    return high, (value - high.astype(F32)).astype(BF16)


def dot(left_side, right_side):
    return jnp.dot(left_side, right_side, preferred_element_type=F32)


def both(value):
    return jnp.concatenate(halves(value), axis=1)


def stacked(value):
    return jnp.concatenate(halves(value), axis=0)


def at(start, size, unit=16):
    return pl.ds(pl.multiple_of(start, unit), size)


def place():
    part = lax.axis_index("tile")
    return part, part // 2, part % 2


def folded(square):
    half = square.shape[0] // 2
    last = square[half:, half:]
    last = jnp.concatenate([last[: half // 2, :], last[half // 2 :, :]], axis=1)
    return jnp.concatenate([square[:half, :], last], axis=0)


def unfolded(rows):
    half = rows.shape[1] // 2
    upper, last = rows[:half, :], rows[half:, :]
    last = jnp.concatenate([last[:, :half], last[:, half:]], axis=0)
    return jnp.concatenate(
        [upper, jnp.concatenate([upper[:, half:].T, last], axis=1)], axis=0
    )


def put_rows(own, other, target, offset=0):
    rows = own.shape[0]
    core = place()[2]
    target[at(offset + core * rows, rows), :] = own[...]
    target[at(offset + (1 - core) * rows, rows), :] = other[...]


def started(*pairs, sems):
    copies = [
        pltpu.make_async_copy(source, target, sems.at[i])
        for i, (source, target) in enumerate(pairs)
    ]
    for copy in copies:
        copy.start()
    return copies


def pack_kernel(
    x_rows, k_rows, g_rows, s_rows, index,
    x_out, k_out, x_own, k_own, g_own, s_out, index_out, sems,
):
    rows, order = x_rows.shape
    half = order // 2
    unit = half // 3
    group = s_rows.shape[0]
    _, near, core = place()
    copies = started(
        (x_rows, x_own),
        (k_rows, k_own),
        (g_rows, g_own),
        (index, index_out),
        *[
            (s_rows.at[:, first : first + group], s_out.at[first : first + group, :])
            for first in range(0, s_out.shape[0], group)
        ],
        sems=sems,
    )
    edge = at(near * half + core * 2 * unit, unit, 128)
    middle = at(near * half + unit, unit, 128)
    opposite = at(near * half + (1 - core) * 2 * unit, unit, 128)
    large = at(core * (rows - unit), unit, 8)
    small = at((1 - core) * unit, rows - unit, 8)
    for copy, own, out in zip(copies, (x_own, k_own), (x_out, k_out)):
        copy.wait()
        out[0:unit, :] = own[large, edge]
        out[unit : 2 * unit, :] = own[large, middle]
        out[2 * unit : unit + rows, :] = own[small, middle]
        block = own[large, opposite]
        out[unit + rows : 3 * unit, :] = jnp.where(
            core == 0, block[: unit // 2, :], block.T[unit // 2 :, :]
        )
        out[3 * unit :, :] = jnp.zeros((out.shape[0] - 3 * unit, unit), F32)
    for copy in copies[2:]:
        copy.wait()


def corner(far, cross, target, live):
    order = target.shape[1]
    half = order // 2
    unit = half // 3
    core = place()[2]

    def joined(first, last):
        mine, theirs = far[first:last, :], cross[first:last, :]
        return jnp.where(core == 0, mine, theirs), jnp.where(core == 0, theirs, mine)

    def put(row, col, value):
        first = half + row * unit
        cols = slice(half + col * unit, half + (col + 1) * unit)
        high, low = halves(value * live[:, cols])
        target[first : first + unit, cols] = high
        target[order + first : order + first + unit, cols] = low

    zero, one = joined(0, unit)
    put(0, 0, zero)
    put(2, 2, one)
    zero, one = joined(unit, 2 * unit)
    put(0, 1, zero)
    put(1, 0, zero.T)
    put(2, 1, one)
    put(1, 2, one.T)
    put(1, 1, jnp.concatenate(joined(2 * unit, 2 * unit + unit // 2), axis=0))
    side = jnp.concatenate(joined(2 * unit + unit // 2, 3 * unit), axis=0)
    put(0, 2, side)
    put(2, 0, side.T)


def spread(whole, target, live):
    half, order = whole.shape
    for rows, cols, value in (
        (slice(0, half), slice(0, order), whole[...]),
        (slice(half, order), slice(0, half), whole[:, half:].T),
    ):
        high, low = halves(value * live[:, cols])
        target[rows, cols] = high
        target[order + rows.start : order + rows.stop, cols] = low


def times(rows, matrix):
    count, order = rows.shape
    high = rows.astype(BF16)
    parts = stacked(rows)
    result = []
    for first in range(0, order, 256):
        cols = slice(first, min(first + 256, order))
        product = dot(parts, matrix[:order, cols])
        result.append((product[:count] + product[count:]) + dot(high, matrix[order:, cols]))
    return jnp.concatenate(result, axis=1)


def times_wide(left_side, right_side, first, last):
    count, width = left_side.shape[0], right_side.shape[1] // 2
    parts = stacked(left_side)
    product = dot(parts, right_side[:, first:last])
    return (product[:count] + product[count:]) + dot(
        parts[:count], right_side[:, width + first : width + last]
    )


def prepare_kernel(
    sizes, x_own, k_own, x_core, k_core, g_own, g_core, g_far, g_cross, index, far, cross,
    x, k, links, live_rows, live_cols, columns, first, whole, gathered,
):
    half, order = whole.shape
    rows = half // 2
    width = links.shape[1]
    group = width // 4
    part, near, core = place()
    for out, axis in ((live_rows, 0), (live_cols, 1)):
        ids = lax.broadcasted_iota(jnp.int32, out.shape, axis)
        ids = jnp.where(ids < half, ids + near * half, ids - near * half)
        out[...] = jnp.where(ids < sizes[0], 1.0, 0.0)
    for own, other, target in ((x_own, x_core, x), (k_own, k_core, k)):
        for side, col in enumerate((near * half, (1 - near) * half)):
            cols = slice(side * half, (side + 1) * half)
            whole[at(core * rows, rows), cols] = own[:, at(col, half, 128)]
            whole[at((1 - core) * rows, rows), cols] = other[:, at(col, half, 128)]
        spread(whole, target, live_cols)
    put_rows(g_own, g_core, gathered)
    put_rows(g_far, g_cross, gathered, half)
    hot = lax.broadcasted_iota(jnp.int32, (width, width), 0) == index[...]
    chosen = dot(gathered[...], hot.astype(F32).astype(BF16))
    links[...] = (chosen * live_rows[...]).astype(BF16)
    corner(far, cross, x, live_cols)
    value = links[:, at(part * group, group, 128)].astype(F32).T
    columns[...] = value
    high = value.astype(BF16)
    first[...] = dot(high, x[:order, :]) + dot(high, x[order:, :])


def global_kernel(
    live, far, cross, x, k_in, links, columns, product, base, s_own,
    keep, send, y_own, y_core, y_far, k, pack, solved,
):
    del k_in
    order, width = links.shape
    half = order // 2
    rows = half // 2
    group = width // 4
    part, near, core = place()
    time = lax.axis_index("tm")
    corner(far, cross, k, live)
    value = 2.0 * columns[...] - times(product[...], k)
    for step in range(TERMS - 1):
        value = columns[...] + value - times(times(value, x), k)
    result = times(value, x)
    left_side = stacked(result)
    solved[...] = result.T
    y_own[...] = solved[at(core * rows, rows), :]
    y_core[:rows, :] = solved[at((1 - core) * rows, rows), :]
    for i, block in enumerate((part, 2 * (1 - near), 2 * (1 - near) + 1)):
        first = rows + i * group
        y_core[first : first + group, :] = s_own[at(block * group, group, 8), :]
    y_far[:rows, :] = solved[at(half + core * rows, rows), :]
    y_far[rows : 2 * rows, :] = solved[at(half + (1 - core) * rows, rows), :]
    y_far[2 * rows :, :] = s_own[at(2 * near * group, 2 * group, 8), :]

    def square(shift):
        cols = at(((part + shift) % 4) * group, group, 128)
        parts = dot(left_side, links[:, cols])
        added = jnp.where(time == 0, base[:, cols], 0.0)
        return parts[:group] + parts[group:] + added

    first = group * 3 // 4
    pack[0:first, :] = folded(square(0))
    pack[first : first + group, :] = square(1)
    across = square(2)
    pack[first + group :, :] = jnp.where(
        part < 2, across[: group // 2, :], across.T[group // 2 :, :]
    )
    size = keep.shape[0]
    side = time % 2
    keep[...] = pack[at(side * size, size, 8), :]
    send[...] = pack[at((1 - side) * size, size, 8), :]


def pair_kernel(
    live, p_own, p_core, p_far, p_cross, x, k, links,
    own_terms, off_terms, next_terms, gathered, turned, columns,
):
    half = x.shape[1] // 2
    rows, width = p_far.shape
    link = width // 2
    share = link // 4
    put_rows(p_own, p_core, gathered)
    put_rows(p_far, p_cross, gathered, half)
    masked = gathered[...] * live[...].astype(BF16)
    gathered[...] = masked
    part = place()[0]
    for first in (0, link):
        block = gathered[:, at(first + (part // 2) * 2 * share, 2 * share, 128)]
        turned[...] = block.astype(F32).T
        half = first * share // link
        columns[half : half + share, :] = turned[at((part % 2) * share, share, 8), :]
    value = columns[...]
    order = x.shape[1]
    high = value.astype(BF16)
    product = dot(high, x[:order, :]) + dot(high, x[order:, :])
    value = 2.0 * value - times(product, k)
    for step in range(TERMS - 1):
        value = columns[...] + value - times(times(value, x), k)
    left_side = stacked(times(value, x))
    terms = dot(left_side, masked)
    terms = terms[: 2 * share] + terms[2 * share :]
    cross = dot(left_side, links[...])
    cross = cross[: 2 * share] + cross[2 * share :]
    next_terms[:, :link] = terms[:share, :link]
    next_terms[:, link:] = cross[:share]
    off_terms[...] = terms[:share, link:]
    own_terms[:, :link] = terms[share:, link:]
    own_terms[:, link:] = cross[share:]


def start_kernel(s_own, y_own, y_core, far, cross, start, scaled, s_rows, y_rows):
    rows, group = y_own.shape
    width = s_rows.shape[1]
    half = width // 2
    part, near, core = place()
    top, bottom = at(near * half, half), at((1 - near) * half, half)
    left, right = at(near * half, half, 128), at((1 - near) * half, half, 128)
    low_left, low_right = (at(width + v * half, half, 128) for v in (near, 1 - near))

    def put(rows, cols, low_cols, value):
        start[rows, cols], start[rows, low_cols] = halves(value)

    mine, theirs = at(core * group, group), at((1 - core) * group, group)
    for i in range(width // group):
        first = i * group
        s_rows[mine, first : first + group] = s_own[first : first + group, :]
    for i, block in enumerate((part ^ 1, 2 * (1 - near), 2 * (1 - near) + 1)):
        first = rows + i * group
        s_rows[theirs, at(block * group, group, 128)] = y_core[first : first + group, :]
    s_rows[theirs, at(part * group, group, 128)] = s_own[at((part ^ 1) * group, group, 8), :].T
    put(top, left, low_left, s_rows[:, left])
    side = s_rows[:, right]
    put(top, right, low_right, side)
    put(bottom, left, low_left, side.T)
    for i in range(half // group):
        first = slice(2 * rows + i * group, 2 * rows + (i + 1) * group)
        put_rows(far.at[first, :], cross.at[first, :], s_rows.at[:, i * group : (i + 1) * group])
    put(bottom, right, low_right, s_rows[:, :half])
    for ref, mask in ((y_own, 0), (y_core, 1), (far, 2), (cross.at[rows:, :], 3)):
        y_rows[:, at((part ^ mask) * group, group, 128)] = ref[:rows, :]
    for first in range(0, width, half):
        scaled[:, first : first + half] = times_wide(y_rows[...], start, first, first + half)


def back_kernel(*refs):
    sums, (start, scaled, schur_out, back_out) = refs[:8], refs[8:12]
    whole, parts, schur, back, sems = refs[12:]
    part = place()[0]
    side = lax.axis_index("tm") % 2
    size = sums[0].shape[0]
    group, width = schur.shape
    span, diagonal = 2 * size, group * 3 // 4
    for mask in range(4):
        for half in range(2):
            rows = at((part ^ mask) * span + (side ^ half) * size, size, 8)
            whole[rows, :] = sums[2 * mask + half][...]

    def put(row, col, value):
        rows = slice(row * group, (row + 1) * group)
        high, low = halves(value)
        parts[rows, col * group : (col + 1) * group] = high
        parts[rows, width + col * group : width + (col + 1) * group] = low

    def across(row):
        first = row * span + diagonal + group
        other = first + 2 * span
        return jnp.concatenate(
            [whole[at(first, group // 2, 8), :], whole[at(other, group // 2, 8), :]], axis=0
        )

    for row in range(4):
        first = row * span
        put(row, row, unfolded(whole[first : first + diagonal, :]))
        value = whole[first + diagonal : first + diagonal + group, :]
        put(row, (row + 1) % 4, value)
        put((row + 1) % 4, row, value.T)
        if row < 2:
            value = across(row)
            put(row, row + 2, value)
            put(row + 2, row, value.T)
    before = (part + 3) % 4
    value = across(part % 2)
    for col, value in (
        (part, unfolded(whole[at(part * span, diagonal, 8), :])),
        ((part + 1) % 4, whole[at(part * span + diagonal, group, 8), :]),
        ((part + 2) % 4, jnp.where(part < 2, value, value.T)),
        (before, whole[at(before * span + diagonal, group, 8), :].T),
    ):
        schur[:, at(col * group, group, 128)] = value
    copies = [pltpu.make_async_copy(schur, schur_out, sems.at[0])]
    copies[0].start()
    value = scaled[...]
    half = width // 2
    result = jnp.concatenate(
        [times_wide(value, parts, first, first + half) for first in (0, half)], axis=1
    )
    for i, first in enumerate((0, half)):
        cols = slice(first, first + half)
        back[:, cols] = 2.0 * value[:, cols] - times_wide(result, start, first, first + half)
        copies.append(
            pltpu.make_async_copy(back.at[:, cols], back_out.at[:, cols], sems.at[1 + i])
        )
        copies[-1].start()
    for copy in copies:
        copy.wait()


def finish_kernel(own_terms, came, link_diag, link_cross):
    link = link_diag.shape[1]
    there = lax.axis_index("tm") + 1 < lax.axis_size("tm")
    link_diag[...] = own_terms[:, :link] + jnp.where(there, came[:, :link], 0.0)
    link_cross[...] = own_terms[:, link:] + jnp.where(there, came[:, link:], 0.0)


def call(kernel, outs, scratch, *args, sizes=None, whole=False, out_whole=False, alias={}, flops=0):
    vmem = pl.BlockSpec(memory_space=pltpu.VMEM)
    specs = [pl.BlockSpec(memory_space=pltpu.HBM) if whole else vmem] * len(args)
    if whole:
        args = [pltpu.with_memory_space_constraint(arg, pltpu.HBM) for arg in args]
    if sizes is not None:
        specs, args = [pl.BlockSpec(memory_space=pltpu.SMEM), *specs], (sizes, *args)
    return pl.pallas_call(
        kernel,
        out_shape=[jax.ShapeDtypeStruct(shape, dtype) for shape, dtype in outs],
        in_specs=specs,
        out_specs=[pl.BlockSpec(memory_space=pltpu.HBM) if out_whole else vmem] * len(outs),
        scratch_shapes=scratch,
        input_output_aliases=alias,
        compiler_params=pltpu.CompilerParams(vmem_limit_bytes=VMEM_BYTES),
        cost_estimate=pl.CostEstimate(flops=flops, bytes_accessed=0, transcendentals=0),
        name=kernel.__name__,
    )(*args)


def after(value, *others):
    return lax.optimization_barrier((value, *others))[0]


def shards(
    blocks, operator, initial, block_sizes, link_index, link_pair, link_global, schur_base,
    schur_start,
):
    operator, initial = operator[0], initial[0]
    pair, glob = link_pair[0], link_global[0]
    rows, order = operator.shape
    half = order // 2
    unit = half // 3
    link, width = pair.shape[1] // 2, glob.shape[1]
    group, share = width // 4, link // 4
    size = group * 9 // 8

    def tile_swap(value, mask):
        return lax.ppermute(value, "tile", [(i, i ^ mask) for i in range(4)])

    def block_swap(value, mask):
        return lax.ppermute(value, "tm", [(i, i ^ mask) for i in range(blocks)])

    def diagonal_swap(value):
        pairs = [
            (b * 4 + i, (b ^ 1) * 4 + (i ^ 2)) for b in range(blocks) for i in range(4)
        ]
        return lax.ppermute(value, ("tm", "tile"), pairs)

    vmem, matrix = pltpu.VMEM, ((2 * order, order), BF16)

    g_far = tile_swap(glob, 2)
    x_sent, k_sent, x_own, k_own, g_own, s_own, index = call(
        pack_kernel,
        [((3 * unit + SPARE, unit), F32), ((3 * unit + 2 * SPARE, unit), F32),
         ((rows, order), F32), ((rows, order), F32), ((rows, width), BF16),
         ((width, group), F32), (link_index.shape, jnp.int32)],
        [pltpu.SemaphoreType.DMA((8,))],
        initial, operator, glob, schur_start, link_index, whole=True,
    )
    x_far, k_far = tile_swap(x_sent, 2), tile_swap(k_sent, 2)
    g_far = after(g_far, x_sent)
    g_cross = tile_swap(g_far, 1)
    x_far, g_cross = lax.optimization_barrier((x_far, g_cross))
    x, k, links, live_rows, live_cols, columns, first = call(
        prepare_kernel,
        [matrix, matrix, ((order, width), BF16), ((order, 1), F32), ((1, order), F32),
         ((group, order), F32), ((group, order), F32)],
        [vmem((half, order), F32), vmem((order, width), BF16)],
        x_own, k_own, tile_swap(x_own, 1), tile_swap(k_own, 1), g_own, tile_swap(g_own, 1),
        g_far, g_cross, index,
        x_far, tile_swap(x_far, 1), sizes=block_sizes,
    )
    k_far = after(k_far, first)
    p_core, p_far = (tile_swap(after(pair, first), m) for m in (1, 2))
    k_cross, p_core = lax.optimization_barrier((tile_swap(k_far, 1), p_core))
    keep, send, y_own, y_core, y_far, k = call(
        global_kernel,
        [((size, group), F32)] * 2 + [((rows, group), F32), ((rows + 3 * group, group), F32)]
        + [((2 * rows + 2 * group, group), F32), matrix],
        [vmem((2 * size, group), F32), vmem((order, group), F32)],
        live_cols, k_far, k_cross, x, k, links, columns, first, schur_base, s_own,
        alias={4: 5},
    )

    y_all = (y_own, tile_swap(y_core, 1), tile_swap(y_far, 2))
    if blocks > 2:
        parts = [block_swap(send, 1), block_swap(keep, 2), block_swap(send, 3)]
        total = (parts[2] + parts[0]) + (parts[1] + keep)
    else:
        total = keep + block_swap(send, 1)
    p_far = after(p_far, keep)
    own_terms, off_terms, next_terms = call(
        pair_kernel,
        [((share, link + width), F32), ((share, link), F32), ((share, link + width), F32)],
        [vmem((order, 2 * link), BF16), vmem((2 * share, order), F32),
         vmem((2 * share, order), F32)],
        live_rows, pair, p_core, p_far, tile_swap(p_far, 1), x, k, after(links, total),
    )
    step = 4
    while step < blocks:
        other = block_swap(total, step)
        if step == 4:
            other, off_terms, *y_all = lax.optimization_barrier((other, off_terms, *y_all))
        total = total + other
        step *= 2
    cross = tile_swap(after(y_all[2], total), 1)
    start, scaled = call(
        start_kernel,
        [((width, 2 * width), BF16), ((rows, width), F32)],
        [vmem((2 * group, width), F32), vmem((rows, width), F32)],
        s_own, *y_all, cross,
    )

    near = after(block_swap(total, 1), scaled)
    here = (total, near)
    there = (after(tile_swap(total, 2), near), after(diagonal_swap(total), near))
    sums = []
    for pieces in (here, there):
        sums += [*pieces, *(tile_swap(piece, 1) for piece in pieces)]
    global_schur, back_cols = call(
        back_kernel,
        [((group, width), F32), ((rows, width), F32)],
        [vmem((8 * size, group), F32), vmem((width, 2 * width), BF16), vmem((group, width), F32),
         vmem((rows, width), F32), pltpu.SemaphoreType.DMA((3,))],
        *sums, start, scaled, out_whole=True,
        flops=int(6 * rows * order * order),
    )
    next_terms = after(next_terms, cross)
    came = lax.ppermute(next_terms, "tm", [(i, i - 1) for i in range(1, blocks)])
    link_diag, link_cross = call(
        finish_kernel,
        [((share, link), F32), ((share, width), F32)],
        [],
        own_terms, came,
    )
    return (
        link_diag[None], off_terms[None], link_cross[None], global_schur, back_cols[None],
    )


def solution(mesh):
    return jax.shard_map(
        functools.partial(shards, mesh.shape["tm"]),
        mesh=mesh,
        in_specs=(
            P("tm", "tile", None),
            P("tm", "tile", None),
            P("tm"),
            P("tm", None),
            P("tm", "tile", None),
            P("tm", "tile", None),
            P("tile", None),
            P("tile", None),
        ),
        out_specs=(
            P("tm", "tile", None),
            P("tm", "tile", None),
            P("tm", "tile", None),
            P("tile", None),
            P("tm", "tile", None),
        ),
        check_vma=False,
    )
```
